32 devices in a mesh: groups: 2 (over x), expert: 8 (over z, y), wave: 2 (over core).
Axes of the slice: x: 2, y: 2, z: 4, core: 2. Of those that a mesh axis runs over, the one named last changes fastest.
Arguments:
- hidden_rows: bfloat16 [512, 2, 2048], P(('groups', 'expert', 'wave')), parts along dimension 0, may hold values from -6 to 6
- expert_ids: int32 [512, 2, 8], P(('groups', 'expert', 'wave')), parts along dimension 0, may hold values from 0 to 15, all different within a row; in each aligned block of 32 rows (0 to 31, 32 to 63, ..., all dimensions but the last counted through in order) at most 24 rows name the same one
- route_weights: float32 [512, 2, 8], P(('groups', 'expert', 'wave')), parts along dimension 0, may hold values from 0.1 to 1
- w_gate: bfloat16 [16, 2048, 768], P('expert', None, 'wave'), may hold values from -0.125 to 0.125
- w_up: bfloat16 [16, 2048, 768], P('expert', None, 'wave'), may hold values from -0.125 to 0.125
- w_down: bfloat16 [16, 768, 2048], P('expert', 'wave'), may hold values from -0.21875 to 0.21875
- codes: int32 [512, 2, 16], P(('groups', 'expert', 'wave')), parts along dimension 0, may hold values from 0 to 1023
- owner_slot: int32 [512], P(('groups', 'expert', 'wave')), parts along dimension 0, may hold values from 0 to 255, as said below
- code_table: bfloat16 [16, 1024, 1024], P(None, 'expert'), may hold values from -1.5 to 1.5
- conv_state: bfloat16 [512, 6, 1024], P(('groups', 'expert', 'wave')), parts along dimension 0, may hold values from -6 to 6
- conv_taps: float32 [7, 1024], replicated, may hold values from -2.4 to 2.4
- conv_bias: float32 [1024], replicated, may hold values from -3 to 3
- upsample: bfloat16 [1024, 512], replicated, may hold values from -0.1875 to 0.1875
Outputs:
- moe_out: bfloat16 [512, 2, 2048], P(('groups', 'expert', 'wave')), parts along dimension 0
- waveform: bfloat16 [512, 2, 512], P(('groups', 'expert', 'wave')), parts along dimension 0
- new_state: bfloat16 [512, 6, 1024], P(('groups', 'expert', 'wave')), parts along dimension 0
The draws below stay inside these ranges and needn't reach their ends.
There are 2 independent parts, one for each index of `groups`. The reference program is written for one: setup_inputs(seed, part) draws one part's arguments, and reference() takes and returns one part's arrays. A program takes and returns all parts, laid end to end along the dimension named above; an argument that names none is the same for every part. Nothing has to cross between parts.
Inputs may be any that keep to these rules, and one draw needn't show every extreme that they name: `expert_ids`: each row names 8 different experts; among the 32 rows of one device no expert is named more than 24 times, a bound that some block reaches. `owner_slot`: A permutation of the slots. Slot o lies on the device holding rows o of the decoder's arrays; a session's slot lies on a device with the same index along wave as the session's own device, so every device holds 16 slots.
All inputs are finite; a program needn't handle non-finite values.
Results may differ from the reference program's by a relative error of at most 0.012.
Values may be sent and summed in bfloat16 or wider, within the bound.
No kernel may reach another device: no remote copies, remote signals or barrier semaphores. Data moves between devices by JAX's collectives and lax.ppermute only.
A program may use at most 64 MiB of HBM per device.

```python
import math
import jax
import jax.numpy as jnp
import numpy as np
from jax import lax

D = 2048
FF = 768
TOP = 8
STEPS = 2
SESS_DEV = 16
CODEBOOKS = 16
CODES = 1024
DC = 1024
KERNEL = 7
UP = 2
OUT_CH = 256
EXPERTS = 16
CAP = 24
SESSIONS = 256
STATE = 6
N_EXPERT = 8
N_WAVE = 2


def draw_owner_slot(key, part):
    count = SESSIONS // N_WAVE
    owners = jnp.zeros((SESSIONS,), jnp.int32)
    within = jnp.arange(count, dtype=jnp.int32)
    for wave_index in range(N_WAVE):
        order = jax.random.permutation(jax.random.fold_in(key, 11 + wave_index), count).astype(jnp.int32)
        where = (within // SESS_DEV * N_WAVE + wave_index) * SESS_DEV + within % SESS_DEV
        target = (order // SESS_DEV * N_WAVE + wave_index) * SESS_DEV + order % SESS_DEV
        owners = owners.at[where].set(target)
    return owners


def place_ends(values, rng, smallest, largest):
    extent = values.shape
    place = [jax.random.randint(jax.random.fold_in(rng, axis), (), 0, extent[axis]) for axis in range(len(extent))]
    values = values.at[tuple(place)].set(smallest)
    longest = extent.index(max(extent))
    place[longest] = (place[longest] + 1) % extent[longest]
    return values.at[tuple(place)].set(largest)


def block_scale(own_key, dims, shards, least, top_value):
    level = 1.0
    for dim, parts in shards:
        draws = jax.random.uniform(jax.random.fold_in(jax.random.fold_in(own_key, 6), dim), (parts,), jnp.float32, least / len(shards), top_value / len(shards))
        level = level * jnp.repeat(jnp.exp(draws), dims[dim] // parts).reshape((-1,) + (1,) * (len(dims) - 1 - dim))
    return level


def shared_out(rng, own, number, rows, amount, top, limit, lean):
    sequence = jax.random.permutation(rng, amount)
    crowded, ordinary = shares(amount, rows * top, limit, lean, True), shares(amount, rows * top, limit, lean, False)
    places = jnp.arange(amount)

    def named(sizes, offset_by):
        used = int((sizes > 0).sum())
        fixed = max(1, used // 4)
        passed = fixed + (places - fixed + offset_by * (used - fixed)) % max(1, amount - fixed)
        return jnp.zeros((amount,), jnp.int32).at[sequence[jnp.where(places < fixed, places, passed)]].set(jnp.asarray(sizes, jnp.int32))

    sizes = jnp.where(number % 4 == 0, named(crowded, number // 4), named(ordinary, number - number // 4 - 1))
    mixed = jax.random.permutation(jax.random.fold_in(own, 3), amount)
    source_of, taker = mixed[0:amount // 2 * 2:2], mixed[1:amount // 2 * 2:2]
    room = jnp.minimum(sizes[source_of] - 1, limit - sizes[taker]) // 2
    room = jnp.where((source_of == sequence[0]) | (taker == sequence[0]) | (sizes[taker] == 0), 0, jnp.maximum(room, 0))
    passed = jax.random.randint(jax.random.fold_in(own, 4), (amount // 2,), 0, 1 << 20) % (room + 1)
    sizes = sizes.at[source_of].add(-passed).at[taker].add(passed)
    members = jnp.searchsorted(jnp.cumsum(sizes), jnp.arange(rows * top), side="right").astype(jnp.int32)
    grid = members.reshape(top, rows).T
    grid = grid[jax.random.permutation(jax.random.fold_in(own, 1), rows)]
    offset_by = jax.random.randint(jax.random.fold_in(own, 2), (rows, 1), 0, top)
    return jnp.take_along_axis(grid, (jnp.arange(top)[None, :] + offset_by) % top, axis=1)


def shares(count, total, bound, skew, full):
    portions = [(1 << 20) // math.isqrt(standing ** skew) + 1 for standing in range(1, count + 1)]
    largest = bound if full else min(bound, max(-(-total // count), total * portions[0] // sum(portions)))
    least = 1 if total - largest >= count - 1 else 0
    given, surplus = [largest] + [least] * (count - 1), total - largest - least * (count - 1)
    while surplus > 0:
        movable = [i for i in range(1, count) if given[i] < largest] or [i for i in range(1, count) if given[i] < bound]
        pool, budget = sum([portions[i] for i in movable]), surplus
        for i in movable:
            extra = min(bound - given[i], max(1, budget * portions[i] // pool), surplus)
            given[i] = given[i] + extra
            surplus = surplus - extra
    return np.array(given)


def centred(stream_key, extent, deviation, bound, split=(), held_as=jnp.bfloat16):
    values = jax.random.normal(stream_key, extent, jnp.float32) * deviation
    if len(split) > 0:
        values = block_scale(stream_key, extent, split, -0.22, 0.18) * values
    return jnp.clip(values, min=-bound, max=bound).astype(held_as)


def setup_inputs(seed: int = 0, part: int = 0) -> dict:
    arg_keys = jax.random.split(jax.random.key(seed), 14)
    part_splits = jax.random.split(jax.random.fold_in(arg_keys[13], part), 14)
    hidden_rows = centred(part_splits[0], (SESSIONS, STEPS, D), 1.0, 6.0, ((0, 16),))
    expert_ids_keys = jax.random.split(jax.random.fold_in(part_splits[1], 1), SESSIONS * STEPS // (SESS_DEV * STEPS))
    expert_ids_turns = jax.random.permutation(jax.random.fold_in(part_splits[1], 3), SESSIONS * STEPS // (SESS_DEV * STEPS))
    expert_ids = jax.vmap(lambda own, number: shared_out(jax.random.fold_in(part_splits[1], 2), own, number, SESS_DEV * STEPS, EXPERTS, TOP, CAP, 1))(expert_ids_keys, expert_ids_turns).reshape((SESSIONS, STEPS, TOP))
    route_weights = jnp.clip(jnp.exp(math.log(1.0) - 2.3025851 * jax.random.uniform(part_splits[2], (SESSIONS, STEPS, TOP), jnp.float32) ** block_scale(part_splits[2], (SESSIONS, STEPS, TOP), ((0, 16),), -0.2, 0.2)), 0.1, 1.0)
    w_gate = centred(arg_keys[3], (EXPERTS, D, FF), D ** -0.5, 0.125, ((0, 8), (2, 2)))
    w_up = centred(arg_keys[4], (EXPERTS, D, FF), D ** -0.5, 0.125, ((0, 8), (2, 2)))
    w_down = centred(arg_keys[5], (EXPERTS, FF, D), FF ** -0.5, 0.21875, ((0, 8), (1, 2)))
    codes = place_ends(jax.random.randint(part_splits[6], (SESSIONS, STEPS, CODEBOOKS), 0, CODES), jax.random.fold_in(part_splits[6], 1), 0, CODES - 1).astype(jnp.int32)
    owner_slot = draw_owner_slot(jax.random.fold_in(jax.random.fold_in(arg_keys[13], part), 71), part)
    code_table = centred(arg_keys[8], (CODEBOOKS, CODES, DC), 0.25, 1.5, ((1, 8),))
    conv_state = centred(part_splits[9], (SESSIONS, STATE, DC), 1.0, 6.0, ((0, 16),))
    conv_taps = centred(arg_keys[10], (KERNEL, DC), 0.4, 2.4, (), jnp.float32)
    conv_bias = centred(arg_keys[11], (DC,), 0.5, 3.0, (), jnp.float32)
    upsample = centred(arg_keys[12], (DC, UP * OUT_CH), DC ** -0.5, 0.1875)
    return dict(hidden_rows=hidden_rows, expert_ids=expert_ids, route_weights=route_weights, w_gate=w_gate, w_up=w_up, w_down=w_down, codes=codes, owner_slot=owner_slot, code_table=code_table, conv_state=conv_state, conv_taps=conv_taps, conv_bias=conv_bias, upsample=upsample)


def round_half(value):
    return lax.optimization_barrier(value.astype(jnp.bfloat16)).astype(jnp.float32)


def reference(hidden_rows, expert_ids, route_weights, w_gate, w_up, w_down, codes, owner_slot, code_table, conv_state, conv_taps, conv_bias, upsample):
    row_total = SESSIONS * STEPS
    tok_rows = hidden_rows.reshape(row_total, D)
    chosen = expert_ids.reshape(row_total * TOP).astype(jnp.int32)
    weights_flat = route_weights.reshape(row_total * TOP)
    most = N_EXPERT * N_WAVE * CAP
    group_width = FF // N_WAVE

    def one_expert(total, index):
        hit = chosen == index
        picked = jnp.nonzero(hit, size=most, fill_value=0)[0].astype(jnp.int32)
        valid = (jnp.arange(most, dtype=jnp.int32) < jnp.sum(hit.astype(jnp.int32))).astype(jnp.float32)
        source = picked // TOP
        inputs = tok_rows[source]
        gate_val = jnp.dot(inputs, w_gate[index], preferred_element_type=jnp.float32)
        up_val = jnp.dot(inputs, w_up[index], preferred_element_type=jnp.float32)
        activated = (jax.nn.silu(gate_val) * up_val).astype(jnp.bfloat16)
        down_rows = w_down[index]
        summed = jnp.zeros((most, D), jnp.float32)
        for group in range(N_WAVE):
            term = jnp.dot(activated[:, group * group_width:(group + 1) * group_width], down_rows[group * group_width:(group + 1) * group_width], preferred_element_type=jnp.float32)
            summed = summed + round_half(term)
        slot_out = round_half(summed)
        total = total.at[source].add(slot_out * (weights_flat[picked] * valid)[:, None])
        return total, None

    mixed, _ = lax.scan(one_expert, jnp.zeros((row_total, D), jnp.float32), jnp.arange(EXPERTS, dtype=jnp.int32))
    moe_out = mixed.astype(jnp.bfloat16).reshape(SESSIONS, STEPS, D)

    books = jnp.arange(CODEBOOKS, dtype=jnp.int32)
    looked = code_table[books[None, None, :], codes].astype(jnp.float32)
    frames = jnp.sum(looked, axis=2)
    owned = jnp.zeros((SESSIONS, STEPS, DC), jnp.float32).at[owner_slot].set(frames)
    history = jnp.concatenate([conv_state.astype(jnp.float32), owned], axis=1)
    filtered = jnp.broadcast_to(conv_bias, (SESSIONS, STEPS, DC))
    for offset in range(KERNEL):
        filtered = filtered + conv_taps[offset] * history[:, STATE - offset:STATE - offset + STEPS]
    decoded = jax.nn.gelu(filtered).astype(jnp.bfloat16)
    samples = jnp.dot(decoded.reshape(SESSIONS * STEPS, DC), upsample, preferred_element_type=jnp.float32)
    waveform = samples.astype(jnp.bfloat16).reshape(SESSIONS, STEPS, UP * OUT_CH)
    new_state = history[:, STEPS:].astype(jnp.bfloat16)
    return (moe_out, waveform, new_state)
```

```python
import functools

import jax
import jax.numpy as jnp
from jax import lax
from jax.experimental import pallas as pl
from jax.experimental.pallas import tpu as pltpu
from jax.sharding import PartitionSpec as P

F32 = jnp.float32
BF16 = jnp.bfloat16
VMEM_LIMIT = 56 * 1024 * 1024


def ring_order(count):
    return list(range(0, count, 2)) + list(range(1, count, 2))[::-1]


def shift(value, distance):
    count = lax.axis_size("expert")
    ring = ring_order(count)
    pairs = [(ring[i], ring[(i + distance) % count]) for i in range(count)]
    return lax.ppermute(value, "expert", pairs)


def swap_wave(value):
    return lax.ppermute(value, "wave", [(0, 1), (1, 0)])


def spread(own):
    count = lax.axis_size("expert")
    half = count // 2
    blocks, step_of = {0: own}, {0: 0}

    def put(offset, value, step):
        blocks[offset % count], step_of[offset % count] = value, step

    put(-1, shift(own, 1), 1)
    put(1, shift(own, -1), 1)
    put(half, shift(own, half), 1)
    for step in range(2, count // 4 + 1):
        put(-step, shift(blocks[(1 - step) % count], 1), step)
        put(step, shift(blocks[step - 1], -1), step)
        put(half - step + 1, shift(blocks[half - step + 2], 1), step)
        put(half + step - 1, shift(blocks[half + step - 2], -1), step)
    return blocks, step_of


def add(*parts):
    total = parts[0].astype(F32)
    for part in parts[1:]:
        total = total + part.astype(F32)
    return total


def collect(parts):
    count = lax.axis_size("expert")
    half = count // 2
    parts = dict(parts)
    for step in range(count // 4, 1, -1):
        moves = (
            (step, 1, step - 1),
            (-step, -1, 1 - step),
            (half + step - 1, 1, half + step - 2),
            (half - step + 1, -1, half - step + 2),
        )
        arrived = [(into % count, shift(parts[come % count], way)) for come, way, into in moves]
        for into in dict(arrived):
            terms = [value for place, value in arrived if place == into]
            parts[into] = add(parts[into], *terms).astype(BF16)
    return parts[0], shift(parts[1], 1), shift(parts[count - 1], -1), shift(parts[half], half)


def experts_kernel(width, expert_count, block_count, first_ref, *refs):
    blocks = refs[:block_count]
    gate_hbm, up_hbm, down_hbm, out_ref, rows_ref, gate_up, down, act_ref, sems = refs[block_count:]
    local = gate_hbm.shape[0]
    units = gate_hbm.shape[2]
    copies = []
    for j in range(local):
        copies.append(
            (
                pltpu.make_async_copy(gate_hbm.at[j], gate_up.at[j, :, 0:units], sems.at[j, 0]),
                pltpu.make_async_copy(
                    up_hbm.at[j], gate_up.at[j, :, units : 2 * units], sems.at[j, 1]
                ),
            )
        )
        for copy in copies[-1]:
            copy.start()
    down_copies = [
        pltpu.make_async_copy(down_hbm.at[j], down.at[j * units : (j + 1) * units], sems.at[j, 2])
        for j in range(local)
    ]
    for copy in down_copies:
        copy.start()
    rows = blocks[0].shape[0]
    weights = []
    for i, block in enumerate(blocks):
        rows_ref[i * rows : (i + 1) * rows, :] = block[:, 0:width]
    meta = jnp.concatenate([block[:, width:].astype(F32) for block in blocks], axis=0)
    lane = lax.broadcasted_iota(jnp.int32, meta.shape, 1)
    first = first_ref[0]
    for j in range(local):
        mine = (lane == first + j) | (lane == expert_count + first + j)
        weights.append(jnp.sum(jnp.where(mine, meta, 0.0), axis=1, keepdims=True))
    for j in range(local):
        for copy in copies[j]:
            copy.wait()
        both = jnp.dot(rows_ref[...], gate_up[j], preferred_element_type=F32)
        gate = both[:, 0:units]
        value = gate * jax.nn.sigmoid(gate) * both[:, units:]
        act_ref[:, j * units : (j + 1) * units] = (value * weights[j]).astype(BF16)
    for copy in down_copies:
        copy.wait()
    out_ref[...] = jnp.dot(act_ref[...], down[...], preferred_element_type=F32).astype(BF16)


def experts(blocks, first, w_gate, w_up, w_down, expert_count):
    local, width, units = w_gate.shape
    rows = blocks[0].shape[0]
    total = rows * len(blocks)
    vmem = pl.BlockSpec(memory_space=pltpu.VMEM)
    hbm = pl.BlockSpec(memory_space=pl.ANY)
    return pl.pallas_call(
        functools.partial(experts_kernel, width, expert_count, len(blocks)),
        out_shape=jax.ShapeDtypeStruct((total, width), BF16),
        in_specs=[pl.BlockSpec(memory_space=pltpu.SMEM)] + [vmem] * len(blocks) + [hbm] * 3,
        out_specs=vmem,
        scratch_shapes=[
            pltpu.VMEM((total, width), BF16),
            pltpu.VMEM((local, width, 2 * units), BF16),
            pltpu.VMEM((local * units, width), BF16),
            pltpu.VMEM((total, local * units), BF16),
            pltpu.SemaphoreType.DMA((local, 3)),
        ],
        compiler_params=pltpu.CompilerParams(vmem_limit_bytes=VMEM_LIMIT),
        cost_estimate=pl.CostEstimate(
            flops=6 * total * width * units * local,
            bytes_accessed=6 * local * width * units,
            transcendentals=total * units * local,
        ),
        name="experts",
    )(first, *blocks, w_gate, w_up, w_down)


def frames_kernel(columns, books, shard, sessions, steps, where_ref, *refs):
    metas = refs[:-3]
    table_ref, out_ref, hot_ref = refs[-3:]
    code_at, slot_at = columns
    rows = metas[0].shape[0]
    meta = jnp.concatenate([m[...] for m in metas], axis=0)
    total = meta.shape[0]
    slot = meta[:, slot_at : slot_at + 2].astype(F32)
    source = (slot[:, 0:1] + 256.0 * slot[:, 1:2]).astype(jnp.int32)
    lane = lax.broadcasted_iota(jnp.int32, (1, total), 1)
    inside = lane % rows
    target = (inside % sessions) * steps + inside // sessions
    for k in range(len(metas)):
        target = target + jnp.where(lane // rows == k, where_ref[k + 1] * rows, 0)
    chooser = jnp.where(source == target, 1.0, 0.0).astype(BF16)
    ordered = lax.dot_general(
        chooser, meta, (((0,), (0,)), ((), ())), preferred_element_type=F32
    )
    low = ordered[:, code_at : code_at + books]
    high = ordered[:, code_at + books : code_at + 2 * books]
    codes = (low + 256.0 * high).astype(jnp.int32) - where_ref[0] * shard
    chunk = 128
    lanes = lax.broadcasted_iota(jnp.int32, (total, chunk), 1)
    for start in range(0, books * shard, chunk):
        first, last = start // shard, (start + chunk - 1) // shard
        code = codes[:, first : first + 1] + (first * shard - start)
        for q in range(first + 1, last + 1):
            shifted = codes[:, q : q + 1] + (q * shard - start)
            code = jnp.where(lanes >= q * shard - start, shifted, code)
        low_end = jnp.maximum(lanes // shard if shard < chunk else 0, 0) * shard
        if shard < chunk:
            hit = (lanes == code) & (code >= low_end) & (code < low_end + shard)
        else:
            hit = (lanes == code)
        hot_ref[:, start : start + chunk] = jnp.where(hit, 1.0, 0.0).astype(BF16)
    out_ref[...] = jnp.dot(hot_ref[...], table_ref[...], preferred_element_type=F32).astype(BF16)


def frame_sums(blocks, where, code_table, columns, width, sessions, steps):
    books, shard, channels = code_table.shape
    rows = blocks[0].shape[0]
    total = rows * len(blocks)
    meta_width = blocks[0].shape[1] - width
    vmem = pl.BlockSpec(memory_space=pltpu.VMEM)
    return pl.pallas_call(
        functools.partial(frames_kernel, columns, books, shard, sessions, steps),
        grid=(1,),
        out_shape=jax.ShapeDtypeStruct((total, channels), BF16),
        in_specs=[pl.BlockSpec(memory_space=pltpu.SMEM)]
        + [pl.BlockSpec((rows, meta_width), lambda i: (0, width // meta_width))] * len(blocks)
        + [vmem],
        out_specs=vmem,
        scratch_shapes=[pltpu.VMEM((total, books * shard), BF16)],
        compiler_params=pltpu.CompilerParams(vmem_limit_bytes=VMEM_LIMIT),
        cost_estimate=pl.CostEstimate(
            flops=2 * total * books * shard * channels,
            bytes_accessed=2 * books * shard * channels,
            transcendentals=0,
        ),
        name="frame_sums",
    )(where, *blocks, code_table.reshape(books * shard, channels))


def decoder_kernel(
    own_ref, one_ref, two_ref, three_ref, state_ref, taps_ref, bias_ref, up_ref, wave_ref, new_ref
):
    past, sessions, _ = state_ref.shape
    taps = taps_ref.shape[0]
    frames = (
        own_ref[...].astype(F32)
        + one_ref[...].astype(F32)
        + two_ref[...].astype(F32)
        + three_ref[...].astype(F32)
    )
    steps = frames.shape[0] // sessions
    history = [state_ref[i].astype(F32) for i in range(past)]
    history += [frames[t * sessions : (t + 1) * sessions] for t in range(steps)]
    outs = []
    for t in range(steps):
        filtered = bias_ref[...] + taps_ref[0:1, :] * history[past + t]
        for j in range(1, taps):
            filtered = filtered + taps_ref[j : j + 1, :] * history[past + t - j]
        outs.append(jax.nn.gelu(filtered).astype(BF16))
    decoded = jnp.concatenate(outs, axis=0)
    wave_ref[...] = jnp.dot(decoded, up_ref[...], preferred_element_type=F32).astype(BF16)
    for i in range(past):
        new_ref[i] = history[i + steps].astype(BF16)


def decoder(terms, conv_state, conv_taps, conv_bias, upsample):
    sessions, past, channels = conv_state.shape
    rows = terms[0].shape[0]
    wave, state = pl.pallas_call(
        decoder_kernel,
        out_shape=(
            jax.ShapeDtypeStruct((rows, upsample.shape[1]), BF16),
            jax.ShapeDtypeStruct((past, sessions, channels), BF16),
        ),
        compiler_params=pltpu.CompilerParams(vmem_limit_bytes=VMEM_LIMIT),
        name="decoder",
    )(
        *terms,
        jnp.transpose(conv_state, (1, 0, 2)),
        conv_taps,
        conv_bias.reshape(1, channels),
        upsample,
    )
    wave = jnp.transpose(wave.reshape(rows // sessions, sessions, -1), (1, 0, 2))
    return wave, jnp.transpose(state, (1, 0, 2))


def per_device(
    hidden_rows,
    expert_ids,
    route_weights,
    w_gate,
    w_up,
    w_down,
    codes,
    owner_slot,
    code_table,
    conv_state,
    conv_taps,
    conv_bias,
    upsample,
):
    count = lax.axis_size("expert")
    n_wave = lax.axis_size("wave")
    sessions, steps, width = hidden_rows.shape
    books = codes.shape[2]
    rows = sessions * steps
    local = w_gate.shape[0]
    expert_count = count * local
    place = lax.axis_index("expert")

    named = (expert_ids[..., None] == jnp.arange(expert_count, dtype=jnp.int32)).astype(F32)
    weight = jnp.sum(named * route_weights[..., None], axis=2)
    high = lax.reduce_precision(weight, 8, 7)
    low = weight - high
    slot = owner_slot // sessions // n_wave * sessions + owner_slot % sessions
    slot = slot[:, None, None] * steps + jnp.arange(steps, dtype=jnp.int32)[None, :, None]
    meta = jnp.concatenate(
        [high.astype(BF16), low.astype(BF16)]
        + [v.astype(BF16) for v in (codes % 256, codes // 256, slot % 256, slot // 256)],
        axis=2,
    ).reshape(rows, -1)
    meta_width = -(-meta.shape[1] // 128) * 128
    meta = jnp.pad(meta, ((0, 0), (0, meta_width - meta.shape[1])))
    columns = (2 * expert_count, 2 * expert_count + 2 * books)

    own = jnp.concatenate([hidden_rows.reshape(rows, width), meta], axis=1)
    blocks, step_of = spread(own)
    other = {k: swap_wave(v) for k, v in blocks.items()}

    ring = jnp.asarray(ring_order(count), jnp.int32)
    mine = jnp.argmax(ring == place).astype(jnp.int32)
    order = list(range(count))
    where = jnp.concatenate([place[None], jnp.take(ring, (mine + jnp.arange(count)) % count)])
    where = where.astype(jnp.int32)
    sums = frame_sums(
        [blocks[k] for k in order], where, code_table, columns, width, sessions, steps
    )
    frame_terms = collect({k: sums[k * rows : (k + 1) * rows] for k in order})

    first = (place * local).astype(jnp.int32)[None]
    by_step = sorted(order, key=lambda k: step_of[k])
    parts = {}
    for start in range(0, count, 4):
        group = by_step[start : start + 4]
        taken = [blocks[k] for k in group] + [other[k] for k in group]
        result = experts(taken, first, w_gate, w_up, w_down, expert_count)
        split = rows * len(group)
        from_other = swap_wave(result[split:])
        for i, k in enumerate(group):
            at = slice(i * rows, (i + 1) * rows)
            parts[k] = add(result[:split][at], from_other[at]).astype(BF16)
    mixed = add(*collect(parts)).astype(BF16)
    samples, carried = decoder(frame_terms, conv_state, conv_taps, conv_bias, upsample)
    return mixed.reshape(sessions, steps, width), samples, carried


def solution(mesh):
    rows = P(("groups", "expert", "wave"), None, None)
    placed = (
        rows,
        rows,
        rows,
        P("expert", None, "wave"),
        P("expert", None, "wave"),
        P("expert", "wave", None),
        rows,
        P(("groups", "expert", "wave")),
        P(None, "expert", None),
        rows,
        P(),
        P(),
        P(),
    )
    return jax.shard_map(
        per_device,
        mesh=mesh,
        in_specs=placed,
        out_specs=(rows, rows, rows),
        check_vma=False,
    )
```

```python
import functools

import jax
import jax.numpy as jnp
from jax import lax
from jax.experimental import pallas as pl
from jax.experimental.pallas import tpu as pltpu
from jax.sharding import PartitionSpec as P

F32 = jnp.float32
BF16 = jnp.bfloat16
VMEM_LIMIT = 28 * 1024 * 1024


def ring_order(count):
    return list(range(0, count, 2)) + list(range(1, count, 2))[::-1]


def shift(value, distance):
    count = lax.axis_size("expert")
    ring = ring_order(count)
    pairs = [(ring[i], ring[(i + distance) % count]) for i in range(count)]
    return lax.ppermute(value, "expert", pairs)


def swap_wave(value):
    return lax.ppermute(value, "wave", [(0, 1), (1, 0)])


def spread(own):
    count = lax.axis_size("expert")
    half = count // 2
    blocks = {0: own}
    blocks[half] = shift(own, half)
    blocks[count - 1] = shift(own, 1)
    blocks[1] = shift(own, -1)
    for step in range(2, count // 4 + 1):
        blocks[count - step] = shift(blocks[count - step + 1], 1)
        blocks[step] = shift(blocks[step - 1], -1)
        blocks[half - step + 1] = shift(blocks[half - step + 2], 1)
        blocks[half + step - 1] = shift(blocks[half + step - 2], -1)
    return blocks


def groups_of_four(count):
    half = count // 2
    later = [
        [step, half + step - 1, count - step, half - step + 1] for step in range(2, count // 4 + 1)
    ]
    return [[0, 1, count - 1, half]] + later


def add(*parts):
    total = parts[0].astype(F32)
    for part in parts[1:]:
        total = total + part.astype(F32)
    return total


def collect(first, later, rows):
    forward = backward = None
    for pair in later[::-1]:
        if forward is not None:
            pair = (add(pair[0], forward).astype(BF16), add(pair[1], backward).astype(BF16))
        forward, backward = shift(pair[0], 1), shift(pair[1], -1)
    own, one, minus, across = first
    if forward is not None:
        one = add(one, forward[:rows]).astype(BF16)
        minus = add(minus, backward[:rows]).astype(BF16)
        across = add(across, forward[rows:], backward[rows:]).astype(BF16)
    half = lax.axis_size("expert") // 2
    return own, shift(across, half), shift(one, 1), shift(minus, -1)


def after(values, *earlier):
    return lax.optimization_barrier((tuple(values), earlier))[0]


def spot(rows, columns, offset):
    down = lax.broadcasted_iota(jnp.int32, (rows, columns), 0)
    across = lax.broadcasted_iota(jnp.int32, (rows, columns), 1)
    return jnp.where(across == down + offset, 1.0, 0.0).astype(BF16)


def digits(value):
    return [(value % 256).astype(F32).astype(BF16), (value // 256).astype(F32).astype(BF16)]


def pack_kernel(columns, n_wave, hidden_ref, ids_ref, weights_ref, codes_ref, owner_ref, out_ref):
    sessions, steps, width = hidden_ref.shape
    expert_count = columns[0] // 2
    books = codes_ref.shape[2]
    meta_width = out_ref.shape[1] - width
    owner = owner_ref[...]
    slots = (owner // sessions // n_wave) * sessions + owner % sessions
    down = lax.broadcasted_iota(jnp.int32, (sessions, sessions), 0)
    across = lax.broadcasted_iota(jnp.int32, (sessions, sessions), 1)
    slot = jnp.sum(jnp.where(down == across, slots, 0).astype(F32), axis=1, keepdims=True)
    slot = slot.astype(jnp.int32)
    lane = lax.broadcasted_iota(jnp.int32, (sessions, meta_width), 1)
    named = lax.broadcasted_iota(jnp.int32, (expert_count, sessions), 0)
    for t in range(steps):
        at = slice(t * sessions, (t + 1) * sessions)
        out_ref[at, 0:width] = hidden_ref[:, t, :]
        weight = jnp.zeros((expert_count, sessions), F32)
        for k in range(ids_ref.shape[1]):
            weight += jnp.where(named == ids_ref[t, k : k + 1, :], weights_ref[t, k : k + 1, :], 0.0)
        high = weight.astype(BF16)
        low = (weight - high.astype(F32)).astype(BF16)
        meta = jnp.zeros((sessions, meta_width), F32)
        for piece, offset in ((high, 0), (low, expert_count)):
            meta += lax.dot_general(
                piece,
                spot(expert_count, meta_width, offset),
                (((0,), (0,)), ((), ())),
                preferred_element_type=F32,
            )
        for i, piece in enumerate(digits(codes_ref[:, t, :])):
            move = spot(books, meta_width, columns[0] + i * books)
            meta += jnp.dot(piece, move, preferred_element_type=F32)
        for i, piece in enumerate(digits(slot * steps + t)):
            meta += jnp.where(lane == columns[1] + i, piece.astype(F32), 0.0)
        out_ref[at, width:] = meta.astype(BF16)


def pack(hidden_rows, expert_ids, route_weights, codes, owner_slot, columns, n_wave):
    sessions, steps, width = hidden_rows.shape
    meta_width = -(-(columns[1] + 2) // 128) * 128
    return pl.pallas_call(
        functools.partial(pack_kernel, columns, n_wave),
        out_shape=jax.ShapeDtypeStruct((steps * sessions, width + meta_width), BF16),
        compiler_params=pltpu.CompilerParams(vmem_limit_bytes=VMEM_LIMIT),
        name="pack",
    )(
        hidden_rows,
        jnp.transpose(expert_ids, (1, 2, 0)),
        jnp.transpose(route_weights, (1, 2, 0)),
        codes,
        owner_slot[None],
    )


def experts_kernel(width, expert_count, counts, place_ref, *refs):
    blocks = refs[: sum(counts)]
    gate_ref, up_ref, down_ref = refs[sum(counts) : sum(counts) + 3]
    outs = refs[sum(counts) + 3 : -2]
    rows_ref, act_ref = refs[-2:]
    local, _, units = gate_ref.shape
    rows = blocks[0].shape[0]
    for i, block in enumerate(blocks):
        rows_ref[i * rows : (i + 1) * rows, :] = block[:, 0:width]
    meta = jnp.concatenate([block[:, width:].astype(F32) for block in blocks], axis=0)
    lane = lax.broadcasted_iota(jnp.int32, meta.shape, 1)
    for j in range(local):
        mine = place_ref[0] * local + j
        hit = (lane == mine) | (lane == expert_count + mine)
        weight = jnp.sum(jnp.where(hit, meta, 0.0), axis=1, keepdims=True)
        gate = jnp.dot(rows_ref[...], gate_ref[j], preferred_element_type=F32)
        up = jnp.dot(rows_ref[...], up_ref[j], preferred_element_type=F32)
        value = gate * jax.nn.sigmoid(gate) * up
        act_ref[:, j * units : (j + 1) * units] = (value * weight).astype(BF16)
    start = 0
    for out_ref in outs:
        size = out_ref.shape[0]
        act = act_ref[start : start + size, :]
        out_ref[...] = jnp.dot(act, down_ref[...], preferred_element_type=F32).astype(BF16)
        start += size


def experts(parts, place, w_gate, w_up, w_down):
    local, width, units = w_gate.shape
    counts = [len(blocks) for blocks in parts]
    blocks = [block for part in parts for block in part]
    rows = blocks[0].shape[0]
    total = rows * len(blocks)
    vmem = pl.BlockSpec(memory_space=pltpu.VMEM)
    return pl.pallas_call(
        functools.partial(
            experts_kernel, width, lax.axis_size("expert") * local, tuple(counts)
        ),
        out_shape=[jax.ShapeDtypeStruct((rows * c, width), BF16) for c in counts],
        in_specs=[pl.BlockSpec(memory_space=pltpu.SMEM)] + [vmem] * (len(blocks) + 3),
        out_specs=[vmem] * len(counts),
        scratch_shapes=[
            pltpu.VMEM((total, width), BF16),
            pltpu.VMEM((total, local * units), BF16),
        ],
        compiler_params=pltpu.CompilerParams(vmem_limit_bytes=VMEM_LIMIT),
        cost_estimate=pl.CostEstimate(
            flops=6 * total * width * units * local,
            bytes_accessed=6 * local * width * units,
            transcendentals=total * units * local,
        ),
        name="experts",
    )(place, *blocks, w_gate, w_up, w_down.reshape(local * units, width))


def frames_kernel(columns, books, shard, sessions, steps, order, place_ref, *refs):
    metas = refs[: len(order)]
    table_ref, out_ref, hot_ref = refs[len(order) :]
    count = len(order)
    code_at, slot_at = columns
    rows = metas[0].shape[0]
    meta = jnp.concatenate([m[...] for m in metas], axis=0)
    total = meta.shape[0]
    slot = meta[:, slot_at : slot_at + 2].astype(F32)
    source = (slot[:, 0:1] + 256.0 * slot[:, 1:2]).astype(jnp.int32)
    lane = lax.broadcasted_iota(jnp.int32, (1, total), 1)
    inside = lane % rows
    target = (inside % sessions) * steps + inside // sessions
    place = place_ref[0]
    turn = jnp.where(place % 2 == 0, place // 2, count - 1 - place // 2)
    for i, k in enumerate(order):
        at = (turn + k) % count
        device = jnp.where(at < count // 2, 2 * at, 2 * (count - 1 - at) + 1)
        target = target + jnp.where(lane // rows == i, device * rows, 0)
    chooser = jnp.where(source == target, 1.0, 0.0).astype(BF16)
    ordered = lax.dot_general(
        chooser, meta, (((0,), (0,)), ((), ())), preferred_element_type=F32
    )
    low = ordered[:, code_at : code_at + books]
    high = ordered[:, code_at + books : code_at + 2 * books]
    codes = (low + 256.0 * high).astype(jnp.int32) - place * shard
    chunk = 128
    lanes = lax.broadcasted_iota(jnp.int32, (total, chunk), 1)
    for start in range(0, books * shard, chunk):
        first, last = start // shard, (start + chunk - 1) // shard
        code = codes[:, first : first + 1] + (first * shard - start)
        for q in range(first + 1, last + 1):
            shifted = codes[:, q : q + 1] + (q * shard - start)
            code = jnp.where(lanes >= q * shard - start, shifted, code)
        hit = lanes == code
        if shard < chunk:
            low_end = lanes // shard * shard
            hit = hit & (code >= low_end) & (code < low_end + shard)
        hot_ref[:, start : start + chunk] = jnp.where(hit, 1.0, 0.0).astype(BF16)
    out_ref[...] = jnp.dot(hot_ref[...], table_ref[...], preferred_element_type=F32).astype(BF16)


def frame_sums(blocks, order, place, code_table, columns, width, sessions, steps):
    books, shard, channels = code_table.shape
    rows = blocks[0].shape[0]
    total = rows * len(order)
    meta_width = blocks[0].shape[1] - width
    vmem = pl.BlockSpec(memory_space=pltpu.VMEM)
    return pl.pallas_call(
        functools.partial(frames_kernel, columns, books, shard, sessions, steps, order),
        grid=(1,),
        out_shape=jax.ShapeDtypeStruct((total, channels), BF16),
        in_specs=[pl.BlockSpec(memory_space=pltpu.SMEM)]
        + [pl.BlockSpec((rows, meta_width), lambda i: (0, width // meta_width))] * len(order)
        + [vmem],
        out_specs=vmem,
        scratch_shapes=[pltpu.VMEM((total, books * shard), BF16)],
        compiler_params=pltpu.CompilerParams(vmem_limit_bytes=VMEM_LIMIT),
        cost_estimate=pl.CostEstimate(
            flops=2 * total * books * shard * channels,
            bytes_accessed=2 * books * shard * channels,
            transcendentals=0,
        ),
        name="frame_sums",
    )(place, *[blocks[k] for k in order], code_table.reshape(books * shard, channels))


def decoder_kernel(*refs):
    terms, (state_ref, taps_ref, bias_ref, up_ref, wave_ref, new_ref) = refs[:-6], refs[-6:]
    past, sessions, _ = state_ref.shape
    taps = taps_ref.shape[0]
    frames = terms[0][...].astype(F32)
    for term in terms[1:]:
        frames = frames + term[...].astype(F32)
    steps = frames.shape[0] // sessions
    history = [state_ref[i].astype(F32) for i in range(past)]
    history += [frames[t * sessions : (t + 1) * sessions] for t in range(steps)]
    for t in range(steps):
        filtered = bias_ref[...] + taps_ref[0:1, :] * history[past + t]
        for j in range(1, taps):
            filtered = filtered + taps_ref[j : j + 1, :] * history[past + t - j]
        decoded = jax.nn.gelu(filtered).astype(BF16)
        sample = jnp.dot(decoded, up_ref[...], preferred_element_type=F32)
        wave_ref[:, t, :] = sample.astype(BF16)
    for i in range(past):
        new_ref[i] = history[i + steps].astype(BF16)


def decoder(terms, conv_state, conv_taps, conv_bias, upsample):
    sessions, past, channels = conv_state.shape
    steps = terms[0].shape[0] // sessions
    wave, state = pl.pallas_call(
        decoder_kernel,
        out_shape=(
            jax.ShapeDtypeStruct((sessions, steps, upsample.shape[1]), BF16),
            jax.ShapeDtypeStruct((past, sessions, channels), BF16),
        ),
        compiler_params=pltpu.CompilerParams(vmem_limit_bytes=VMEM_LIMIT),
        name="decoder",
    )(
        *terms,
        jnp.transpose(conv_state, (1, 0, 2)),
        conv_taps,
        conv_bias.reshape(1, channels),
        upsample,
    )
    return wave, jnp.transpose(state, (1, 0, 2))


def last_sum_kernel(*refs):
    terms, out_ref = refs[:-1], refs[-1]
    sessions, steps, _ = out_ref.shape
    total = terms[0][...].astype(F32)
    for term in terms[1:]:
        total = total + term[...].astype(F32)
    for t in range(steps):
        out_ref[:, t, :] = total[t * sessions : (t + 1) * sessions].astype(BF16)


def last_sum(terms, shape):
    return pl.pallas_call(
        last_sum_kernel,
        out_shape=jax.ShapeDtypeStruct(shape, BF16),
        compiler_params=pltpu.CompilerParams(vmem_limit_bytes=VMEM_LIMIT),
        name="last_sum",
    )(*terms)


def per_device(
    hidden_rows,
    expert_ids,
    route_weights,
    w_gate,
    w_up,
    w_down,
    codes,
    owner_slot,
    code_table,
    conv_state,
    conv_taps,
    conv_bias,
    upsample,
):
    count = lax.axis_size("expert")
    sessions, steps, width = hidden_rows.shape
    rows = sessions * steps
    books = codes.shape[2]
    expert_count = count * w_gate.shape[0]
    place = lax.axis_index("expert").astype(jnp.int32)[None]
    columns = (2 * expert_count, 2 * expert_count + 2 * books)

    own = pack(
        hidden_rows,
        expert_ids,
        route_weights,
        codes,
        owner_slot,
        columns,
        lax.axis_size("wave"),
    )
    blocks = spread(own)
    other = {k: swap_wave(v) for k, v in blocks.items()}
    groups = groups_of_four(count)

    def work(parts):
        return experts(parts, place, w_gate, w_up, w_down)

    near = groups[0]
    near_other, near_own = work([[other[k] for k in near], [blocks[k] for k in near]])
    near_other = swap_wave(near_other)
    for k in groups[-1]:
        blocks[k], other[k] = after((blocks[k], other[k]), near_own)

    order = [k for group in groups for k in group]
    sums = frame_sums(blocks, order, place, code_table, columns, width, sessions, steps)
    quarter = [sums[i * rows : (i + 1) * rows] for i in range(4)]
    pairs = [
        (sums[i * rows : (i + 2) * rows], sums[(i + 2) * rows : (i + 4) * rows])
        for i in range(4, count, 4)
    ]
    frames = collect(quarter, pairs, rows)

    later = []
    for group in groups[1:]:
        (from_other,) = work([[other[k] for k in group]])
        from_other = swap_wave(from_other)
        (result,) = work([[blocks[k] for k in group]])
        both = [
            add(result[at], from_other[at]).astype(BF16)
            for at in (slice(0, 2 * rows), slice(2 * rows, 4 * rows))
        ]
        later.append(both)
    first = [
        add(near_own[i * rows : (i + 1) * rows], near_other[i * rows : (i + 1) * rows])
        for i in range(4)
    ]
    first = [first[0]] + [v.astype(BF16) for v in first[1:]]
    terms = collect(first, later, rows)
    samples, carried = decoder(frames, conv_state, conv_taps, conv_bias, upsample)
    terms = after(terms, samples)
    mixed = last_sum(terms, hidden_rows.shape)
    return mixed, samples, carried


def solution(mesh):
    rows = P(("groups", "expert", "wave"), None, None)
    placed = (
        rows,
        rows,
        rows,
        P("expert", None, "wave"),
        P("expert", None, "wave"),
        P("expert", "wave", None),
        rows,
        P(("groups", "expert", "wave")),
        P(None, "expert", None),
        rows,
        P(),
        P(),
        P(),
    )
    return jax.shard_map(
        per_device,
        mesh=mesh,
        in_specs=placed,
        out_specs=(rows, rows, rows),
        check_vma=False,
    )
```

```python
import functools

import jax
import jax.numpy as jnp
from jax import lax
from jax.experimental import pallas as pl
from jax.experimental.pallas import tpu as pltpu
from jax.sharding import PartitionSpec as P

F32 = jnp.float32
BF16 = jnp.bfloat16
VMEM_LIMIT = 28 * 1024 * 1024


def ring_order(count):
    return list(range(0, count, 2)) + list(range(1, count, 2))[::-1]


def shift(value, distance):
    count = lax.axis_size("expert")
    ring = ring_order(count)
    pairs = [(ring[i], ring[(i + distance) % count]) for i in range(count)]
    return lax.ppermute(value, "expert", pairs)


def swap_wave(value):
    return lax.ppermute(value, "wave", [(0, 1), (1, 0)])


def collect(parts, hold):
    count = lax.axis_size("expert")
    half = count // 2
    parts = dict(parts)
    for step in range(count // 4, 1, -1):
        moves = (
            (step, 1, step - 1),
            (count - step, -1, count + 1 - step),
            (half + step - 1, 1, half + step - 2),
            (half - step + 1, -1, half - step + 2),
        )
        arrived = [(into, shift(parts[come], way)) for come, way, into in moves]
        for into in dict(arrived):
            terms = [value for place, value in arrived if place == into]
            parts[into] = add(parts[into], *terms).astype(BF16)
    nearest = (parts[1], parts[count - 1], parts[half])
    one, minus, across = hold(nearest) or nearest
    return parts[0], shift(across, half), shift(one, 1), shift(minus, -1)


def add(*parts):
    total = parts[0].astype(F32)
    for part in parts[1:]:
        total = total + part.astype(F32)
    return total


def after(values, *earlier):
    return lax.optimization_barrier((tuple(values), earlier))[0]


def spot(rows, columns, offset):
    down = lax.broadcasted_iota(jnp.int32, (rows, columns), 0)
    across = lax.broadcasted_iota(jnp.int32, (rows, columns), 1)
    return jnp.where(across == down + offset, 1.0, 0.0).astype(BF16)


def digits(value):
    return [(value % 256).astype(F32).astype(BF16), (value // 256).astype(F32).astype(BF16)]


def pack_kernel(columns, n_wave, *refs):
    sources, out_ref, (hidden_ref, ids_ref, weights_ref, codes_ref, owner_ref, sems) = (
        refs[:5],
        refs[5],
        refs[6:],
    )
    copies = [
        pltpu.make_async_copy(source, held, sems.at[i])
        for i, (source, held) in enumerate(zip(sources, refs[6:11]))
    ]
    for copy in copies:
        copy.start()
    for copy in copies:
        copy.wait()
    sessions, steps, width = hidden_ref.shape
    expert_count = columns[0] // 2
    books = codes_ref.shape[2]
    meta_width = out_ref.shape[1] - width
    owner = owner_ref[...]
    slots = (owner // sessions // n_wave) * sessions + owner % sessions
    down = lax.broadcasted_iota(jnp.int32, (sessions, sessions), 0)
    across = lax.broadcasted_iota(jnp.int32, (sessions, sessions), 1)
    slot = jnp.sum(jnp.where(down == across, slots, 0).astype(F32), axis=1, keepdims=True)
    slot = slot.astype(jnp.int32)
    lane = lax.broadcasted_iota(jnp.int32, (sessions, meta_width), 1)
    named = lax.broadcasted_iota(jnp.int32, (expert_count, sessions), 0)
    for t in range(steps):
        at = slice(t * sessions, (t + 1) * sessions)
        out_ref[at, 0:width] = hidden_ref[:, t, :]
        weight = jnp.zeros((expert_count, sessions), F32)
        for k in range(ids_ref.shape[1]):
            weight += jnp.where(named == ids_ref[t, k : k + 1, :], weights_ref[t, k : k + 1, :], 0.0)
        high = weight.astype(BF16)
        low = (weight - high.astype(F32)).astype(BF16)
        meta = jnp.zeros((sessions, meta_width), F32)
        for piece, offset in ((high, 0), (low, expert_count)):
            meta += lax.dot_general(
                piece,
                spot(expert_count, meta_width, offset),
                (((0,), (0,)), ((), ())),
                preferred_element_type=F32,
            )
        for i, piece in enumerate(digits(codes_ref[:, t, :])):
            move = spot(books, meta_width, columns[0] + i * books)
            meta += jnp.dot(piece, move, preferred_element_type=F32)
        for i, piece in enumerate(digits(slot * steps + t)):
            meta += jnp.where(lane == columns[1] + i, piece.astype(F32), 0.0)
        out_ref[at, width:] = meta.astype(BF16)


def pack(hidden_rows, expert_ids, route_weights, codes, owner_slot, columns, n_wave):
    sessions, steps, width = hidden_rows.shape
    meta_width = -(-(columns[1] + 2) // 128) * 128
    args = (
        hidden_rows,
        jnp.transpose(expert_ids, (1, 2, 0)),
        jnp.transpose(route_weights, (1, 2, 0)),
        codes,
        owner_slot[None],
    )
    return pl.pallas_call(
        functools.partial(pack_kernel, columns, n_wave),
        out_shape=jax.ShapeDtypeStruct((steps * sessions, width + meta_width), BF16),
        in_specs=[pl.BlockSpec(memory_space=pltpu.HBM)] * len(args),
        out_specs=pl.BlockSpec(memory_space=pltpu.VMEM),
        scratch_shapes=[pltpu.VMEM(arg.shape, arg.dtype) for arg in args]
        + [pltpu.SemaphoreType.DMA((len(args),))],
        compiler_params=pltpu.CompilerParams(vmem_limit_bytes=VMEM_LIMIT),
        name="pack",
    )(*[pltpu.with_memory_space_constraint(arg, pltpu.HBM) for arg in args])


def load_kernel(*refs):
    count = len(refs) // 2 - 1
    sources, held, sems = refs[1 : count + 1], refs[count + 1 : -1], refs[-1]
    copies = [
        pltpu.make_async_copy(source, ref, sems.at[i])
        for i, (source, ref) in enumerate(zip(sources, held))
    ]
    for copy in copies:
        copy.start()
    for copy in copies:
        copy.wait()


def load(earlier, *arrays):
    hbm = pl.BlockSpec(memory_space=pltpu.HBM)
    return pl.pallas_call(
        load_kernel,
        out_shape=[pltpu.VMEM(v.shape, v.dtype) for v in arrays],
        in_specs=[pl.BlockSpec(memory_space=pl.ANY)] + [hbm] * len(arrays),
        out_specs=[pl.BlockSpec(memory_space=pltpu.VMEM)] * len(arrays),
        scratch_shapes=[pltpu.SemaphoreType.DMA((len(arrays),))],
        compiler_params=pltpu.CompilerParams(vmem_limit_bytes=VMEM_LIMIT),
        cost_estimate=pl.CostEstimate(
            flops=0, bytes_accessed=sum(2 * v.size for v in arrays), transcendentals=0
        ),
        name="load",
    )(earlier, *[pltpu.with_memory_space_constraint(v, pltpu.HBM) for v in arrays])


def experts_kernel(width, expert_count, counts, place_ref, *refs):
    blocks = refs[: sum(counts)]
    gate_ref, up_ref, down_ref = refs[sum(counts) : sum(counts) + 3]
    outs = refs[sum(counts) + 3 : -2]
    rows_ref, act_ref = refs[-2:]
    local, _, units = gate_ref.shape
    rows = blocks[0].shape[0]
    for i, block in enumerate(blocks):
        rows_ref[i * rows : (i + 1) * rows, :] = block[:, 0:width]
    meta = jnp.concatenate([block[:, width:].astype(F32) for block in blocks], axis=0)
    lane = lax.broadcasted_iota(jnp.int32, meta.shape, 1)
    for j in range(local):
        mine = place_ref[0] * local + j
        hit = (lane == mine) | (lane == expert_count + mine)
        weight = jnp.sum(jnp.where(hit, meta, 0.0), axis=1, keepdims=True)
        gate = jnp.dot(rows_ref[...], gate_ref[j], preferred_element_type=F32)
        up = jnp.dot(rows_ref[...], up_ref[j], preferred_element_type=F32)
        value = gate * jax.nn.sigmoid(gate) * up
        act_ref[:, j * units : (j + 1) * units] = (value * weight).astype(BF16)
    start = 0
    for out_ref in outs:
        size = out_ref.shape[0]
        act = act_ref[start : start + size, :]
        out_ref[...] = jnp.dot(act, down_ref[...], preferred_element_type=F32).astype(BF16)
        start += size


def experts(parts, place, w_gate, w_up, w_down):
    local, width, units = w_gate.shape
    counts = [len(blocks) for blocks in parts]
    blocks = [block for part in parts for block in part]
    rows = blocks[0].shape[0]
    total = rows * len(blocks)
    vmem = pl.BlockSpec(memory_space=pltpu.VMEM)
    return pl.pallas_call(
        functools.partial(
            experts_kernel, width, lax.axis_size("expert") * local, tuple(counts)
        ),
        out_shape=[jax.ShapeDtypeStruct((rows * c, width), BF16) for c in counts],
        in_specs=[pl.BlockSpec(memory_space=pltpu.SMEM)] + [vmem] * (len(blocks) + 3),
        out_specs=[vmem] * len(counts),
        scratch_shapes=[
            pltpu.VMEM((total, width), BF16),
            pltpu.VMEM((total, local * units), BF16),
        ],
        compiler_params=pltpu.CompilerParams(vmem_limit_bytes=VMEM_LIMIT),
        cost_estimate=pl.CostEstimate(
            flops=6 * total * width * units * local,
            bytes_accessed=6 * local * width * units,
            transcendentals=total * units * local,
        ),
        name="experts",
    )(place, *blocks, w_gate, w_up, w_down)


def frames_kernel(columns, books, shard, sessions, steps, order, place_ref, *refs):
    metas = refs[: len(order)]
    table_ref, out_ref, hot_ref = refs[len(order) :]
    count = len(order)
    code_at, slot_at = columns
    rows = metas[0].shape[0]
    meta = jnp.concatenate([m[...] for m in metas], axis=0)
    total = meta.shape[0]
    slot = meta[:, slot_at : slot_at + 2].astype(F32)
    source = (slot[:, 0:1] + 256.0 * slot[:, 1:2]).astype(jnp.int32)
    lane = lax.broadcasted_iota(jnp.int32, (1, total), 1)
    inside = lane % rows
    target = (inside % sessions) * steps + inside // sessions
    place = place_ref[0]
    turn = jnp.where(place % 2 == 0, place // 2, count - 1 - place // 2)
    for i, k in enumerate(order):
        at = (turn + k) % count
        device = jnp.where(at < count // 2, 2 * at, 2 * (count - 1 - at) + 1)
        target = target + jnp.where(lane // rows == i, device * rows, 0)
    chooser = jnp.where(source == target, 1.0, 0.0).astype(BF16)
    ordered = lax.dot_general(
        chooser, meta, (((0,), (0,)), ((), ())), preferred_element_type=F32
    )
    low = ordered[:, code_at : code_at + books]
    high = ordered[:, code_at + books : code_at + 2 * books]
    codes = (low + 256.0 * high).astype(jnp.int32) - place * shard
    chunk = 128
    lanes = lax.broadcasted_iota(jnp.int32, (total, chunk), 1)
    for start in range(0, books * shard, chunk):
        first, last = start // shard, (start + chunk - 1) // shard
        code = codes[:, first : first + 1] + (first * shard - start)
        for q in range(first + 1, last + 1):
            shifted = codes[:, q : q + 1] + (q * shard - start)
            code = jnp.where(lanes >= q * shard - start, shifted, code)
        hit = lanes == code
        if shard < chunk:
            low_end = lanes // shard * shard
            hit = hit & (code >= low_end) & (code < low_end + shard)
        hot_ref[:, start : start + chunk] = jnp.where(hit, 1.0, 0.0).astype(BF16)
    out_ref[...] = jnp.dot(hot_ref[...], table_ref[...], preferred_element_type=F32).astype(BF16)


def frame_sums(blocks, order, place, code_table, columns, width, sessions, steps):
    books, shard, channels = code_table.shape
    rows = blocks[0].shape[0]
    total = rows * len(order)
    meta_width = blocks[0].shape[1] - width
    vmem = pl.BlockSpec(memory_space=pltpu.VMEM)
    return pl.pallas_call(
        functools.partial(frames_kernel, columns, books, shard, sessions, steps, order),
        grid=(1,),
        out_shape=jax.ShapeDtypeStruct((total, channels), BF16),
        in_specs=[pl.BlockSpec(memory_space=pltpu.SMEM)]
        + [pl.BlockSpec((rows, meta_width), lambda i: (0, width // meta_width))] * len(order)
        + [vmem],
        out_specs=vmem,
        scratch_shapes=[pltpu.VMEM((total, books * shard), BF16)],
        compiler_params=pltpu.CompilerParams(vmem_limit_bytes=VMEM_LIMIT),
        cost_estimate=pl.CostEstimate(
            flops=2 * total * books * shard * channels,
            bytes_accessed=2 * books * shard * channels,
            transcendentals=0,
        ),
        name="frame_sums",
    )(place, *[blocks[k] for k in order], code_table.reshape(books * shard, channels))


def decoder_kernel(*refs):
    terms, (state_ref, taps_ref, bias_ref, up_ref, wave_ref, new_ref) = refs[:-6], refs[-6:]
    past, sessions, _ = state_ref.shape
    taps = taps_ref.shape[0]
    frames = terms[0][...].astype(F32)
    for term in terms[1:]:
        frames = frames + term[...].astype(F32)
    steps = frames.shape[0] // sessions
    history = [state_ref[i].astype(F32) for i in range(past)]
    history += [frames[t * sessions : (t + 1) * sessions] for t in range(steps)]
    for t in range(steps):
        filtered = bias_ref[...] + taps_ref[0:1, :] * history[past + t]
        for j in range(1, taps):
            filtered = filtered + taps_ref[j : j + 1, :] * history[past + t - j]
        decoded = jax.nn.gelu(filtered).astype(BF16)
        sample = jnp.dot(decoded, up_ref[...], preferred_element_type=F32)
        wave_ref[:, t, :] = sample.astype(BF16)
    for i in range(past):
        new_ref[i] = history[i + steps].astype(BF16)


def decoder(terms, conv_state, conv_taps, conv_bias, upsample):
    sessions, past, channels = conv_state.shape
    steps = terms[0].shape[0] // sessions
    wave, state = pl.pallas_call(
        decoder_kernel,
        out_shape=(
            jax.ShapeDtypeStruct((sessions, steps, upsample.shape[1]), BF16),
            jax.ShapeDtypeStruct((past, sessions, channels), BF16),
        ),
        compiler_params=pltpu.CompilerParams(vmem_limit_bytes=VMEM_LIMIT),
        name="decoder",
    )(
        *terms,
        jnp.transpose(conv_state, (1, 0, 2)),
        conv_taps,
        conv_bias.reshape(1, channels),
        upsample,
    )
    return wave, jnp.transpose(state, (1, 0, 2))


def last_sum_kernel(*refs):
    terms, out_ref = refs[:-1], refs[-1]
    sessions, steps, _ = out_ref.shape
    total = terms[0][...].astype(F32)
    for term in terms[1:]:
        total = total + term[...].astype(F32)
    for t in range(steps):
        out_ref[:, t, :] = total[t * sessions : (t + 1) * sessions].astype(BF16)


def last_sum(terms, shape):
    return pl.pallas_call(
        last_sum_kernel,
        out_shape=jax.ShapeDtypeStruct(shape, BF16),
        compiler_params=pltpu.CompilerParams(vmem_limit_bytes=VMEM_LIMIT),
        name="last_sum",
    )(*terms)


def per_device(
    hidden_rows,
    expert_ids,
    route_weights,
    w_gate,
    w_up,
    w_down,
    codes,
    owner_slot,
    code_table,
    conv_state,
    conv_taps,
    conv_bias,
    upsample,
):
    count = lax.axis_size("expert")
    sessions, steps, width = hidden_rows.shape
    rows = sessions * steps
    books = codes.shape[2]
    expert_count = count * w_gate.shape[0]
    place = lax.axis_index("expert").astype(jnp.int32)[None]
    columns = (2 * expert_count, 2 * expert_count + 2 * books)

    own = pack(
        hidden_rows,
        expert_ids,
        route_weights,
        codes,
        owner_slot,
        columns,
        lax.axis_size("wave"),
    )
    half = count // 2
    local, _, units = w_gate.shape
    held = load(own, w_gate, w_up, w_down.reshape(local * units, width))

    token = [held]

    def work(*parts):
        (turn,) = after((place,), token[0])
        token[0] = experts(parts, turn, *held)
        return token[0]

    blocks, other, mine, swapped = {0: own}, {0: swap_wave(own)}, {}, {}
    behind = ahead = own
    fresh = [0]
    for step in range(1, half + 1):
        behind = shift(behind, 1)
        got = [(count - step, behind)]
        if step < half:
            ahead = shift(ahead, -1)
            got.append((step, ahead))
        got = list(zip([k for k, _ in got], after([v for _, v in got], token[0])))
        behind, ahead = got[0][1], got[-1][1]
        for k, value in got:
            blocks[k], other[k] = value, swap_wave(value)
        if step == 1:
            fresh += [k for k, _ in got]
            continue
        if step < half:
            theirs, ours = work([other[k] for k in fresh], [blocks[k] for k in fresh])
        else:
            (theirs,) = work([other[k] for k in fresh])
            (ours,) = work([blocks[k] for k in fresh])
        theirs = swap_wave(theirs)
        for i, k in enumerate(fresh):
            mine[k], swapped[k] = [v[i * rows : (i + 1) * rows] for v in (ours, theirs)]
        fresh = [k for k, _ in got]
    order = list(range(count))
    parts = {k: add(mine[k], swapped[k]) for k in mine}
    parts = {k: v.astype(BF16) if k else v for k, v in parts.items()}
    (turn,) = after((place,), [parts[k] for k in parts if k not in (0, 1, count - 1)])
    sums = frame_sums(blocks, order, turn, code_table, columns, width, sessions, steps)
    token[0] = sums
    theirs, ours = work([other[k] for k in fresh], [blocks[k] for k in fresh])
    parts[half] = add(ours, swap_wave(theirs)).astype(BF16)

    sends = []
    frames = collect({k: sums[k * rows : (k + 1) * rows] for k in order}, sends.extend)
    samples, carried = decoder(frames, conv_state, conv_taps, conv_bias, upsample)
    terms = collect(parts, lambda values: after(values, sends))
    mixed = last_sum(terms, hidden_rows.shape)
    return mixed, samples, carried


def solution(mesh):
    rows = P(("groups", "expert", "wave"), None, None)
    placed = (
        rows,
        rows,
        rows,
        P("expert", None, "wave"),
        P("expert", None, "wave"),
        P("expert", "wave", None),
        rows,
        P(("groups", "expert", "wave")),
        P(None, "expert", None),
        rows,
        P(),
        P(),
        P(),
    )
    return jax.shard_map(
        per_device,
        mesh=mesh,
        in_specs=placed,
        out_specs=(rows, rows, rows),
        check_vma=False,
    )
```

```python
import functools

import jax
import jax.numpy as jnp
from jax import lax
from jax.experimental import pallas as pl
from jax.experimental.pallas import tpu as pltpu
from jax.sharding import PartitionSpec as P

F32 = jnp.float32
BF16 = jnp.bfloat16
VMEM_LIMIT = 8 * 1024 * 1024


def ring_order(count):
    return list(range(0, count, 2)) + list(range(1, count, 2))[::-1]


def shift(value, distance):
    count = lax.axis_size("expert")
    ring = ring_order(count)
    pairs = [(ring[i], ring[(i + distance) % count]) for i in range(count)]
    return lax.ppermute(value, "expert", pairs)


def swap_wave(value):
    return lax.ppermute(value, "wave", [(0, 1), (1, 0)])


def tidy(plan):
    arrays, numbers = [], {}

    def number(source):
        array, row = source
        if id(array) not in numbers:
            numbers[id(array)] = len(arrays)
            arrays.append(array)
        return numbers[id(array)], row

    return arrays, [[[[number(v) for v in part] for part in block] for block in out] for out in plan]


def summed(refs, sources, rows, columns):
    total = None
    for index, row in sources:
        value = refs[index][row : row + rows, columns].astype(F32)
        total = value if total is None else total + value
    return total


def join_kernel(plan, rows, width, *refs):
    outs = refs[-len(plan) :]
    for out_ref, blocks in zip(outs, plan):
        for i, (left, right, whole) in enumerate(blocks):
            at = slice(i * rows, (i + 1) * rows)
            total = summed(refs, left, rows, slice(None))
            for index, row in whole:
                total = total + refs[index][row : row + rows, 0:width].astype(F32)
            out_ref[at, 0:width] = total.astype(BF16)
            total = summed(refs, right, rows, slice(None))
            for index, row in whole:
                total = total + refs[index][row : row + rows, width:].astype(F32)
            out_ref[at, width:] = total.astype(BF16)


def join(plan, rows, width, channels):
    arrays, numbered = tidy(plan)
    return pl.pallas_call(
        functools.partial(join_kernel, numbered, rows, width),
        out_shape=[jax.ShapeDtypeStruct((rows * len(out), width + channels), BF16) for out in plan],
        compiler_params=pltpu.CompilerParams(vmem_limit_bytes=VMEM_LIMIT),
        cost_estimate=pl.CostEstimate(flops=0, bytes_accessed=1 << 20, transcendentals=0),
        name="join",
    )(*arrays)


def collect(left, right, rows, width, channels):
    count = lax.axis_size("expert")
    half = count // 2
    ahead, back = [], []
    for step in range(count // 4, 1, -1):
        pairs = ((step, half + step - 1), (count - step, half - step + 1))
        plan = [
            [(left[k], right[k], [(v, i * rows) for v in got]) for i, k in enumerate(pair)]
            for pair, got in zip(pairs, (ahead, back))
        ]
        forward, backward = join(plan, rows, width, channels)
        ahead, back = [shift(forward, 1)], [shift(backward, -1)]
    one = (left[1], right[1], [(v, 0) for v in ahead])
    minus = (left[count - 1], right[count - 1], [(v, 0) for v in back])
    across = (left[half], right[half], [(v, rows) for v in ahead + back])
    one, minus, across = join([[one], [minus], [across]], rows, width, channels)
    return shift(one, 1), shift(minus, -1), shift(across, half)


def after(values, *earlier):
    return lax.optimization_barrier((tuple(values), earlier))[0]


def spot(rows, columns, offset):
    down = lax.broadcasted_iota(jnp.int32, (rows, columns), 0)
    across = lax.broadcasted_iota(jnp.int32, (rows, columns), 1)
    return jnp.where(across == down + offset, 1.0, 0.0).astype(BF16)


def digits(value):
    return [(value % 256).astype(F32).astype(BF16), (value // 256).astype(F32).astype(BF16)]


def pack_kernel(columns, n_wave, _, *refs):
    sources, out_ref, held = refs[:5], refs[5], refs[6:11]
    sems = refs[11]
    copies = [
        pltpu.make_async_copy(source, ref, sems.at[i])
        for i, (source, ref) in enumerate(zip(sources, held))
    ]
    hidden_ref, ids_ref, weights_ref, codes_ref, owner_ref = held
    for copy in copies:
        copy.start()
    for copy in copies:
        copy.wait()
    sessions, steps, width = hidden_ref.shape
    expert_count = columns[0] // 2
    books = codes_ref.shape[2]
    meta_width = out_ref.shape[1] - width
    owner = owner_ref[...]
    slots = (owner // sessions // n_wave) * sessions + owner % sessions
    down = lax.broadcasted_iota(jnp.int32, (sessions, sessions), 0)
    across = lax.broadcasted_iota(jnp.int32, (sessions, sessions), 1)
    slot = jnp.sum(jnp.where(down == across, slots, 0).astype(F32), axis=1, keepdims=True)
    slot = slot.astype(jnp.int32)
    lane = lax.broadcasted_iota(jnp.int32, (sessions, meta_width), 1)
    named = lax.broadcasted_iota(jnp.int32, (expert_count, sessions), 0)
    for t in range(steps):
        at = slice(t * sessions, (t + 1) * sessions)
        out_ref[at, 0:width] = hidden_ref[:, t, :]
        weight = jnp.zeros((expert_count, sessions), F32)
        for k in range(ids_ref.shape[1]):
            weight += jnp.where(named == ids_ref[t, k : k + 1, :], weights_ref[t, k : k + 1, :], 0.0)
        high = weight.astype(BF16)
        low = (weight - high.astype(F32)).astype(BF16)
        meta = jnp.zeros((sessions, meta_width), F32)
        for piece, offset in ((high, 0), (low, expert_count)):
            meta += lax.dot_general(
                piece,
                spot(expert_count, meta_width, offset),
                (((0,), (0,)), ((), ())),
                preferred_element_type=F32,
            )
        for i, piece in enumerate(digits(codes_ref[:, t, :])):
            move = spot(books, meta_width, columns[0] + i * books)
            meta += jnp.dot(piece, move, preferred_element_type=F32)
        for i, piece in enumerate(digits(slot * steps + t)):
            meta += jnp.where(lane == columns[1] + i, piece.astype(F32), 0.0)
        out_ref[at, width:] = meta.astype(BF16)


def pack(place, hidden_rows, expert_ids, route_weights, codes, owner_slot, columns, n_wave):
    sessions, steps, width = hidden_rows.shape
    meta_width = -(-(columns[1] + 2) // 128) * 128
    args = (
        hidden_rows,
        jnp.transpose(expert_ids, (1, 2, 0)),
        jnp.transpose(route_weights, (1, 2, 0)),
        codes,
        owner_slot[None],
    )
    return pl.pallas_call(
        functools.partial(pack_kernel, columns, n_wave),
        out_shape=jax.ShapeDtypeStruct((steps * sessions, width + meta_width), BF16),
        in_specs=[pl.BlockSpec(memory_space=pltpu.SMEM)]
        + [pl.BlockSpec(memory_space=pltpu.HBM)] * len(args),
        out_specs=pl.BlockSpec(memory_space=pltpu.VMEM),
        scratch_shapes=[pltpu.VMEM(arg.shape, arg.dtype) for arg in args]
        + [pltpu.SemaphoreType.DMA((len(args),))],
        compiler_params=pltpu.CompilerParams(vmem_limit_bytes=VMEM_LIMIT),
        name="pack",
    )(place, *[pltpu.with_memory_space_constraint(arg, pltpu.HBM) for arg in args])


def load_kernel(*refs):
    count = len(refs) // 2 - 1
    sources, held, sems = refs[1 : count + 1], refs[count + 1 : -1], refs[-1]
    copies = [
        pltpu.make_async_copy(source, ref, sems.at[i])
        for i, (source, ref) in enumerate(zip(sources, held))
    ]
    for copy in copies:
        copy.start()
    for copy in copies:
        copy.wait()


def load(earlier, *arrays):
    hbm = pl.BlockSpec(memory_space=pltpu.HBM)
    return pl.pallas_call(
        load_kernel,
        out_shape=[pltpu.VMEM(v.shape, v.dtype) for v in arrays],
        in_specs=[pl.BlockSpec(memory_space=pl.ANY)] + [hbm] * len(arrays),
        out_specs=[pl.BlockSpec(memory_space=pltpu.VMEM)] * len(arrays),
        scratch_shapes=[pltpu.SemaphoreType.DMA((len(arrays),))],
        compiler_params=pltpu.CompilerParams(vmem_limit_bytes=VMEM_LIMIT),
        cost_estimate=pl.CostEstimate(
            flops=0, bytes_accessed=sum(2 * v.size for v in arrays), transcendentals=0
        ),
        name="load",
    )(earlier, *[pltpu.with_memory_space_constraint(v, pltpu.HBM) for v in arrays])


def experts_kernel(width, expert_count, block_count, place_ref, *refs):
    blocks = refs[:block_count]
    parts = [refs[i : i + 3] for i in range(block_count, len(refs) - 3, 3)]
    out_ref, rows_ref, act_ref = refs[-3:]
    rows = blocks[0].shape[0]
    for i, block in enumerate(blocks):
        rows_ref[i * rows : (i + 1) * rows, :] = block[:, 0:width]
    meta = jnp.concatenate([block[:, width:].astype(F32) for block in blocks], axis=0)
    lane = lax.broadcasted_iota(jnp.int32, meta.shape, 1)
    total = None
    for gate_ref, up_ref, down_ref in parts:
        local, _, units = gate_ref.shape
        for j in range(local):
            mine = place_ref[0] * local + j
            hit = (lane == mine) | (lane == expert_count + mine)
            weight = jnp.sum(jnp.where(hit, meta, 0.0), axis=1, keepdims=True)
            gate = jnp.dot(rows_ref[...], gate_ref[j], preferred_element_type=F32)
            up = jnp.dot(rows_ref[...], up_ref[j], preferred_element_type=F32)
            value = gate * jax.nn.sigmoid(gate) * up
            act_ref[:, j * units : (j + 1) * units] = (value * weight).astype(BF16)
        result = jnp.dot(act_ref[...], down_ref[...], preferred_element_type=F32)
        total = result if total is None else total + result
    out_ref[...] = total.astype(BF16)


def experts(blocks, place, held):
    local, width, units = held[0][0].shape
    rows = blocks[0].shape[0]
    total = rows * len(blocks)
    vmem = pl.BlockSpec(memory_space=pltpu.VMEM)
    weights = [v for part in held for v in part]
    return pl.pallas_call(
        functools.partial(
            experts_kernel, width, lax.axis_size("expert") * local, len(blocks)
        ),
        out_shape=jax.ShapeDtypeStruct((total, width), BF16),
        in_specs=[pl.BlockSpec(memory_space=pltpu.SMEM)] + [vmem] * (len(blocks) + len(weights)),
        out_specs=vmem,
        scratch_shapes=[
            pltpu.VMEM((total, width), BF16),
            pltpu.VMEM((total, local * units), BF16),
        ],
        compiler_params=pltpu.CompilerParams(vmem_limit_bytes=VMEM_LIMIT),
        cost_estimate=pl.CostEstimate(
            flops=6 * total * width * units * local * len(held),
            bytes_accessed=2 * sum(v.size for v in weights),
            transcendentals=total * units * local * len(held),
        ),
        name="experts",
    )(place, *blocks, *weights)


def frames_kernel(columns, books, shard, sessions, steps, order, place_ref, *refs):
    metas = refs[: len(order)]
    table_ref, out_ref, hot_ref = refs[len(order) :]
    count = len(order)
    code_at, slot_at = columns
    rows = metas[0].shape[0]
    meta = jnp.concatenate([m[...] for m in metas], axis=0)
    total = meta.shape[0]
    slot = meta[:, slot_at : slot_at + 2].astype(F32)
    source = (slot[:, 0:1] + 256.0 * slot[:, 1:2]).astype(jnp.int32)
    lane = lax.broadcasted_iota(jnp.int32, (1, total), 1)
    inside = lane % rows
    target = (inside % sessions) * steps + inside // sessions
    place = place_ref[0]
    turn = jnp.where(place % 2 == 0, place // 2, count - 1 - place // 2)
    for i, k in enumerate(order):
        at = (turn + k) % count
        device = jnp.where(at < count // 2, 2 * at, 2 * (count - 1 - at) + 1)
        target = target + jnp.where(lane // rows == i, device * rows, 0)
    chooser = jnp.where(source == target, 1.0, 0.0).astype(BF16)
    ordered = lax.dot_general(
        chooser, meta, (((0,), (0,)), ((), ())), preferred_element_type=F32
    )
    low = ordered[:, code_at : code_at + books]
    high = ordered[:, code_at + books : code_at + 2 * books]
    codes = (low + 256.0 * high).astype(jnp.int32) - place * shard
    chunk = 128
    lanes = lax.broadcasted_iota(jnp.int32, (total, chunk), 1)
    for start in range(0, books * shard, chunk):
        first, last = start // shard, (start + chunk - 1) // shard
        code = codes[:, first : first + 1] + (first * shard - start)
        for q in range(first + 1, last + 1):
            shifted = codes[:, q : q + 1] + (q * shard - start)
            code = jnp.where(lanes >= q * shard - start, shifted, code)
        hit = lanes == code
        if shard < chunk:
            low_end = lanes // shard * shard
            hit = hit & (code >= low_end) & (code < low_end + shard)
        hot_ref[:, start : start + chunk] = jnp.where(hit, 1.0, 0.0).astype(BF16)
    out_ref[...] = jnp.dot(hot_ref[...], table_ref[...], preferred_element_type=F32).astype(BF16)


def frame_sums(blocks, order, place, code_table, columns, width, sessions, steps):
    books, shard, channels = code_table.shape
    rows = blocks[0].shape[0]
    total = rows * len(order)
    meta_width = blocks[0].shape[1] - width
    vmem = pl.BlockSpec(memory_space=pltpu.VMEM)
    return pl.pallas_call(
        functools.partial(frames_kernel, columns, books, shard, sessions, steps, order),
        grid=(1,),
        out_shape=jax.ShapeDtypeStruct((total, channels), BF16),
        in_specs=[pl.BlockSpec(memory_space=pltpu.SMEM)]
        + [pl.BlockSpec((rows, meta_width), lambda i: (0, width // meta_width))] * len(order)
        + [vmem],
        out_specs=vmem,
        scratch_shapes=[pltpu.VMEM((total, books * shard), BF16)],
        compiler_params=pltpu.CompilerParams(vmem_limit_bytes=VMEM_LIMIT + 12 * total * total),
        cost_estimate=pl.CostEstimate(
            flops=2 * total * books * shard * channels,
            bytes_accessed=2 * books * shard * channels,
            transcendentals=0,
        ),
        name="frame_sums",
    )(place, *[blocks[k] for k in order], code_table.reshape(books * shard, channels))


def finish_kernel(left, right, whole, width, *refs):
    state_ref, taps_ref, bias_ref, up_ref, mixed_ref, wave_ref, new_ref = refs[-7:]
    past, sessions, _ = state_ref.shape
    steps = mixed_ref.shape[1]
    rows = steps * sessions
    taps = taps_ref.shape[0]
    frames = summed(refs, right, rows, slice(None))
    for index, row in whole:
        frames = frames + refs[index][row : row + rows, width:].astype(F32)
    history = [state_ref[i].astype(F32) for i in range(past)]
    history += [frames[t * sessions : (t + 1) * sessions] for t in range(steps)]
    decoded = []
    for t in range(steps):
        filtered = bias_ref[...] + taps_ref[0:1, :] * history[past + t]
        for j in range(1, taps):
            filtered = filtered + taps_ref[j : j + 1, :] * history[past + t - j]
        decoded.append(jax.nn.gelu(filtered).astype(BF16))
    samples = jnp.dot(jnp.concatenate(decoded), up_ref[...], preferred_element_type=F32)
    total = summed(refs, left, rows, slice(None))
    for index, row in whole:
        total = total + refs[index][row : row + rows, 0:width].astype(F32)
    for t in range(steps):
        at = slice(t * sessions, (t + 1) * sessions)
        wave_ref[:, t, :] = samples[at].astype(BF16)
        mixed_ref[:, t, :] = total[at].astype(BF16)
    for i in range(past):
        new_ref[i] = history[i + steps].astype(BF16)


def finish(left, right, arrived, width, conv_state, conv_taps, conv_bias, upsample, steps):
    sessions, past, channels = conv_state.shape
    arrays, numbered = tidy([[(left, right, [(v, 0) for v in arrived])]])
    mixed, wave, state = pl.pallas_call(
        functools.partial(finish_kernel, *numbered[0][0], width),
        out_shape=(
            jax.ShapeDtypeStruct((sessions, steps, width), BF16),
            jax.ShapeDtypeStruct((sessions, steps, upsample.shape[1]), BF16),
            jax.ShapeDtypeStruct((past, sessions, channels), BF16),
        ),
        compiler_params=pltpu.CompilerParams(vmem_limit_bytes=VMEM_LIMIT),
        cost_estimate=pl.CostEstimate(flops=0, bytes_accessed=1 << 21, transcendentals=0),
        name="finish",
    )(
        *arrays,
        jnp.transpose(conv_state, (1, 0, 2)),
        conv_taps,
        conv_bias.reshape(1, channels),
        upsample,
    )
    return mixed, wave, jnp.transpose(state, (1, 0, 2))


def per_device(
    hidden_rows,
    expert_ids,
    route_weights,
    w_gate,
    w_up,
    w_down,
    codes,
    owner_slot,
    code_table,
    conv_state,
    conv_taps,
    conv_bias,
    upsample,
):
    count = lax.axis_size("expert")
    sessions, steps, width = hidden_rows.shape
    rows = sessions * steps
    books = codes.shape[2]
    expert_count = count * w_gate.shape[0]
    place = lax.axis_index("expert").astype(jnp.int32)[None]
    columns = (2 * expert_count, 2 * expert_count + 2 * books)

    own = pack(
        place,
        hidden_rows,
        expert_ids,
        route_weights,
        codes,
        owner_slot,
        columns,
        lax.axis_size("wave"),
    )
    half = count // 2
    weights = (w_gate, w_up, w_down.reshape(-1, width))
    sibling = [swap_wave(v) for v in weights]
    held = [load(own, *weights)]

    blocks = {0: own}
    behind = ahead = own
    for step in range(1, half + 1):
        behind = shift(behind, 1)
        got = {count - step: behind}
        if step < half:
            ahead = shift(ahead, -1)
            got[step] = ahead
        first = held[0] if step == 1 else sibling[step - 2 : step - 1]
        got = dict(zip(got, after(got.values(), first)))
        behind, ahead = got[count - step], got.get(step)
        blocks.update(got)

    held.append(sibling)
    order = list(range(count))
    near = [0, 1, count - 1, half]
    groups = [near]
    for step in range(2, count // 4 + 1):
        groups.append([step, half + step - 1, count - step, half - step + 1])
    left, turn = {}, place
    for group in groups[::-1]:
        if group is near:
            sums = frame_sums(blocks, order, turn, code_table, columns, width, sessions, steps)
            (turn,) = after((place,), sums)
        result = experts([blocks[k] for k in group], turn, held)
        (turn,) = after((place,), result)
        for i, k in enumerate(group):
            left[k] = [(result, i * rows)]
    right = {k: [(sums, k * rows)] for k in order}
    arrived = collect(left, right, rows, width, code_table.shape[2])
    return finish(
        left[0], right[0], arrived, width, conv_state, conv_taps, conv_bias, upsample, steps
    )


def solution(mesh):
    rows = P(("groups", "expert", "wave"), None, None)
    placed = (
        rows,
        rows,
        rows,
        P("expert", None, "wave"),
        P("expert", None, "wave"),
        P("expert", "wave", None),
        rows,
        P(("groups", "expert", "wave")),
        P(None, "expert", None),
        rows,
        P(),
        P(),
        P(),
    )
    return jax.shard_map(
        per_device,
        mesh=mesh,
        in_specs=placed,
        out_specs=(rows, rows, rows),
        check_vma=False,
    )
```

```python
import functools

import jax
import jax.numpy as jnp
from jax import lax
from jax.experimental import pallas as pl
from jax.experimental.pallas import tpu as pltpu
from jax.sharding import PartitionSpec as P

F32 = jnp.float32
BF16 = jnp.bfloat16
VMEM_LIMIT = 8 * 1024 * 1024


def ring_order(count):
    return list(range(0, count, 2)) + list(range(1, count, 2))[::-1]


def shift(value, distance):
    count = lax.axis_size("expert")
    ring = ring_order(count)
    pairs = [(ring[i], ring[(i + distance) % count]) for i in range(count)]
    return lax.ppermute(value, "expert", pairs)


def swap_wave(value):
    return lax.ppermute(value, "wave", [(0, 1), (1, 0)])


def tidy(plan):
    arrays, numbers = [], {}

    def number(source):
        array, row = source
        if id(array) not in numbers:
            numbers[id(array)] = len(arrays)
            arrays.append(array)
        return numbers[id(array)], row

    return arrays, [[[[number(v) for v in part] for part in block] for block in out] for out in plan]


def summed(refs, sources, rows, columns):
    total = None
    for index, row in sources:
        value = refs[index][row : row + rows, columns].astype(F32)
        total = value if total is None else total + value
    return total


def join_kernel(plan, rows, width, *refs):
    for out_ref, ((left, right),) in zip(refs[-len(plan) :], plan):
        out_ref[:, 0:width] = summed(refs, left, rows, slice(None)).astype(BF16)
        out_ref[:, width:] = summed(refs, right, rows, slice(None)).astype(BF16)


def join(plan, rows, width, channels):
    arrays, numbered = tidy([[pair] for pair in plan])
    return pl.pallas_call(
        functools.partial(join_kernel, numbered, rows, width),
        out_shape=[jax.ShapeDtypeStruct((rows, width + channels), BF16)] * len(plan),
        compiler_params=pltpu.CompilerParams(vmem_limit_bytes=VMEM_LIMIT),
        cost_estimate=pl.CostEstimate(flops=0, bytes_accessed=1 << 20, transcendentals=0),
        name="join",
    )(*arrays)


def carry(pairs):
    ahead = back = None
    for forward, backward in pairs[::-1]:
        if ahead is not None:
            forward = (forward.astype(F32) + ahead.astype(F32)).astype(BF16)
            backward = (backward.astype(F32) + back.astype(F32)).astype(BF16)
        ahead, back = shift(forward, 1), shift(backward, -1)
    return ahead, back


def towards(near, arrived, rows):
    ahead, back = arrived
    return (
        [(near, rows), (ahead, 0)],
        [(near, 2 * rows), (back, 0)],
        [(near, 3 * rows), (ahead, rows), (back, rows)],
    )


def after(values, *earlier):
    return lax.optimization_barrier((tuple(values), earlier))[0]


def spot(rows, columns, offset):
    down = lax.broadcasted_iota(jnp.int32, (rows, columns), 0)
    across = lax.broadcasted_iota(jnp.int32, (rows, columns), 1)
    return jnp.where(across == down + offset, 1.0, 0.0).astype(BF16)


def digits(value):
    return [(value % 256).astype(F32).astype(BF16), (value // 256).astype(F32).astype(BF16)]


def pack_kernel(columns, n_wave, _, *refs):
    sources, out_ref, held = refs[:5], refs[5], refs[6:11]
    sems = refs[11]
    copies = [
        pltpu.make_async_copy(source, ref, sems.at[i])
        for i, (source, ref) in enumerate(zip(sources, held))
    ]
    hidden_ref, ids_ref, weights_ref, codes_ref, owner_ref = held
    for copy in copies:
        copy.start()
    for copy in copies:
        copy.wait()
    sessions, steps, width = hidden_ref.shape
    expert_count = columns[0] // 2
    books = codes_ref.shape[2]
    meta_width = out_ref.shape[1] - width
    owner = owner_ref[...]
    slots = (owner // sessions // n_wave) * sessions + owner % sessions
    down = lax.broadcasted_iota(jnp.int32, (sessions, sessions), 0)
    across = lax.broadcasted_iota(jnp.int32, (sessions, sessions), 1)
    slot = jnp.sum(jnp.where(down == across, slots, 0).astype(F32), axis=1, keepdims=True)
    slot = slot.astype(jnp.int32)
    lane = lax.broadcasted_iota(jnp.int32, (sessions, meta_width), 1)
    named = lax.broadcasted_iota(jnp.int32, (expert_count, sessions), 0)
    for t in range(steps):
        at = slice(t * sessions, (t + 1) * sessions)
        out_ref[at, 0:width] = hidden_ref[:, t, :]
        weight = jnp.zeros((expert_count, sessions), F32)
        for k in range(ids_ref.shape[1]):
            weight += jnp.where(named == ids_ref[t, k : k + 1, :], weights_ref[t, k : k + 1, :], 0.0)
        high = weight.astype(BF16)
        low = (weight - high.astype(F32)).astype(BF16)
        meta = jnp.zeros((sessions, meta_width), F32)
        for piece, offset in ((high, 0), (low, expert_count)):
            meta += lax.dot_general(
                piece,
                spot(expert_count, meta_width, offset),
                (((0,), (0,)), ((), ())),
                preferred_element_type=F32,
            )
        for i, piece in enumerate(digits(codes_ref[:, t, :])):
            move = spot(books, meta_width, columns[0] + i * books)
            meta += jnp.dot(piece, move, preferred_element_type=F32)
        for i, piece in enumerate(digits(slot * steps + t)):
            meta += jnp.where(lane == columns[1] + i, piece.astype(F32), 0.0)
        out_ref[at, width:] = meta.astype(BF16)


def pack(place, hidden_rows, expert_ids, route_weights, codes, owner_slot, columns, n_wave):
    sessions, steps, width = hidden_rows.shape
    meta_width = -(-(columns[1] + 2) // 128) * 128
    args = (
        hidden_rows,
        jnp.transpose(expert_ids, (1, 2, 0)),
        jnp.transpose(route_weights, (1, 2, 0)),
        codes,
        owner_slot[None],
    )
    return pl.pallas_call(
        functools.partial(pack_kernel, columns, n_wave),
        out_shape=jax.ShapeDtypeStruct((steps * sessions, width + meta_width), BF16),
        in_specs=[pl.BlockSpec(memory_space=pltpu.SMEM)]
        + [pl.BlockSpec(memory_space=pltpu.HBM)] * len(args),
        out_specs=pl.BlockSpec(memory_space=pltpu.VMEM),
        scratch_shapes=[pltpu.VMEM(arg.shape, arg.dtype) for arg in args]
        + [pltpu.SemaphoreType.DMA((len(args),))],
        compiler_params=pltpu.CompilerParams(vmem_limit_bytes=VMEM_LIMIT),
        name="pack",
    )(place, *[pltpu.with_memory_space_constraint(arg, pltpu.HBM) for arg in args])


def load_kernel(*refs):
    count = len(refs) // 2 - 1
    sources, held, sems = refs[1 : count + 1], refs[count + 1 : -1], refs[-1]
    copies = [
        pltpu.make_async_copy(source, ref, sems.at[i])
        for i, (source, ref) in enumerate(zip(sources, held))
    ]
    for copy in copies:
        copy.start()
    for copy in copies:
        copy.wait()


def load(earlier, *arrays):
    hbm = pl.BlockSpec(memory_space=pltpu.HBM)
    return pl.pallas_call(
        load_kernel,
        out_shape=[pltpu.VMEM(v.shape, v.dtype) for v in arrays],
        in_specs=[pl.BlockSpec(memory_space=pl.ANY)] + [hbm] * len(arrays),
        out_specs=[pl.BlockSpec(memory_space=pltpu.VMEM)] * len(arrays),
        scratch_shapes=[pltpu.SemaphoreType.DMA((len(arrays),))],
        compiler_params=pltpu.CompilerParams(vmem_limit_bytes=VMEM_LIMIT),
        cost_estimate=pl.CostEstimate(
            flops=0, bytes_accessed=sum(2 * v.size for v in arrays), transcendentals=0
        ),
        name="load",
    )(earlier, *[pltpu.with_memory_space_constraint(v, pltpu.HBM) for v in arrays])


def experts_kernel(width, expert_count, block_count, out_count, place_ref, *refs):
    blocks = refs[:block_count]
    parts = [refs[i : i + 3] for i in range(block_count, len(refs) - 2 - out_count, 3)]
    outs, (rows_ref, act_ref) = refs[-2 - out_count : -2], refs[-2:]
    rows = blocks[0].shape[0]
    for i, block in enumerate(blocks):
        rows_ref[i * rows : (i + 1) * rows, :] = block[:, 0:width]
    meta = jnp.concatenate([block[:, width:].astype(F32) for block in blocks], axis=0)
    lane = lax.broadcasted_iota(jnp.int32, meta.shape, 1)
    total = None
    for gate_ref, up_ref, down_ref in parts:
        local, _, units = gate_ref.shape
        for j in range(local):
            mine = place_ref[0] * local + j
            hit = (lane == mine) | (lane == expert_count + mine)
            weight = jnp.sum(jnp.where(hit, meta, 0.0), axis=1, keepdims=True)
            gate = jnp.dot(rows_ref[...], gate_ref[j], preferred_element_type=F32)
            up = jnp.dot(rows_ref[...], up_ref[j], preferred_element_type=F32)
            value = gate * jax.nn.sigmoid(gate) * up
            act_ref[:, j * units : (j + 1) * units] = (value * weight).astype(BF16)
        result = jnp.dot(act_ref[...], down_ref[...], preferred_element_type=F32)
        total = result if total is None else total + result
    start = 0
    for out_ref in outs:
        size = out_ref.shape[0]
        out_ref[...] = total[start : start + size].astype(BF16)
        start += size


def experts(blocks, split, place, held):
    local, width, units = held[0][0].shape
    rows = blocks[0].shape[0]
    total = rows * len(blocks)
    vmem = pl.BlockSpec(memory_space=pltpu.VMEM)
    weights = [v for part in held for v in part]
    return pl.pallas_call(
        functools.partial(
            experts_kernel, width, lax.axis_size("expert") * local, len(blocks), split
        ),
        out_shape=[jax.ShapeDtypeStruct((total // split, width), BF16)] * split,
        in_specs=[pl.BlockSpec(memory_space=pltpu.SMEM)] + [vmem] * (len(blocks) + len(weights)),
        out_specs=[vmem] * split,
        scratch_shapes=[
            pltpu.VMEM((total, width), BF16),
            pltpu.VMEM((total, local * units), BF16),
        ],
        compiler_params=pltpu.CompilerParams(vmem_limit_bytes=VMEM_LIMIT),
        cost_estimate=pl.CostEstimate(
            flops=6 * total * width * units * local * len(held),
            bytes_accessed=2 * sum(v.size for v in weights),
            transcendentals=total * units * local * len(held),
        ),
        name="experts",
    )(place, *blocks, *weights)


def frames_kernel(columns, books, shard, sessions, steps, order, place_ref, *refs):
    metas = refs[: len(order)]
    table_ref, *outs, hot_ref = refs[len(order) :]
    count = len(order)
    code_at, slot_at = columns
    rows = metas[0].shape[0]
    meta = jnp.concatenate([m[...] for m in metas], axis=0)
    total = meta.shape[0]
    slot = meta[:, slot_at : slot_at + 2].astype(F32)
    source = (slot[:, 0:1] + 256.0 * slot[:, 1:2]).astype(jnp.int32)
    lane = lax.broadcasted_iota(jnp.int32, (1, total), 1)
    inside = lane % rows
    target = (inside % sessions) * steps + inside // sessions
    place = place_ref[0]
    turn = jnp.where(place % 2 == 0, place // 2, count - 1 - place // 2)
    for i, k in enumerate(order):
        at = (turn + k) % count
        device = jnp.where(at < count // 2, 2 * at, 2 * (count - 1 - at) + 1)
        target = target + jnp.where(lane // rows == i, device * rows, 0)
    chooser = jnp.where(source == target, 1.0, 0.0).astype(BF16)
    ordered = lax.dot_general(
        chooser, meta, (((0,), (0,)), ((), ())), preferred_element_type=F32
    )
    low = ordered[:, code_at : code_at + books]
    high = ordered[:, code_at + books : code_at + 2 * books]
    codes = (low + 256.0 * high).astype(jnp.int32) - place * shard
    chunk = 128
    lanes = lax.broadcasted_iota(jnp.int32, (total, chunk), 1)
    for start in range(0, books * shard, chunk):
        first, last = start // shard, (start + chunk - 1) // shard
        code = codes[:, first : first + 1] + (first * shard - start)
        for q in range(first + 1, last + 1):
            shifted = codes[:, q : q + 1] + (q * shard - start)
            code = jnp.where(lanes >= q * shard - start, shifted, code)
        hit = lanes == code
        if shard < chunk:
            low_end = lanes // shard * shard
            hit = hit & (code >= low_end) & (code < low_end + shard)
        hot_ref[:, start : start + chunk] = jnp.where(hit, 1.0, 0.0).astype(BF16)
    result = jnp.dot(hot_ref[...], table_ref[...], preferred_element_type=F32)
    start = 0
    for out_ref in outs:
        size = out_ref.shape[0]
        out_ref[...] = result[start : start + size].astype(BF16)
        start += size


def frame_sums(blocks, order, sizes, place, code_table, columns, width, sessions, steps):
    books, shard, channels = code_table.shape
    rows = blocks[0].shape[0]
    total = rows * len(order)
    meta_width = blocks[0].shape[1] - width
    vmem = pl.BlockSpec(memory_space=pltpu.VMEM)
    return pl.pallas_call(
        functools.partial(frames_kernel, columns, books, shard, sessions, steps, order),
        grid=(1,),
        out_shape=[jax.ShapeDtypeStruct((rows * size, channels), BF16) for size in sizes],
        in_specs=[pl.BlockSpec(memory_space=pltpu.SMEM)]
        + [pl.BlockSpec((rows, meta_width), lambda i: (0, width // meta_width))] * len(order)
        + [vmem],
        out_specs=[vmem] * len(sizes),
        scratch_shapes=[pltpu.VMEM((total, books * shard), BF16)],
        compiler_params=pltpu.CompilerParams(vmem_limit_bytes=VMEM_LIMIT + 12 * total * total),
        cost_estimate=pl.CostEstimate(
            flops=2 * total * books * shard * channels,
            bytes_accessed=2 * books * shard * channels,
            transcendentals=0,
        ),
        name="frame_sums",
    )(place, *[blocks[k] for k in order], code_table.reshape(books * shard, channels))


def finish_kernel(left, right, whole, width, *refs):
    state_ref, taps_ref, bias_ref, up_ref, mixed_ref, wave_ref, new_ref = refs[-7:]
    past, sessions, _ = state_ref.shape
    steps = mixed_ref.shape[1]
    rows = steps * sessions
    taps = taps_ref.shape[0]
    frames = summed(refs, right, rows, slice(None))
    for index, row in whole:
        frames = frames + refs[index][row : row + rows, width:].astype(F32)
    history = [state_ref[i].astype(F32) for i in range(past)]
    history += [frames[t * sessions : (t + 1) * sessions] for t in range(steps)]
    decoded = []
    for t in range(steps):
        filtered = bias_ref[...] + taps_ref[0:1, :] * history[past + t]
        for j in range(1, taps):
            filtered = filtered + taps_ref[j : j + 1, :] * history[past + t - j]
        decoded.append(jax.nn.gelu(filtered).astype(BF16))
    samples = jnp.dot(jnp.concatenate(decoded), up_ref[...], preferred_element_type=F32)
    total = summed(refs, left, rows, slice(None))
    for index, row in whole:
        total = total + refs[index][row : row + rows, 0:width].astype(F32)
    for t in range(steps):
        at = slice(t * sessions, (t + 1) * sessions)
        wave_ref[:, t, :] = samples[at].astype(BF16)
        mixed_ref[:, t, :] = total[at].astype(BF16)
    for i in range(past):
        new_ref[i] = history[i + steps].astype(BF16)


def finish(left, right, arrived, width, conv_state, conv_taps, conv_bias, upsample, steps):
    sessions, past, channels = conv_state.shape
    arrays, numbered = tidy([[(left, right, [(v, 0) for v in arrived])]])
    mixed, wave, state = pl.pallas_call(
        functools.partial(finish_kernel, *numbered[0][0], width),
        out_shape=(
            jax.ShapeDtypeStruct((sessions, steps, width), BF16),
            jax.ShapeDtypeStruct((sessions, steps, upsample.shape[1]), BF16),
            jax.ShapeDtypeStruct((past, sessions, channels), BF16),
        ),
        compiler_params=pltpu.CompilerParams(vmem_limit_bytes=VMEM_LIMIT),
        cost_estimate=pl.CostEstimate(flops=0, bytes_accessed=1 << 21, transcendentals=0),
        name="finish",
    )(
        *arrays,
        jnp.transpose(conv_state, (1, 0, 2)),
        conv_taps,
        conv_bias.reshape(1, channels),
        upsample,
    )
    return mixed, wave, jnp.transpose(state, (1, 0, 2))


def per_device(
    hidden_rows,
    expert_ids,
    route_weights,
    w_gate,
    w_up,
    w_down,
    codes,
    owner_slot,
    code_table,
    conv_state,
    conv_taps,
    conv_bias,
    upsample,
):
    count = lax.axis_size("expert")
    sessions, steps, width = hidden_rows.shape
    rows = sessions * steps
    books = codes.shape[2]
    expert_count = count * w_gate.shape[0]
    place = lax.axis_index("expert").astype(jnp.int32)[None]
    columns = (2 * expert_count, 2 * expert_count + 2 * books)

    own = pack(
        place,
        hidden_rows,
        expert_ids,
        route_weights,
        codes,
        owner_slot,
        columns,
        lax.axis_size("wave"),
    )
    half = count // 2
    weights = (w_gate, w_up, w_down.reshape(-1, width))
    sibling = [swap_wave(v) for v in after(weights, own)]
    held = [load(own, *weights)]

    blocks = {0: own}
    behind = ahead = own
    for step in range(1, half + 1):
        behind = shift(behind, 1)
        got = {count - step: behind}
        if step < half:
            ahead = shift(ahead, -1)
            got[step] = ahead
        first = held[0] if step == 1 else sibling[step - 2 : step - 1]
        got = dict(zip(got, after(got.values(), first)))
        behind, ahead = got[count - step], got.get(step)
        blocks.update(got)

    held.append(sibling)
    near = [0, 1, count - 1, half]
    far = [
        [step, half + step - 1, count - step, half - step + 1] for step in range(2, count // 4 + 1)
    ]
    pairs, turn = [], place
    for group in far[::-1]:
        pairs.insert(0, experts([blocks[k] for k in group], 2, turn, held))
        (turn,) = after((place,), pairs[0])
    arrived = carry(pairs)
    order = near + [k for group in far for k in group]
    sizes = [4] + [2] * (2 * len(far))
    near_frames, *rest = frame_sums(
        blocks, order, sizes, turn, code_table, columns, width, sessions, steps
    )
    frames_arrived = carry(list(zip(rest[::2], rest[1::2])))
    (turn,) = after((place,), near_frames)
    (near_rows,) = experts([blocks[k] for k in near], 1, turn, held)
    left = towards(near_rows, arrived, rows)
    right = towards(near_frames, frames_arrived, rows)
    one, minus, across = join(list(zip(left, right)), rows, width, code_table.shape[2])
    last = [shift(one, 1), shift(minus, -1), shift(across, half)]
    return finish(
        [(near_rows, 0)],
        [(near_frames, 0)],
        last,
        width,
        conv_state,
        conv_taps,
        conv_bias,
        upsample,
        steps,
    )


def solution(mesh):
    rows = P(("groups", "expert", "wave"), None, None)
    placed = (
        rows,
        rows,
        rows,
        P("expert", None, "wave"),
        P("expert", None, "wave"),
        P("expert", "wave", None),
        rows,
        P(("groups", "expert", "wave")),
        P(None, "expert", None),
        rows,
        P(),
        P(),
        P(),
    )
    return jax.shard_map(
        per_device,
        mesh=mesh,
        in_specs=placed,
        out_specs=(rows, rows, rows),
        check_vma=False,
    )
```

```python
import functools

import jax
import jax.numpy as jnp
from jax import lax
from jax.experimental import pallas as pl
from jax.experimental.pallas import tpu as pltpu
from jax.sharding import PartitionSpec as P

F32 = jnp.float32
BF16 = jnp.bfloat16
VMEM_LIMIT = 8 * 1024 * 1024


def ring_order(count):
    return list(range(0, count, 2)) + list(range(1, count, 2))[::-1]


def shift(value, distance):
    count = lax.axis_size("expert")
    ring = ring_order(count)
    pairs = [(ring[i], ring[(i + distance) % count]) for i in range(count)]
    return lax.ppermute(value, "expert", pairs)


def swap_wave(value):
    return lax.ppermute(value, "wave", [(0, 1), (1, 0)])


def tidy(plan):
    arrays, numbers = [], {}

    def number(source):
        array, row = source
        if id(array) not in numbers:
            numbers[id(array)] = len(arrays)
            arrays.append(array)
        return numbers[id(array)], row

    return arrays, [[[[number(v) for v in part] for part in block] for block in out] for out in plan]


def summed(refs, sources, rows, columns):
    total = None
    for index, row in sources:
        value = refs[index][row : row + rows, columns].astype(F32)
        total = value if total is None else total + value
    return total


def join_kernel(plan, rows, width, *refs):
    for out_ref, ((left, right),) in zip(refs[-len(plan) :], plan):
        out_ref[:, 0:width] = summed(refs, left, rows, slice(None)).astype(BF16)
        out_ref[:, width:] = summed(refs, right, rows, slice(None)).astype(BF16)


def join(plan, rows, width, channels):
    arrays, numbered = tidy([[pair] for pair in plan])
    return pl.pallas_call(
        functools.partial(join_kernel, numbered, rows, width),
        out_shape=[jax.ShapeDtypeStruct((rows, width + channels), BF16)] * len(plan),
        compiler_params=pltpu.CompilerParams(vmem_limit_bytes=VMEM_LIMIT),
        cost_estimate=pl.CostEstimate(flops=0, bytes_accessed=1 << 20, transcendentals=0),
        name="join",
    )(*arrays)


def carry(pairs):
    ahead = back = None
    for forward, backward in pairs[::-1]:
        if ahead is not None:
            forward = (forward.astype(F32) + ahead.astype(F32)).astype(BF16)
            backward = (backward.astype(F32) + back.astype(F32)).astype(BF16)
        ahead, back = shift(forward, 1), shift(backward, -1)
    return ahead, back


def towards(near, arrived, rows):
    ahead, back = arrived
    return (
        [(near, rows), (ahead, 0)],
        [(near, 2 * rows), (back, 0)],
        [(near, 3 * rows), (ahead, rows), (back, rows)],
    )


def after(values, *earlier):
    return lax.optimization_barrier((tuple(values), earlier))[0]


def spot(rows, columns, offset):
    down = lax.broadcasted_iota(jnp.int32, (rows, columns), 0)
    across = lax.broadcasted_iota(jnp.int32, (rows, columns), 1)
    return jnp.where(across == down + offset, 1.0, 0.0).astype(BF16)


def digits(value):
    return [(value % 256).astype(F32).astype(BF16), (value // 256).astype(F32).astype(BF16)]


def pack_kernel(columns, n_wave, _, *refs):
    sources, out_ref, held = refs[:5], refs[5], refs[6:11]
    sems = refs[11]
    copies = [
        pltpu.make_async_copy(source, ref, sems.at[i])
        for i, (source, ref) in enumerate(zip(sources, held))
    ]
    hidden_ref, ids_ref, weights_ref, codes_ref, owner_ref = held
    for copy in copies:
        copy.start()
    for copy in copies:
        copy.wait()
    sessions, steps, width = hidden_ref.shape
    expert_count = columns[0] // 2
    books = codes_ref.shape[2]
    meta_width = out_ref.shape[1] - width
    owner = owner_ref[...]
    slots = (owner // sessions // n_wave) * sessions + owner % sessions
    down = lax.broadcasted_iota(jnp.int32, (sessions, sessions), 0)
    across = lax.broadcasted_iota(jnp.int32, (sessions, sessions), 1)
    slot = jnp.sum(jnp.where(down == across, slots, 0).astype(F32), axis=1, keepdims=True)
    slot = slot.astype(jnp.int32)
    lane = lax.broadcasted_iota(jnp.int32, (sessions, meta_width), 1)
    named = lax.broadcasted_iota(jnp.int32, (expert_count, sessions), 0)
    for t in range(steps):
        at = slice(t * sessions, (t + 1) * sessions)
        out_ref[at, 0:width] = hidden_ref[:, t, :]
        weight = jnp.zeros((expert_count, sessions), F32)
        for k in range(ids_ref.shape[1]):
            weight += jnp.where(named == ids_ref[t, k : k + 1, :], weights_ref[t, k : k + 1, :], 0.0)
        high = weight.astype(BF16)
        low = (weight - high.astype(F32)).astype(BF16)
        meta = jnp.zeros((sessions, meta_width), F32)
        for piece, offset in ((high, 0), (low, expert_count)):
            meta += lax.dot_general(
                piece,
                spot(expert_count, meta_width, offset),
                (((0,), (0,)), ((), ())),
                preferred_element_type=F32,
            )
        for i, piece in enumerate(digits(codes_ref[:, t, :])):
            move = spot(books, meta_width, columns[0] + i * books)
            meta += jnp.dot(piece, move, preferred_element_type=F32)
        for i, piece in enumerate(digits(slot * steps + t)):
            meta += jnp.where(lane == columns[1] + i, piece.astype(F32), 0.0)
        out_ref[at, width:] = meta.astype(BF16)


def pack(place, hidden_rows, expert_ids, route_weights, codes, owner_slot, columns, n_wave):
    sessions, steps, width = hidden_rows.shape
    meta_width = -(-(columns[1] + 2) // 128) * 128
    args = (
        hidden_rows,
        jnp.transpose(expert_ids, (1, 2, 0)),
        jnp.transpose(route_weights, (1, 2, 0)),
        codes,
        owner_slot[None],
    )
    return pl.pallas_call(
        functools.partial(pack_kernel, columns, n_wave),
        out_shape=jax.ShapeDtypeStruct((steps * sessions, width + meta_width), BF16),
        in_specs=[pl.BlockSpec(memory_space=pltpu.SMEM)]
        + [pl.BlockSpec(memory_space=pltpu.HBM)] * len(args),
        out_specs=pl.BlockSpec(memory_space=pltpu.VMEM),
        scratch_shapes=[pltpu.VMEM(arg.shape, arg.dtype) for arg in args]
        + [pltpu.SemaphoreType.DMA((len(args),))],
        compiler_params=pltpu.CompilerParams(vmem_limit_bytes=VMEM_LIMIT),
        name="pack",
    )(place, *[pltpu.with_memory_space_constraint(arg, pltpu.HBM) for arg in args])


def load_kernel(*refs):
    count = len(refs) // 2 - 1
    sources, held, sems = refs[1 : count + 1], refs[count + 1 : -1], refs[-1]
    copies = [
        pltpu.make_async_copy(source, ref, sems.at[i])
        for i, (source, ref) in enumerate(zip(sources, held))
    ]
    for copy in copies:
        copy.start()
    for copy in copies:
        copy.wait()


def load(earlier, *arrays):
    hbm = pl.BlockSpec(memory_space=pltpu.HBM)
    return pl.pallas_call(
        load_kernel,
        out_shape=[pltpu.VMEM(v.shape, v.dtype) for v in arrays],
        in_specs=[pl.BlockSpec(memory_space=pl.ANY)] + [hbm] * len(arrays),
        out_specs=[pl.BlockSpec(memory_space=pltpu.VMEM)] * len(arrays),
        scratch_shapes=[pltpu.SemaphoreType.DMA((len(arrays),))],
        compiler_params=pltpu.CompilerParams(vmem_limit_bytes=VMEM_LIMIT),
        cost_estimate=pl.CostEstimate(
            flops=0, bytes_accessed=sum(2 * v.size for v in arrays), transcendentals=0
        ),
        name="load",
    )(earlier, *[pltpu.with_memory_space_constraint(v, pltpu.HBM) for v in arrays])


def experts_kernel(width, expert_count, block_count, out_count, place_ref, *refs):
    blocks = refs[:block_count]
    parts = [refs[i : i + 3] for i in range(block_count, len(refs) - 2 - out_count, 3)]
    outs, (rows_ref, act_ref) = refs[-2 - out_count : -2], refs[-2:]
    rows = blocks[0].shape[0]
    for i, block in enumerate(blocks):
        rows_ref[i * rows : (i + 1) * rows, :] = block[:, 0:width]
    meta = jnp.concatenate([block[:, width:].astype(F32) for block in blocks], axis=0)
    lane = lax.broadcasted_iota(jnp.int32, meta.shape, 1)
    total = None
    for gate_ref, up_ref, down_ref in parts:
        local, _, units = gate_ref.shape
        for j in range(local):
            mine = place_ref[0] * local + j
            hit = (lane == mine) | (lane == expert_count + mine)
            weight = jnp.sum(jnp.where(hit, meta, 0.0), axis=1, keepdims=True)
            both = jnp.concatenate([gate_ref[j], up_ref[j]], axis=1)
            both = jnp.dot(rows_ref[...], both, preferred_element_type=F32)
            gate, up = both[:, 0:units], both[:, units:]
            value = gate * jax.nn.sigmoid(gate) * up
            act_ref[:, j * units : (j + 1) * units] = (value * weight).astype(BF16)
        result = jnp.dot(act_ref[...], down_ref[...], preferred_element_type=F32)
        total = result if total is None else total + result
    start = 0
    for out_ref in outs:
        size = out_ref.shape[0]
        out_ref[...] = total[start : start + size].astype(BF16)
        start += size


def experts(blocks, split, place, held):
    local, width, units = held[0][0].shape
    rows = blocks[0].shape[0]
    total = rows * len(blocks)
    vmem = pl.BlockSpec(memory_space=pltpu.VMEM)
    weights = [v for part in held for v in part]
    return pl.pallas_call(
        functools.partial(
            experts_kernel, width, lax.axis_size("expert") * local, len(blocks), split
        ),
        out_shape=[jax.ShapeDtypeStruct((total // split, width), BF16)] * split,
        in_specs=[pl.BlockSpec(memory_space=pltpu.SMEM)] + [vmem] * (len(blocks) + len(weights)),
        out_specs=[vmem] * split,
        scratch_shapes=[
            pltpu.VMEM((total, width), BF16),
            pltpu.VMEM((total, local * units), BF16),
        ],
        compiler_params=pltpu.CompilerParams(vmem_limit_bytes=VMEM_LIMIT),
        cost_estimate=pl.CostEstimate(
            flops=6 * total * width * units * local * len(held),
            bytes_accessed=2 * sum(v.size for v in weights),
            transcendentals=total * units * local * len(held),
        ),
        name="experts",
    )(place, *blocks, *weights)


def frames_kernel(columns, books, shard, sessions, steps, order, place_ref, *refs):
    metas = refs[: len(order)]
    table_ref, *outs, hot_ref = refs[len(order) :]
    count = len(order)
    code_at, slot_at = columns
    rows = metas[0].shape[0]
    meta = jnp.concatenate([m[...] for m in metas], axis=0)
    total = meta.shape[0]
    column = lax.broadcasted_iota(jnp.int32, (8, meta.shape[1]), 1)
    digit = lax.broadcasted_iota(jnp.int32, (8, meta.shape[1]), 0)
    picks = jnp.where((column == slot_at + digit) & (digit < 2), 1.0, 0.0).astype(BF16)
    slots = lax.dot_general(picks, meta, (((1,), (1,)), ((), ())), preferred_element_type=F32)
    source = (slots[0:1] + 256.0 * slots[1:2]).astype(jnp.int32)
    row = lax.broadcasted_iota(jnp.int32, (total, 1), 0)
    inside = row % rows
    target = (inside % sessions) * steps + inside // sessions
    place = place_ref[0]
    turn = jnp.where(place % 2 == 0, place // 2, count - 1 - place // 2)
    for i, k in enumerate(order):
        at = (turn + k) % count
        device = jnp.where(at < count // 2, 2 * at, 2 * (count - 1 - at) + 1)
        target = target + jnp.where(row // rows == i, device * rows, 0)
    chooser = jnp.where(target == source, 1.0, 0.0).astype(BF16)
    ordered = jnp.dot(chooser, meta, preferred_element_type=F32).astype(BF16)
    lanes = books * shard
    column = lax.broadcasted_iota(jnp.int32, (meta.shape[1], lanes), 0) - code_at
    book = lax.broadcasted_iota(jnp.int32, (meta.shape[1], lanes), 1) // shard
    spread = jnp.where(column == book, 1.0, jnp.where(column == book + books, 256.0, 0.0))
    codes = jnp.dot(ordered, spread.astype(BF16), preferred_element_type=F32)
    entry = lax.broadcasted_iota(jnp.int32, (1, lanes), 1) % shard + place * shard
    hot_ref[...] = jnp.where(codes == entry.astype(F32), 1.0, 0.0).astype(BF16)
    result = jnp.dot(hot_ref[...], table_ref[...], preferred_element_type=F32)
    start = 0
    for out_ref in outs:
        size = out_ref.shape[0]
        out_ref[...] = result[start : start + size].astype(BF16)
        start += size


def frame_sums(blocks, order, sizes, place, code_table, columns, width, sessions, steps):
    books, shard, channels = code_table.shape
    rows = blocks[0].shape[0]
    total = rows * len(order)
    meta_width = blocks[0].shape[1] - width
    vmem = pl.BlockSpec(memory_space=pltpu.VMEM)
    return pl.pallas_call(
        functools.partial(frames_kernel, columns, books, shard, sessions, steps, order),
        grid=(1,),
        out_shape=[jax.ShapeDtypeStruct((rows * size, channels), BF16) for size in sizes],
        in_specs=[pl.BlockSpec(memory_space=pltpu.SMEM)]
        + [pl.BlockSpec((rows, meta_width), lambda i: (0, width // meta_width))] * len(order)
        + [vmem],
        out_specs=[vmem] * len(sizes),
        scratch_shapes=[pltpu.VMEM((total, books * shard), BF16)],
        compiler_params=pltpu.CompilerParams(vmem_limit_bytes=VMEM_LIMIT + 12 * total * total),
        cost_estimate=pl.CostEstimate(
            flops=2 * total * books * shard * channels,
            bytes_accessed=2 * books * shard * channels,
            transcendentals=0,
        ),
        name="frame_sums",
    )(place, *[blocks[k] for k in order], code_table.reshape(books * shard, channels))


def finish_kernel(left, right, whole, width, *refs):
    state_ref, taps_ref, bias_ref, up_ref, mixed_ref, wave_ref, new_ref = refs[-7:]
    past, sessions, _ = state_ref.shape
    steps = mixed_ref.shape[1]
    rows = steps * sessions
    taps = taps_ref.shape[0]
    frames = summed(refs, right, rows, slice(None))
    for index, row in whole:
        frames = frames + refs[index][row : row + rows, width:].astype(F32)
    history = [state_ref[i].astype(F32) for i in range(past)]
    history += [frames[t * sessions : (t + 1) * sessions] for t in range(steps)]
    decoded = []
    for t in range(steps):
        filtered = bias_ref[...] + taps_ref[0:1, :] * history[past + t]
        for j in range(1, taps):
            filtered = filtered + taps_ref[j : j + 1, :] * history[past + t - j]
        decoded.append(jax.nn.gelu(filtered).astype(BF16))
    samples = jnp.dot(jnp.concatenate(decoded), up_ref[...], preferred_element_type=F32)
    total = summed(refs, left, rows, slice(None))
    for index, row in whole:
        total = total + refs[index][row : row + rows, 0:width].astype(F32)
    for t in range(steps):
        at = slice(t * sessions, (t + 1) * sessions)
        wave_ref[:, t, :] = samples[at].astype(BF16)
        mixed_ref[:, t, :] = total[at].astype(BF16)
    for i in range(past):
        new_ref[i] = history[i + steps].astype(BF16)


def finish(left, right, arrived, width, conv_state, conv_taps, conv_bias, upsample, steps):
    sessions, past, channels = conv_state.shape
    arrays, numbered = tidy([[(left, right, [(v, 0) for v in arrived])]])
    mixed, wave, state = pl.pallas_call(
        functools.partial(finish_kernel, *numbered[0][0], width),
        out_shape=(
            jax.ShapeDtypeStruct((sessions, steps, width), BF16),
            jax.ShapeDtypeStruct((sessions, steps, upsample.shape[1]), BF16),
            jax.ShapeDtypeStruct((past, sessions, channels), BF16),
        ),
        compiler_params=pltpu.CompilerParams(vmem_limit_bytes=VMEM_LIMIT),
        cost_estimate=pl.CostEstimate(flops=0, bytes_accessed=1 << 21, transcendentals=0),
        name="finish",
    )(
        *arrays,
        jnp.transpose(conv_state, (1, 0, 2)),
        conv_taps,
        conv_bias.reshape(1, channels),
        upsample,
    )
    return mixed, wave, jnp.transpose(state, (1, 0, 2))


def per_device(
    hidden_rows,
    expert_ids,
    route_weights,
    w_gate,
    w_up,
    w_down,
    codes,
    owner_slot,
    code_table,
    conv_state,
    conv_taps,
    conv_bias,
    upsample,
):
    count = lax.axis_size("expert")
    sessions, steps, width = hidden_rows.shape
    rows = sessions * steps
    books = codes.shape[2]
    expert_count = count * w_gate.shape[0]
    place = lax.axis_index("expert").astype(jnp.int32)[None]
    columns = (2 * expert_count, 2 * expert_count + 2 * books)

    own = pack(
        place,
        hidden_rows,
        expert_ids,
        route_weights,
        codes,
        owner_slot,
        columns,
        lax.axis_size("wave"),
    )
    half = count // 2
    weights = (w_gate, w_up, w_down.reshape(-1, width))
    sibling = [swap_wave(v) for v in after(weights, own)]
    held = [load(own, *weights)]

    blocks = {0: own}
    behind = ahead = own
    for step in range(1, half + 1):
        behind = shift(behind, 1)
        got = {count - step: behind}
        if step < half:
            ahead = shift(ahead, -1)
            got[step] = ahead
        first = held[0] if step == 1 else sibling[step - 2 : step - 1]
        got = {k: after((v,), first)[0] for k, v in got.items()}
        behind, ahead = got[count - step], got.get(step)
        blocks.update(got)

    held.append(sibling)
    near = [0, 1, count - 1, half]
    far = [
        [step, half + step - 1, count - step, half - step + 1] for step in range(2, count // 4 + 1)
    ]
    pairs, turn = [], place
    for group in far[::-1]:
        pairs.insert(0, experts([blocks[k] for k in group], 2, turn, held))
        (turn,) = after((place,), pairs[0])
    arrived = carry(pairs)
    order = near + [k for group in far for k in group]
    sizes = [4] + [2] * (2 * len(far))
    near_frames, *rest = frame_sums(
        blocks, order, sizes, turn, code_table, columns, width, sessions, steps
    )
    frames_arrived = carry(list(zip(rest[::2], rest[1::2])))
    (turn,) = after((place,), near_frames)
    (near_rows,) = experts([blocks[k] for k in near], 1, turn, held)
    left = towards(near_rows, arrived, rows)
    right = towards(near_frames, frames_arrived, rows)
    one, minus, across = join(list(zip(left, right)), rows, width, code_table.shape[2])
    last = [shift(one, 1), shift(minus, -1), shift(across, half)]
    return finish(
        [(near_rows, 0)],
        [(near_frames, 0)],
        last,
        width,
        conv_state,
        conv_taps,
        conv_bias,
        upsample,
        steps,
    )


def solution(mesh):
    rows = P(("groups", "expert", "wave"), None, None)
    placed = (
        rows,
        rows,
        rows,
        P("expert", None, "wave"),
        P("expert", None, "wave"),
        P("expert", "wave", None),
        rows,
        P(("groups", "expert", "wave")),
        P(None, "expert", None),
        rows,
        P(),
        P(),
        P(),
    )
    return jax.shard_map(
        per_device,
        mesh=mesh,
        in_specs=placed,
        out_specs=(rows, rows, rows),
        check_vma=False,
    )
```

```python
import functools

import jax
import jax.numpy as jnp
from jax import lax
from jax.experimental import pallas as pl
from jax.experimental.pallas import tpu as pltpu
from jax.sharding import PartitionSpec as P

F32 = jnp.float32
BF16 = jnp.bfloat16
VMEM_LIMIT = 8 * 1024 * 1024


def ring_order(count):
    return list(range(0, count, 2)) + list(range(1, count, 2))[::-1]


def shift(value, distance):
    count = lax.axis_size("expert")
    ring = ring_order(count)
    pairs = [(ring[i], ring[(i + distance) % count]) for i in range(count)]
    return lax.ppermute(value, "expert", pairs)


def swap_wave(value):
    return lax.ppermute(value, "wave", [(0, 1), (1, 0)])


def tidy(plan):
    arrays, numbers = [], {}

    def number(source):
        array, row = source
        if id(array) not in numbers:
            numbers[id(array)] = len(arrays)
            arrays.append(array)
        return numbers[id(array)], row

    return arrays, [[[[number(v) for v in part] for part in block] for block in out] for out in plan]


def summed(refs, sources, rows, columns):
    total = None
    for index, row in sources:
        value = refs[index][row : row + rows, columns].astype(F32)
        total = value if total is None else total + value
    return total


def join_kernel(plan, rows, width, *refs):
    for out_ref, ((left, right),) in zip(refs[-len(plan) :], plan):
        out_ref[:, 0:width] = summed(refs, left, rows, slice(None)).astype(BF16)
        out_ref[:, width:] = summed(refs, right, rows, slice(None)).astype(BF16)


def join(plan, rows, width, channels):
    arrays, numbered = tidy([[pair] for pair in plan])
    return pl.pallas_call(
        functools.partial(join_kernel, numbered, rows, width),
        out_shape=[jax.ShapeDtypeStruct((rows, width + channels), BF16)] * len(plan),
        compiler_params=pltpu.CompilerParams(vmem_limit_bytes=VMEM_LIMIT),
        cost_estimate=pl.CostEstimate(flops=0, bytes_accessed=1 << 20, transcendentals=0),
        name="join",
    )(*arrays)


def carry(pairs):
    ahead = back = None
    for forward, backward in pairs[::-1]:
        if ahead is not None:
            forward = (forward.astype(F32) + ahead.astype(F32)).astype(BF16)
            backward = (backward.astype(F32) + back.astype(F32)).astype(BF16)
        ahead, back = shift(forward, 1), shift(backward, -1)
    return ahead, back


def towards(near, arrived, rows):
    ahead, back = arrived
    return (
        [(near, rows), (ahead, 0)],
        [(near, 2 * rows), (back, 0)],
        [(near, 3 * rows), (ahead, rows), (back, rows)],
    )


def after(values, *earlier):
    return lax.optimization_barrier((tuple(values), earlier))[0]


def spot(rows, columns, offset):
    down = lax.broadcasted_iota(jnp.int32, (rows, columns), 0)
    across = lax.broadcasted_iota(jnp.int32, (rows, columns), 1)
    return jnp.where(across == down + offset, 1.0, 0.0).astype(BF16)


def digits(value):
    return [(value % 256).astype(F32).astype(BF16), (value // 256).astype(F32).astype(BF16)]


def pack_kernel(columns, n_wave, _, *refs):
    sources, out_ref, held = refs[:5], refs[5], refs[6:11]
    sems = refs[11]
    copies = [
        pltpu.make_async_copy(source, ref, sems.at[i])
        for i, (source, ref) in enumerate(zip(sources, held))
    ]
    hidden_ref, ids_ref, weights_ref, codes_ref, owner_ref = held
    for copy in copies:
        copy.start()
    for copy in copies:
        copy.wait()
    sessions, steps, width = hidden_ref.shape
    expert_count = columns[0] // 2
    books = codes_ref.shape[2]
    meta_width = out_ref.shape[1] - width
    owner = owner_ref[...]
    slots = (owner // sessions // n_wave) * sessions + owner % sessions
    down = lax.broadcasted_iota(jnp.int32, (sessions, sessions), 0)
    across = lax.broadcasted_iota(jnp.int32, (sessions, sessions), 1)
    slot = jnp.sum(jnp.where(down == across, slots, 0).astype(F32), axis=1, keepdims=True)
    slot = slot.astype(jnp.int32)
    lane = lax.broadcasted_iota(jnp.int32, (sessions, meta_width), 1)
    named = lax.broadcasted_iota(jnp.int32, (expert_count, sessions), 0)
    for t in range(steps):
        at = slice(t * sessions, (t + 1) * sessions)
        out_ref[at, 0:width] = hidden_ref[:, t, :]
        weight = jnp.zeros((expert_count, sessions), F32)
        for k in range(ids_ref.shape[1]):
            weight += jnp.where(named == ids_ref[t, k : k + 1, :], weights_ref[t, k : k + 1, :], 0.0)
        high = weight.astype(BF16)
        low = (weight - high.astype(F32)).astype(BF16)
        meta = jnp.zeros((sessions, meta_width), F32)
        for piece, offset in ((high, 0), (low, expert_count)):
            meta += lax.dot_general(
                piece,
                spot(expert_count, meta_width, offset),
                (((0,), (0,)), ((), ())),
                preferred_element_type=F32,
            )
        for i, piece in enumerate(digits(codes_ref[:, t, :])):
            move = spot(books, meta_width, columns[0] + i * books)
            meta += jnp.dot(piece, move, preferred_element_type=F32)
        for i, piece in enumerate(digits(slot * steps + t)):
            meta += jnp.where(lane == columns[1] + i, piece.astype(F32), 0.0)
        out_ref[at, width:] = meta.astype(BF16)


def pack(place, hidden_rows, expert_ids, route_weights, codes, owner_slot, columns, n_wave):
    sessions, steps, width = hidden_rows.shape
    meta_width = -(-(columns[1] + 2) // 128) * 128
    args = (
        hidden_rows,
        jnp.transpose(expert_ids, (1, 2, 0)),
        jnp.transpose(route_weights, (1, 2, 0)),
        codes,
        owner_slot[None],
    )
    return pl.pallas_call(
        functools.partial(pack_kernel, columns, n_wave),
        out_shape=jax.ShapeDtypeStruct((steps * sessions, width + meta_width), BF16),
        in_specs=[pl.BlockSpec(memory_space=pltpu.SMEM)]
        + [pl.BlockSpec(memory_space=pltpu.HBM)] * len(args),
        out_specs=pl.BlockSpec(memory_space=pltpu.VMEM),
        scratch_shapes=[pltpu.VMEM(arg.shape, arg.dtype) for arg in args]
        + [pltpu.SemaphoreType.DMA((len(args),))],
        compiler_params=pltpu.CompilerParams(vmem_limit_bytes=VMEM_LIMIT),
        name="pack",
    )(place, *[pltpu.with_memory_space_constraint(arg, pltpu.HBM) for arg in args])


def load_kernel(*refs):
    count = len(refs) // 2 - 1
    sources, held, sems = refs[1 : count + 1], refs[count + 1 : -1], refs[-1]
    copies = [
        pltpu.make_async_copy(source, ref, sems.at[i])
        for i, (source, ref) in enumerate(zip(sources, held))
    ]
    for copy in copies:
        copy.start()
    for copy in copies:
        copy.wait()


def load(earlier, *arrays):
    hbm = pl.BlockSpec(memory_space=pltpu.HBM)
    return pl.pallas_call(
        load_kernel,
        out_shape=[pltpu.VMEM(v.shape, v.dtype) for v in arrays],
        in_specs=[pl.BlockSpec(memory_space=pl.ANY)] + [hbm] * len(arrays),
        out_specs=[pl.BlockSpec(memory_space=pltpu.VMEM)] * len(arrays),
        scratch_shapes=[pltpu.SemaphoreType.DMA((len(arrays),))],
        compiler_params=pltpu.CompilerParams(vmem_limit_bytes=VMEM_LIMIT),
        cost_estimate=pl.CostEstimate(
            flops=0, bytes_accessed=sum(2 * v.size for v in arrays), transcendentals=0
        ),
        name="load",
    )(earlier, *[pltpu.with_memory_space_constraint(v, pltpu.HBM) for v in arrays])


def experts_kernel(width, expert_count, block_count, out_count, place_ref, *refs):
    blocks = refs[:block_count]
    parts = [refs[i : i + 3] for i in range(block_count, len(refs) - 2 - out_count, 3)]
    outs, (rows_ref, act_ref) = refs[-2 - out_count : -2], refs[-2:]
    rows = blocks[0].shape[0]
    for i, block in enumerate(blocks):
        rows_ref[i * rows : (i + 1) * rows, :] = block[:, 0:width]
    meta = jnp.concatenate([block[:, width:].astype(F32) for block in blocks], axis=0)
    lane = lax.broadcasted_iota(jnp.int32, meta.shape, 1)
    total = None
    for gate_ref, up_ref, down_ref in parts:
        local, _, units = gate_ref.shape
        for j in range(local):
            mine = place_ref[0] * local + j
            hit = (lane == mine) | (lane == expert_count + mine)
            weight = jnp.sum(jnp.where(hit, meta, 0.0), axis=1, keepdims=True)
            both = jnp.concatenate([gate_ref[j], up_ref[j]], axis=1)
            both = jnp.dot(rows_ref[...], both, preferred_element_type=F32)
            gate, up = both[:, 0:units], both[:, units:]
            value = gate * jax.nn.sigmoid(gate) * up
            act_ref[:, j * units : (j + 1) * units] = (value * weight).astype(BF16)
        result = jnp.dot(act_ref[...], down_ref[...], preferred_element_type=F32)
        total = result if total is None else total + result
    start = 0
    for out_ref in outs:
        size = out_ref.shape[0]
        out_ref[...] = total[start : start + size].astype(BF16)
        start += size


def experts(blocks, split, place, held):
    local, width, units = held[0][0].shape
    rows = blocks[0].shape[0]
    total = rows * len(blocks)
    vmem = pl.BlockSpec(memory_space=pltpu.VMEM)
    weights = [v for part in held for v in part]
    return pl.pallas_call(
        functools.partial(
            experts_kernel, width, lax.axis_size("expert") * local, len(blocks), split
        ),
        out_shape=[jax.ShapeDtypeStruct((total // split, width), BF16)] * split,
        in_specs=[pl.BlockSpec(memory_space=pltpu.SMEM)] + [vmem] * (len(blocks) + len(weights)),
        out_specs=[vmem] * split,
        scratch_shapes=[
            pltpu.VMEM((total, width), BF16),
            pltpu.VMEM((total, local * units), BF16),
        ],
        compiler_params=pltpu.CompilerParams(vmem_limit_bytes=VMEM_LIMIT),
        cost_estimate=pl.CostEstimate(
            flops=6 * total * width * units * local * len(held),
            bytes_accessed=2 * sum(v.size for v in weights),
            transcendentals=total * units * local * len(held),
        ),
        name="experts",
    )(place, *blocks, *weights)


def frames_kernel(columns, books, shard, sessions, steps, order, place_ref, *refs):
    metas = refs[: len(order)]
    table_ref, *outs, hot_ref = refs[len(order) :]
    count = len(order)
    code_at, slot_at = columns
    rows = metas[0].shape[0]
    meta = jnp.concatenate([m[...] for m in metas], axis=0)
    total = meta.shape[0]
    column = lax.broadcasted_iota(jnp.int32, (8, meta.shape[1]), 1)
    digit = lax.broadcasted_iota(jnp.int32, (8, meta.shape[1]), 0)
    picks = jnp.where((column == slot_at + digit) & (digit < 2), 1.0, 0.0).astype(BF16)
    slots = lax.dot_general(picks, meta, (((1,), (1,)), ((), ())), preferred_element_type=F32)
    source = (slots[0:1] + 256.0 * slots[1:2]).astype(jnp.int32)
    row = lax.broadcasted_iota(jnp.int32, (total, 1), 0)
    inside = row % rows
    target = (inside % sessions) * steps + inside // sessions
    place = place_ref[0]
    turn = jnp.where(place % 2 == 0, place // 2, count - 1 - place // 2)
    for i, k in enumerate(order):
        at = (turn + k) % count
        device = jnp.where(at < count // 2, 2 * at, 2 * (count - 1 - at) + 1)
        target = target + jnp.where(row // rows == i, device * rows, 0)
    chooser = jnp.where(target == source, 1.0, 0.0).astype(BF16)
    ordered = jnp.dot(chooser, meta, preferred_element_type=F32).astype(BF16)
    lanes = books * shard
    column = lax.broadcasted_iota(jnp.int32, (meta.shape[1], lanes), 0) - code_at
    book = lax.broadcasted_iota(jnp.int32, (meta.shape[1], lanes), 1) // shard
    spread = jnp.where(column == book, 1.0, jnp.where(column == book + books, 256.0, 0.0))
    codes = jnp.dot(ordered, spread.astype(BF16), preferred_element_type=F32)
    entry = lax.broadcasted_iota(jnp.int32, (1, lanes), 1) % shard + place * shard
    hot_ref[...] = jnp.where(codes == entry.astype(F32), 1.0, 0.0).astype(BF16)
    result = jnp.dot(hot_ref[...], table_ref[...], preferred_element_type=F32)
    start = 0
    for out_ref in outs:
        size = out_ref.shape[0]
        out_ref[...] = result[start : start + size].astype(BF16)
        start += size


def frame_sums(blocks, order, sizes, place, code_table, columns, width, sessions, steps):
    books, shard, channels = code_table.shape
    rows = blocks[0].shape[0]
    total = rows * len(order)
    meta_width = blocks[0].shape[1] - width
    vmem = pl.BlockSpec(memory_space=pltpu.VMEM)
    return pl.pallas_call(
        functools.partial(frames_kernel, columns, books, shard, sessions, steps, order),
        grid=(1,),
        out_shape=[jax.ShapeDtypeStruct((rows * size, channels), BF16) for size in sizes],
        in_specs=[pl.BlockSpec(memory_space=pltpu.SMEM)]
        + [pl.BlockSpec((rows, meta_width), lambda i: (0, width // meta_width))] * len(order)
        + [vmem],
        out_specs=[vmem] * len(sizes),
        scratch_shapes=[pltpu.VMEM((total, books * shard), BF16)],
        compiler_params=pltpu.CompilerParams(vmem_limit_bytes=VMEM_LIMIT + 12 * total * total),
        cost_estimate=pl.CostEstimate(
            flops=2 * total * books * shard * channels,
            bytes_accessed=2 * books * shard * channels,
            transcendentals=0,
        ),
        name="frame_sums",
    )(place, *[blocks[k] for k in order], code_table.reshape(books * shard, channels))


def finish_kernel(left, right, whole, width, *refs):
    state_ref, taps_ref, bias_ref, up_ref, mixed_ref, wave_ref, new_ref = refs[-7:]
    past, sessions, _ = state_ref.shape
    steps = mixed_ref.shape[1]
    rows = steps * sessions
    taps = taps_ref.shape[0]
    frames = summed(refs, right, rows, slice(None))
    for index, row in whole:
        frames = frames + refs[index][row : row + rows, width:].astype(F32)
    history = [state_ref[i].astype(F32) for i in range(past)]
    history += [frames[t * sessions : (t + 1) * sessions] for t in range(steps)]
    decoded = []
    for t in range(steps):
        filtered = bias_ref[...] + taps_ref[0:1, :] * history[past + t]
        for j in range(1, taps):
            filtered = filtered + taps_ref[j : j + 1, :] * history[past + t - j]
        decoded.append(jax.nn.gelu(filtered).astype(BF16))
    samples = jnp.dot(jnp.concatenate(decoded), up_ref[...], preferred_element_type=F32)
    total = summed(refs, left, rows, slice(None))
    for index, row in whole:
        total = total + refs[index][row : row + rows, 0:width].astype(F32)
    for t in range(steps):
        at = slice(t * sessions, (t + 1) * sessions)
        wave_ref[:, t, :] = samples[at].astype(BF16)
        mixed_ref[:, t, :] = total[at].astype(BF16)
    for i in range(past):
        new_ref[i] = history[i + steps].astype(BF16)


def finish(left, right, arrived, width, conv_state, conv_taps, conv_bias, upsample, steps):
    sessions, past, channels = conv_state.shape
    arrays, numbered = tidy([[(left, right, [(v, 0) for v in arrived])]])
    mixed, wave, state = pl.pallas_call(
        functools.partial(finish_kernel, *numbered[0][0], width),
        out_shape=(
            jax.ShapeDtypeStruct((sessions, steps, width), BF16),
            jax.ShapeDtypeStruct((sessions, steps, upsample.shape[1]), BF16),
            jax.ShapeDtypeStruct((past, sessions, channels), BF16),
        ),
        compiler_params=pltpu.CompilerParams(vmem_limit_bytes=VMEM_LIMIT),
        cost_estimate=pl.CostEstimate(flops=0, bytes_accessed=1 << 21, transcendentals=0),
        name="finish",
    )(
        *arrays,
        jnp.transpose(conv_state, (1, 0, 2)),
        conv_taps,
        conv_bias.reshape(1, channels),
        upsample,
    )
    return mixed, wave, jnp.transpose(state, (1, 0, 2))


def per_device(
    hidden_rows,
    expert_ids,
    route_weights,
    w_gate,
    w_up,
    w_down,
    codes,
    owner_slot,
    code_table,
    conv_state,
    conv_taps,
    conv_bias,
    upsample,
):
    count = lax.axis_size("expert")
    sessions, steps, width = hidden_rows.shape
    rows = sessions * steps
    books = codes.shape[2]
    expert_count = count * w_gate.shape[0]
    place = lax.axis_index("expert").astype(jnp.int32)[None]
    columns = (2 * expert_count, 2 * expert_count + 2 * books)

    own = pack(
        place,
        hidden_rows,
        expert_ids,
        route_weights,
        codes,
        owner_slot,
        columns,
        lax.axis_size("wave"),
    )
    half = count // 2
    weights = (w_gate, w_up, w_down.reshape(-1, width))
    sibling = [swap_wave(v) for v in after(weights, own)]
    held = [load(own, *weights)]

    blocks = {0: own}
    behind = ahead = own
    for step in range(1, half + 1):
        got = {step: shift(ahead, -1)}
        if step < half:
            got[count - step] = shift(behind, 1)
        first = held[0] if step == 1 else sibling[step - 2 : step - 1]
        got = {k: after((v,), first)[0] for k, v in got.items()}
        ahead, behind = got[step], got.get(count - step)
        blocks.update(got)

    held.append(sibling)
    near = [0, 1, count - 1, half]
    far = [
        [step, half + step - 1, count - step, half - step + 1] for step in range(2, count // 4 + 1)
    ]
    pairs, turn = [], place
    for group in far[::-1]:
        pairs.insert(0, experts([blocks[k] for k in group], 2, turn, held))
        (turn,) = after((place,), pairs[0])
    arrived = carry(pairs)
    order = near + [k for group in far for k in group]
    sizes = [4] + [2] * (2 * len(far))
    near_frames, *rest = frame_sums(
        blocks, order, sizes, turn, code_table, columns, width, sessions, steps
    )
    frames_arrived = carry(list(zip(rest[::2], rest[1::2])))
    (turn,) = after((place,), near_frames)
    (near_rows,) = experts([blocks[k] for k in near], 1, turn, held)
    left = towards(near_rows, arrived, rows)
    right = towards(near_frames, frames_arrived, rows)
    one, minus, across = join(list(zip(left, right)), rows, width, code_table.shape[2])
    last = [shift(one, 1), shift(minus, -1), shift(across, half)]
    return finish(
        [(near_rows, 0)],
        [(near_frames, 0)],
        last,
        width,
        conv_state,
        conv_taps,
        conv_bias,
        upsample,
        steps,
    )


def solution(mesh):
    rows = P(("groups", "expert", "wave"), None, None)
    placed = (
        rows,
        rows,
        rows,
        P("expert", None, "wave"),
        P("expert", None, "wave"),
        P("expert", "wave", None),
        rows,
        P(("groups", "expert", "wave")),
        P(None, "expert", None),
        rows,
        P(),
        P(),
        P(),
    )
    return jax.shard_map(
        per_device,
        mesh=mesh,
        in_specs=placed,
        out_specs=(rows, rows, rows),
        check_vma=False,
    )
```

```python
import functools

import jax
import jax.numpy as jnp
from jax import lax
from jax.experimental import pallas as pl
from jax.experimental.pallas import tpu as pltpu
from jax.sharding import PartitionSpec as P

F32 = jnp.float32
BF16 = jnp.bfloat16
VMEM_LIMIT = 8 * 1024 * 1024


def ring_order(count):
    return list(range(0, count, 2)) + list(range(1, count, 2))[::-1]


def shift(value, distance):
    count = lax.axis_size("expert")
    ring = ring_order(count)
    pairs = [(ring[i], ring[(i + distance) % count]) for i in range(count)]
    return lax.ppermute(value, "expert", pairs)


def swap_wave(value):
    return lax.ppermute(value, "wave", [(0, 1), (1, 0)])


def tidy(plan):
    arrays, numbers = [], {}

    def number(source):
        array, row = source
        if id(array) not in numbers:
            numbers[id(array)] = len(arrays)
            arrays.append(array)
        return numbers[id(array)], row

    return arrays, [[[[number(v) for v in part] for part in block] for block in out] for out in plan]


def summed(refs, sources, rows, columns):
    total = None
    for index, row in sources:
        value = refs[index][row : row + rows, columns].astype(F32)
        total = value if total is None else total + value
    return total


def join_kernel(plan, rows, width, *refs):
    for out_ref, ((left, right),) in zip(refs[-len(plan) :], plan):
        out_ref[:, 0:width] = summed(refs, left, rows, slice(None)).astype(BF16)
        out_ref[:, width:] = summed(refs, right, rows, slice(None)).astype(BF16)


def join(plan, rows, width, channels):
    arrays, numbered = tidy([[pair] for pair in plan])
    return pl.pallas_call(
        functools.partial(join_kernel, numbered, rows, width),
        out_shape=[jax.ShapeDtypeStruct((rows, width + channels), BF16)] * len(plan),
        compiler_params=pltpu.CompilerParams(vmem_limit_bytes=VMEM_LIMIT),
        cost_estimate=pl.CostEstimate(flops=0, bytes_accessed=1 << 20, transcendentals=0),
        name="join",
    )(*arrays)


def carry(pairs):
    ahead = back = None
    for forward, backward in pairs[::-1]:
        if ahead is not None:
            forward = (forward.astype(F32) + ahead.astype(F32)).astype(BF16)
            backward = (backward.astype(F32) + back.astype(F32)).astype(BF16)
        ahead, back = shift(forward, 1), shift(backward, -1)
    return ahead, back


def towards(near, arrived, rows):
    ahead, back = arrived
    return (
        [(near, rows), (ahead, 0)],
        [(near, 2 * rows), (back, 0)],
        [(near, 3 * rows), (ahead, rows), (back, rows)],
    )


def after(values, *earlier):
    return lax.optimization_barrier((tuple(values), earlier))[0]


def spot(rows, columns, offset):
    down = lax.broadcasted_iota(jnp.int32, (rows, columns), 0)
    across = lax.broadcasted_iota(jnp.int32, (rows, columns), 1)
    return jnp.where(across == down + offset, 1.0, 0.0).astype(BF16)


def digits(value):
    return [(value % 256).astype(F32).astype(BF16), (value // 256).astype(F32).astype(BF16)]


def pack_kernel(columns, n_wave, _, *refs):
    sources, out_ref, held = refs[:5], refs[5], refs[6:11]
    sems = refs[11]
    copies = [
        pltpu.make_async_copy(source, ref, sems.at[i])
        for i, (source, ref) in enumerate(zip(sources, held))
    ]
    hidden_ref, ids_ref, weights_ref, codes_ref, owner_ref = held
    for copy in copies:
        copy.start()
    for copy in copies[1:]:
        copy.wait()
    sessions, steps, width = hidden_ref.shape
    expert_count = columns[0] // 2
    books = codes_ref.shape[2]
    meta_width = out_ref.shape[1] - width
    owner = owner_ref[...]
    slots = (owner // sessions // n_wave) * sessions + owner % sessions
    down = lax.broadcasted_iota(jnp.int32, (sessions, sessions), 0)
    across = lax.broadcasted_iota(jnp.int32, (sessions, sessions), 1)
    slot = jnp.sum(jnp.where(down == across, slots, 0).astype(F32), axis=1, keepdims=True)
    slot = slot.astype(jnp.int32)
    lane = lax.broadcasted_iota(jnp.int32, (sessions, meta_width), 1)
    named = lax.broadcasted_iota(jnp.int32, (expert_count, sessions), 0)
    for t in range(steps):
        at = slice(t * sessions, (t + 1) * sessions)
        weight = jnp.zeros((expert_count, sessions), F32)
        for k in range(ids_ref.shape[1]):
            weight += jnp.where(named == ids_ref[t, k : k + 1, :], weights_ref[t, k : k + 1, :], 0.0)
        high = weight.astype(BF16)
        low = (weight - high.astype(F32)).astype(BF16)
        meta = jnp.zeros((sessions, meta_width), F32)
        for piece, offset in ((high, 0), (low, expert_count)):
            meta += lax.dot_general(
                piece,
                spot(expert_count, meta_width, offset),
                (((0,), (0,)), ((), ())),
                preferred_element_type=F32,
            )
        for i, piece in enumerate(digits(codes_ref[:, t, :])):
            move = spot(books, meta_width, columns[0] + i * books)
            meta += jnp.dot(piece, move, preferred_element_type=F32)
        for i, piece in enumerate(digits(slot * steps + t)):
            meta += jnp.where(lane == columns[1] + i, piece.astype(F32), 0.0)
        out_ref[at, width:] = meta.astype(BF16)
    copies[0].wait()
    for t in range(steps):
        out_ref[t * sessions : (t + 1) * sessions, 0:width] = hidden_ref[:, t, :]


def pack(place, hidden_rows, expert_ids, route_weights, codes, owner_slot, columns, n_wave):
    sessions, steps, width = hidden_rows.shape
    meta_width = -(-(columns[1] + 2) // 128) * 128
    args = (
        hidden_rows,
        jnp.transpose(expert_ids, (1, 2, 0)),
        jnp.transpose(route_weights, (1, 2, 0)),
        codes,
        owner_slot[None],
    )
    return pl.pallas_call(
        functools.partial(pack_kernel, columns, n_wave),
        out_shape=jax.ShapeDtypeStruct((steps * sessions, width + meta_width), BF16),
        in_specs=[pl.BlockSpec(memory_space=pltpu.SMEM)]
        + [pl.BlockSpec(memory_space=pltpu.HBM)] * len(args),
        out_specs=pl.BlockSpec(memory_space=pltpu.VMEM),
        scratch_shapes=[pltpu.VMEM(arg.shape, arg.dtype) for arg in args]
        + [pltpu.SemaphoreType.DMA((len(args),))],
        compiler_params=pltpu.CompilerParams(vmem_limit_bytes=VMEM_LIMIT),
        name="pack",
    )(place, *[pltpu.with_memory_space_constraint(arg, pltpu.HBM) for arg in args])


def load_kernel(code_at, books, shard, *refs):
    count = (len(refs) - 3) // 2
    sources, held, spread_ref, sems = refs[1 : count + 1], refs[count + 1 : -2], refs[-2], refs[-1]
    copies = [
        pltpu.make_async_copy(source, ref, sems.at[i])
        for i, (source, ref) in enumerate(zip(sources, held))
    ]
    for copy in copies:
        copy.start()
    column = lax.broadcasted_iota(jnp.int32, spread_ref.shape, 0) - code_at
    book = lax.broadcasted_iota(jnp.int32, spread_ref.shape, 1) // shard
    spread = jnp.where(column == book, 1.0, jnp.where(column == book + books, 256.0, 0.0))
    spread_ref[...] = spread.astype(BF16)
    for copy in copies:
        copy.wait()


def load(earlier, arrays, meta_width, code_at, books, shard):
    hbm = pl.BlockSpec(memory_space=pltpu.HBM)
    return pl.pallas_call(
        functools.partial(load_kernel, code_at, books, shard),
        out_shape=[pltpu.VMEM(v.shape, v.dtype) for v in arrays]
        + [pltpu.VMEM((meta_width, books * shard), BF16)],
        in_specs=[pl.BlockSpec(memory_space=pl.ANY)] + [hbm] * len(arrays),
        out_specs=[pl.BlockSpec(memory_space=pltpu.VMEM)] * (len(arrays) + 1),
        scratch_shapes=[pltpu.SemaphoreType.DMA((len(arrays),))],
        compiler_params=pltpu.CompilerParams(vmem_limit_bytes=VMEM_LIMIT),
        cost_estimate=pl.CostEstimate(
            flops=0, bytes_accessed=sum(2 * v.size for v in arrays), transcendentals=0
        ),
        name="load",
    )(earlier, *[pltpu.with_memory_space_constraint(v, pltpu.HBM) for v in arrays])


def experts_kernel(width, expert_count, block_count, out_count, place_ref, *refs):
    blocks = refs[:block_count]
    parts = [refs[i : i + 3] for i in range(block_count, len(refs) - 2 - out_count, 3)]
    outs, (rows_ref, act_ref) = refs[-2 - out_count : -2], refs[-2:]
    rows = blocks[0].shape[0]
    for i, block in enumerate(blocks):
        rows_ref[i * rows : (i + 1) * rows, :] = block[:, 0:width]
    meta = jnp.concatenate([block[:, width:].astype(F32) for block in blocks], axis=0)
    lane = lax.broadcasted_iota(jnp.int32, meta.shape, 1)
    total = None
    for gate_ref, up_ref, down_ref in parts:
        local, _, units = gate_ref.shape
        for j in range(local):
            mine = place_ref[0] * local + j
            hit = (lane == mine) | (lane == expert_count + mine)
            weight = jnp.sum(jnp.where(hit, meta, 0.0), axis=1, keepdims=True)
            both = jnp.concatenate([gate_ref[j], up_ref[j]], axis=1)
            both = jnp.dot(rows_ref[...], both, preferred_element_type=F32)
            gate, up = both[:, 0:units], both[:, units:]
            value = gate * jax.nn.sigmoid(gate) * up
            act_ref[:, j * units : (j + 1) * units] = (value * weight).astype(BF16)
        result = jnp.dot(act_ref[...], down_ref[...], preferred_element_type=F32)
        total = result if total is None else total + result
    start = 0
    for out_ref in outs:
        size = out_ref.shape[0]
        out_ref[...] = total[start : start + size].astype(BF16)
        start += size


def experts(blocks, split, place, held):
    local, width, units = held[0][0].shape
    rows = blocks[0].shape[0]
    total = rows * len(blocks)
    vmem = pl.BlockSpec(memory_space=pltpu.VMEM)
    weights = [v for part in held for v in part]
    return pl.pallas_call(
        functools.partial(
            experts_kernel, width, lax.axis_size("expert") * local, len(blocks), split
        ),
        out_shape=[jax.ShapeDtypeStruct((total // split, width), BF16)] * split,
        in_specs=[pl.BlockSpec(memory_space=pltpu.SMEM)] + [vmem] * (len(blocks) + len(weights)),
        out_specs=[vmem] * split,
        scratch_shapes=[
            pltpu.VMEM((total, width), BF16),
            pltpu.VMEM((total, local * units), BF16),
        ],
        compiler_params=pltpu.CompilerParams(vmem_limit_bytes=VMEM_LIMIT),
        cost_estimate=pl.CostEstimate(
            flops=6 * total * width * units * local * len(held),
            bytes_accessed=2 * sum(v.size for v in weights),
            transcendentals=total * units * local * len(held),
        ),
        name="experts",
    )(place, *blocks, *weights)


def frames_kernel(slot_at, shard, sessions, steps, sources, order, place_ref, *refs):
    count = len(sources)
    metas, (spread_ref, table_ref, *outs, hot_ref) = refs[:count], refs[count:]
    rows = metas[0].shape[0]
    meta = jnp.concatenate([m[...] for m in metas], axis=0)
    column = lax.broadcasted_iota(jnp.int32, (8, meta.shape[1]), 1)
    digit = lax.broadcasted_iota(jnp.int32, (8, meta.shape[1]), 0)
    picks = jnp.where((column == slot_at + digit) & (digit < 2), 1.0, 0.0).astype(BF16)
    slots = lax.dot_general(picks, meta, (((1,), (1,)), ((), ())), preferred_element_type=F32)
    source = (slots[0:1] + 256.0 * slots[1:2]).astype(jnp.int32)
    row = lax.broadcasted_iota(jnp.int32, (rows * len(order), 1), 0)
    inside = row % rows
    target = (inside % sessions) * steps + inside // sessions
    place = place_ref[0]
    turn = jnp.where(place % 2 == 0, place // 2, count - 1 - place // 2)
    for i, k in enumerate(order):
        at = (turn + k) % count
        device = jnp.where(at < count // 2, 2 * at, 2 * (count - 1 - at) + 1)
        target = target + jnp.where(row // rows == i, device * rows, 0)
    chooser = jnp.where(target == source, 1.0, 0.0).astype(BF16)
    ordered = jnp.dot(chooser, meta, preferred_element_type=F32).astype(BF16)
    codes = jnp.dot(ordered, spread_ref[...], preferred_element_type=F32)
    entry = lax.broadcasted_iota(jnp.int32, (1, hot_ref.shape[1]), 1) % shard + place * shard
    hot_ref[...] = jnp.where(codes == entry.astype(F32), 1.0, 0.0).astype(BF16)
    result = jnp.dot(hot_ref[...], table_ref[...], preferred_element_type=F32)
    start = 0
    for out_ref in outs:
        size = out_ref.shape[0]
        out_ref[...] = result[start : start + size].astype(BF16)
        start += size


def frame_sums(blocks, order, split, place, code_table, spread, slot_at, sessions, steps):
    books, shard, channels = code_table.shape
    meta_width = spread.shape[0]
    sources = list(range(len(blocks)))
    rows, width = blocks[0].shape
    total = rows * len(order)
    block = pl.BlockSpec((rows, meta_width), lambda i: (0, width // meta_width - 1))
    vmem = pl.BlockSpec(memory_space=pltpu.VMEM)
    return pl.pallas_call(
        functools.partial(frames_kernel, slot_at, shard, sessions, steps, sources, order),
        grid=(1,),
        out_shape=[jax.ShapeDtypeStruct((total // split, channels), BF16)] * split,
        in_specs=[pl.BlockSpec(memory_space=pltpu.SMEM)] + [block] * len(sources) + [vmem] * 2,
        out_specs=[vmem] * split,
        scratch_shapes=[pltpu.VMEM((total, books * shard), BF16)],
        compiler_params=pltpu.CompilerParams(
            vmem_limit_bytes=VMEM_LIMIT + 12 * total * rows * len(sources)
        ),
        cost_estimate=pl.CostEstimate(
            flops=2 * total * books * shard * channels,
            bytes_accessed=2 * books * shard * channels,
            transcendentals=0,
        ),
        name="frame_sums",
    )(place, *[blocks[k] for k in sources], spread, code_table.reshape(books * shard, channels))


def finish_kernel(left, right, whole, width, *refs):
    state_ref, taps_ref, bias_ref, up_ref, mixed_ref, wave_ref, new_ref = refs[-7:]
    past, sessions, _ = state_ref.shape
    steps = mixed_ref.shape[1]
    rows = steps * sessions
    taps = taps_ref.shape[0]
    frames = summed(refs, right, rows, slice(None))
    for index, row in whole:
        frames = frames + refs[index][row : row + rows, width:].astype(F32)
    history = [state_ref[i].astype(F32) for i in range(past)]
    history += [frames[t * sessions : (t + 1) * sessions] for t in range(steps)]
    decoded = []
    for t in range(steps):
        filtered = bias_ref[...] + taps_ref[0:1, :] * history[past + t]
        for j in range(1, taps):
            filtered = filtered + taps_ref[j : j + 1, :] * history[past + t - j]
        decoded.append(jax.nn.gelu(filtered).astype(BF16))
    samples = jnp.dot(jnp.concatenate(decoded), up_ref[...], preferred_element_type=F32)
    total = summed(refs, left, rows, slice(None))
    for index, row in whole:
        total = total + refs[index][row : row + rows, 0:width].astype(F32)
    for t in range(steps):
        at = slice(t * sessions, (t + 1) * sessions)
        wave_ref[:, t, :] = samples[at].astype(BF16)
        mixed_ref[:, t, :] = total[at].astype(BF16)
    for i in range(past):
        new_ref[i] = history[i + steps].astype(BF16)


def finish(left, right, arrived, width, conv_state, conv_taps, conv_bias, upsample, steps):
    sessions, past, channels = conv_state.shape
    arrays, numbered = tidy([[(left, right, [(v, 0) for v in arrived])]])
    mixed, wave, state = pl.pallas_call(
        functools.partial(finish_kernel, *numbered[0][0], width),
        out_shape=(
            jax.ShapeDtypeStruct((sessions, steps, width), BF16),
            jax.ShapeDtypeStruct((sessions, steps, upsample.shape[1]), BF16),
            jax.ShapeDtypeStruct((past, sessions, channels), BF16),
        ),
        compiler_params=pltpu.CompilerParams(vmem_limit_bytes=VMEM_LIMIT),
        cost_estimate=pl.CostEstimate(flops=0, bytes_accessed=1 << 21, transcendentals=0),
        name="finish",
    )(
        *arrays,
        jnp.transpose(conv_state, (1, 0, 2)),
        conv_taps,
        conv_bias.reshape(1, channels),
        upsample,
    )
    return mixed, wave, jnp.transpose(state, (1, 0, 2))


def per_device(
    hidden_rows,
    expert_ids,
    route_weights,
    w_gate,
    w_up,
    w_down,
    codes,
    owner_slot,
    code_table,
    conv_state,
    conv_taps,
    conv_bias,
    upsample,
):
    count = lax.axis_size("expert")
    sessions, steps, width = hidden_rows.shape
    rows = sessions * steps
    books = codes.shape[2]
    expert_count = count * w_gate.shape[0]
    place = lax.axis_index("expert").astype(jnp.int32)[None]
    columns = (2 * expert_count, 2 * expert_count + 2 * books)

    own = pack(
        place,
        hidden_rows,
        expert_ids,
        route_weights,
        codes,
        owner_slot,
        columns,
        lax.axis_size("wave"),
    )
    half = count // 2
    weights = (w_gate, w_up, w_down.reshape(-1, width))
    sibling = [swap_wave(v) for v in after(weights, own)]
    meta_width = own.shape[1] - width
    *loaded, spread = load(
        own, weights, meta_width, columns[0], books, code_table.shape[1]
    )
    held = [loaded]

    blocks = {0: own}
    behind = ahead = own
    for step in range(1, half + 1):
        got = {step: shift(ahead, -1)}
        if step < half:
            got[count - step] = shift(behind, 1)
        first = held[0] if step == 1 else sibling[step - 2 : step - 1]
        got = {k: after((v,), first)[0] for k, v in got.items()}
        ahead, behind = got[step], got.get(count - step)
        blocks.update(got)

    held.append(sibling)
    near = [0, 1, count - 1, half]
    far = [
        [step, half + step - 1, count - step, half - step + 1] for step in range(2, count // 4 + 1)
    ]
    pairs, turn = [], place
    for group in far[::-1]:
        pairs.insert(0, experts([blocks[k] for k in group], 2, turn, held))
        (turn,) = after((place,), pairs[0])
    arrived = carry(pairs)

    def frames(order, split, turn):
        return frame_sums(
            blocks, order, split, turn, code_table, spread, columns[1], sessions, steps
        )

    far_frames = frames([k for group in far for k in group], 2 * len(far), turn)
    frames_arrived = carry(list(zip(far_frames[::2], far_frames[1::2])))
    (turn,) = after((place,), far_frames)
    (near_rows,) = experts([blocks[k] for k in near], 1, turn, held)
    (turn,) = after((place,), near_rows)
    (near_frames,) = frames(near, 1, turn)
    left = towards(near_rows, arrived, rows)
    right = towards(near_frames, frames_arrived, rows)
    one, minus, across = join(list(zip(left, right)), rows, width, code_table.shape[2])
    last = [shift(one, 1), shift(minus, -1), shift(across, half)]
    return finish(
        [(near_rows, 0)],
        [(near_frames, 0)],
        last,
        width,
        conv_state,
        conv_taps,
        conv_bias,
        upsample,
        steps,
    )


def solution(mesh):
    rows = P(("groups", "expert", "wave"), None, None)
    placed = (
        rows,
        rows,
        rows,
        P("expert", None, "wave"),
        P("expert", None, "wave"),
        P("expert", "wave", None),
        rows,
        P(("groups", "expert", "wave")),
        P(None, "expert", None),
        rows,
        P(),
        P(),
        P(),
    )
    return jax.shard_map(
        per_device,
        mesh=mesh,
        in_specs=placed,
        out_specs=(rows, rows, rows),
        check_vma=False,
    )
```

```python
import functools

import jax
import jax.numpy as jnp
from jax import lax
from jax.experimental import pallas as pl
from jax.experimental.pallas import tpu as pltpu
from jax.sharding import PartitionSpec as P

F32 = jnp.float32
BF16 = jnp.bfloat16
VMEM_LIMIT = 8 * 1024 * 1024


def ring_order(count):
    return list(range(0, count, 2)) + list(range(1, count, 2))[::-1]


def shift(value, distance):
    count = lax.axis_size("expert")
    ring = ring_order(count)
    pairs = [(ring[i], ring[(i + distance) % count]) for i in range(count)]
    return lax.ppermute(value, "expert", pairs)


def swap_wave(value):
    return lax.ppermute(value, "wave", [(0, 1), (1, 0)])


def tidy(plan):
    arrays, numbers = [], {}

    def number(source):
        array, row = source
        if id(array) not in numbers:
            numbers[id(array)] = len(arrays)
            arrays.append(array)
        return numbers[id(array)], row

    return arrays, [[[[number(v) for v in part] for part in block] for block in out] for out in plan]


def summed(refs, sources, rows, columns):
    total = None
    for index, row in sources:
        value = refs[index][row : row + rows, columns].astype(F32)
        total = value if total is None else total + value
    return total


def join_kernel(plan, rows, width, *refs):
    for out_ref, ((left, right),) in zip(refs[-len(plan) :], plan):
        out_ref[:, 0:width] = summed(refs, left, rows, slice(None)).astype(BF16)
        out_ref[:, width:] = summed(refs, right, rows, slice(None)).astype(BF16)


def join(plan, rows, width, channels):
    arrays, numbered = tidy([[pair] for pair in plan])
    return pl.pallas_call(
        functools.partial(join_kernel, numbered, rows, width),
        out_shape=[jax.ShapeDtypeStruct((rows, width + channels), BF16)] * len(plan),
        compiler_params=pltpu.CompilerParams(vmem_limit_bytes=VMEM_LIMIT),
        cost_estimate=pl.CostEstimate(flops=0, bytes_accessed=1 << 20, transcendentals=0),
        name="join",
    )(*arrays)


def carry(pairs):
    ahead = back = None
    for forward, backward in pairs[::-1]:
        if ahead is not None:
            forward = (forward.astype(F32) + ahead.astype(F32)).astype(BF16)
            backward = (backward.astype(F32) + back.astype(F32)).astype(BF16)
        ahead, back = shift(forward, 1), shift(backward, -1)
    return ahead, back


def towards(near, arrived, rows):
    ahead, back = arrived
    return (
        [(near, rows), (ahead, 0)],
        [(near, 2 * rows), (back, 0)],
        [(near, 3 * rows), (ahead, rows), (back, rows)],
    )


def after(values, *earlier):
    return lax.optimization_barrier((tuple(values), earlier))[0]


def spot(rows, columns, offset):
    down = lax.broadcasted_iota(jnp.int32, (rows, columns), 0)
    across = lax.broadcasted_iota(jnp.int32, (rows, columns), 1)
    return jnp.where(across == down + offset, 1.0, 0.0).astype(BF16)


def digits(value):
    return [(value % 256).astype(F32).astype(BF16), (value // 256).astype(F32).astype(BF16)]


def pack_kernel(columns, n_wave, _, *refs):
    sources, out_ref, held = refs[:5], refs[5], refs[6:11]
    sems = refs[11]
    copies = [
        pltpu.make_async_copy(source, ref, sems.at[i])
        for i, (source, ref) in enumerate(zip(sources, held))
    ]
    hidden_ref, ids_ref, weights_ref, codes_ref, owner_ref = held
    for copy in copies:
        copy.start()
    for copy in copies[1:]:
        copy.wait()
    sessions, steps, width = hidden_ref.shape
    expert_count = columns[0] // 2
    books = codes_ref.shape[2]
    meta_width = out_ref.shape[1] - width
    owner = owner_ref[...]
    slots = (owner // sessions // n_wave) * sessions + owner % sessions
    down = lax.broadcasted_iota(jnp.int32, (sessions, sessions), 0)
    across = lax.broadcasted_iota(jnp.int32, (sessions, sessions), 1)
    slot = jnp.sum(jnp.where(down == across, slots, 0).astype(F32), axis=1, keepdims=True)
    slot = slot.astype(jnp.int32)
    lane = lax.broadcasted_iota(jnp.int32, (sessions, meta_width), 1)
    named = lax.broadcasted_iota(jnp.int32, (expert_count, sessions), 0)
    for t in range(steps):
        at = slice(t * sessions, (t + 1) * sessions)
        weight = jnp.zeros((expert_count, sessions), F32)
        for k in range(ids_ref.shape[1]):
            weight += jnp.where(named == ids_ref[t, k : k + 1, :], weights_ref[t, k : k + 1, :], 0.0)
        high = weight.astype(BF16)
        low = (weight - high.astype(F32)).astype(BF16)
        meta = jnp.zeros((sessions, meta_width), F32)
        for piece, offset in ((high, 0), (low, expert_count)):
            meta += lax.dot_general(
                piece,
                spot(expert_count, meta_width, offset),
                (((0,), (0,)), ((), ())),
                preferred_element_type=F32,
            )
        for i, piece in enumerate(digits(codes_ref[:, t, :])):
            move = spot(books, meta_width, columns[0] + i * books)
            meta += jnp.dot(piece, move, preferred_element_type=F32)
        for i, piece in enumerate(digits(slot * steps + t)):
            meta += jnp.where(lane == columns[1] + i, piece.astype(F32), 0.0)
        out_ref[at, width:] = meta.astype(BF16)
    copies[0].wait()
    for t in range(steps):
        out_ref[t * sessions : (t + 1) * sessions, 0:width] = hidden_ref[:, t, :]


def pack(place, hidden_rows, expert_ids, route_weights, codes, owner_slot, columns, n_wave):
    sessions, steps, width = hidden_rows.shape
    meta_width = -(-(columns[1] + 2) // 128) * 128
    args = (
        hidden_rows,
        jnp.transpose(expert_ids, (1, 2, 0)),
        jnp.transpose(route_weights, (1, 2, 0)),
        codes,
        owner_slot[None],
    )
    return pl.pallas_call(
        functools.partial(pack_kernel, columns, n_wave),
        out_shape=jax.ShapeDtypeStruct((steps * sessions, width + meta_width), BF16),
        in_specs=[pl.BlockSpec(memory_space=pltpu.SMEM)]
        + [pl.BlockSpec(memory_space=pltpu.HBM)] * len(args),
        out_specs=pl.BlockSpec(memory_space=pltpu.VMEM),
        scratch_shapes=[pltpu.VMEM(arg.shape, arg.dtype) for arg in args]
        + [pltpu.SemaphoreType.DMA((len(args),))],
        compiler_params=pltpu.CompilerParams(vmem_limit_bytes=VMEM_LIMIT),
        name="pack",
    )(place, *[pltpu.with_memory_space_constraint(arg, pltpu.HBM) for arg in args])


def load_kernel(code_at, books, shard, *refs):
    count = (len(refs) - 3) // 2
    sources, held, spread_ref, sems = refs[1 : count + 1], refs[count + 1 : -2], refs[-2], refs[-1]
    copies = [
        pltpu.make_async_copy(source, ref, sems.at[i])
        for i, (source, ref) in enumerate(zip(sources, held))
    ]
    for copy in copies:
        copy.start()
    column = lax.broadcasted_iota(jnp.int32, spread_ref.shape, 0) - code_at
    book = lax.broadcasted_iota(jnp.int32, spread_ref.shape, 1) // shard
    spread = jnp.where(column == book, 1.0, jnp.where(column == book + books, 256.0, 0.0))
    spread_ref[...] = spread.astype(BF16)
    for copy in copies:
        copy.wait()


def load(earlier, arrays, meta_width, code_at, books, shard):
    hbm = pl.BlockSpec(memory_space=pltpu.HBM)
    return pl.pallas_call(
        functools.partial(load_kernel, code_at, books, shard),
        out_shape=[pltpu.VMEM(v.shape, v.dtype) for v in arrays]
        + [pltpu.VMEM((meta_width, books * shard), BF16)],
        in_specs=[pl.BlockSpec(memory_space=pl.ANY)] + [hbm] * len(arrays),
        out_specs=[pl.BlockSpec(memory_space=pltpu.VMEM)] * (len(arrays) + 1),
        scratch_shapes=[pltpu.SemaphoreType.DMA((len(arrays),))],
        compiler_params=pltpu.CompilerParams(vmem_limit_bytes=VMEM_LIMIT),
        cost_estimate=pl.CostEstimate(
            flops=0, bytes_accessed=sum(2 * v.size for v in arrays), transcendentals=0
        ),
        name="load",
    )(earlier, *[pltpu.with_memory_space_constraint(v, pltpu.HBM) for v in arrays])


def experts_kernel(width, expert_count, block_count, out_count, place_ref, *refs):
    blocks = refs[:block_count]
    parts = [refs[i : i + 3] for i in range(block_count, len(refs) - 2 - out_count, 3)]
    outs, (rows_ref, act_ref) = refs[-2 - out_count : -2], refs[-2:]
    rows = blocks[0].shape[0]
    for i, block in enumerate(blocks):
        rows_ref[i * rows : (i + 1) * rows, :] = block[:, 0:width]
    meta = jnp.concatenate([block[:, width:].astype(F32) for block in blocks], axis=0)
    lane = lax.broadcasted_iota(jnp.int32, meta.shape, 1)
    total = None
    for gate_ref, up_ref, down_ref in parts:
        local, _, units = gate_ref.shape
        for j in range(local):
            mine = place_ref[0] * local + j
            hit = (lane == mine) | (lane == expert_count + mine)
            weight = jnp.sum(jnp.where(hit, meta, 0.0), axis=1, keepdims=True)
            both = jnp.concatenate([gate_ref[j], up_ref[j]], axis=1)
            both = jnp.dot(rows_ref[...], both, preferred_element_type=F32)
            gate, up = both[:, 0:units], both[:, units:]
            value = gate * jax.nn.sigmoid(gate) * up
            act_ref[:, j * units : (j + 1) * units] = (value * weight).astype(BF16)
        result = jnp.dot(act_ref[...], down_ref[...], preferred_element_type=F32)
        total = result if total is None else total + result
    start = 0
    for out_ref in outs:
        size = out_ref.shape[0]
        out_ref[...] = total[start : start + size].astype(BF16)
        start += size


def experts(blocks, split, place, held):
    local, width, units = held[0][0].shape
    rows = blocks[0].shape[0]
    total = rows * len(blocks)
    vmem = pl.BlockSpec(memory_space=pltpu.VMEM)
    weights = [v for part in held for v in part]
    return pl.pallas_call(
        functools.partial(
            experts_kernel, width, lax.axis_size("expert") * local, len(blocks), split
        ),
        out_shape=[jax.ShapeDtypeStruct((total // split, width), BF16)] * split,
        in_specs=[pl.BlockSpec(memory_space=pltpu.SMEM)] + [vmem] * (len(blocks) + len(weights)),
        out_specs=[vmem] * split,
        scratch_shapes=[
            pltpu.VMEM((total, width), BF16),
            pltpu.VMEM((total, local * units), BF16),
        ],
        compiler_params=pltpu.CompilerParams(vmem_limit_bytes=VMEM_LIMIT),
        cost_estimate=pl.CostEstimate(
            flops=6 * total * width * units * local * len(held),
            bytes_accessed=2 * sum(v.size for v in weights),
            transcendentals=total * units * local * len(held),
        ),
        name="experts",
    )(place, *blocks, *weights)


def frames_kernel(slot_at, shard, sessions, steps, sources, order, place_ref, *refs):
    count = len(sources)
    metas, (spread_ref, table_ref, *outs, hot_ref) = refs[:count], refs[count:]
    rows = metas[0].shape[0]
    last = metas[0].shape[1] - spread_ref.shape[0]
    meta = jnp.concatenate([m[:, last:] for m in metas], axis=0)
    column = lax.broadcasted_iota(jnp.int32, (8, meta.shape[1]), 1)
    digit = lax.broadcasted_iota(jnp.int32, (8, meta.shape[1]), 0)
    picks = jnp.where((column == slot_at + digit) & (digit < 2), 1.0, 0.0).astype(BF16)
    slots = lax.dot_general(picks, meta, (((1,), (1,)), ((), ())), preferred_element_type=F32)
    source = (slots[0:1] + 256.0 * slots[1:2]).astype(jnp.int32)
    row = lax.broadcasted_iota(jnp.int32, (rows * len(order), 1), 0)
    inside = row % rows
    target = (inside % sessions) * steps + inside // sessions
    place = place_ref[0]
    turn = jnp.where(place % 2 == 0, place // 2, count - 1 - place // 2)
    for i, k in enumerate(order):
        at = (turn + k) % count
        device = jnp.where(at < count // 2, 2 * at, 2 * (count - 1 - at) + 1)
        target = target + jnp.where(row // rows == i, device * rows, 0)
    chooser = jnp.where(target == source, 1.0, 0.0).astype(BF16)
    ordered = jnp.dot(chooser, meta, preferred_element_type=F32).astype(BF16)
    codes = jnp.dot(ordered, spread_ref[...], preferred_element_type=F32)
    entry = lax.broadcasted_iota(jnp.int32, (1, hot_ref.shape[1]), 1) % shard + place * shard
    hot_ref[...] = jnp.where(codes == entry.astype(F32), 1.0, 0.0).astype(BF16)
    result = jnp.dot(hot_ref[...], table_ref[...], preferred_element_type=F32)
    start = 0
    for out_ref in outs:
        size = out_ref.shape[0]
        out_ref[...] = result[start : start + size].astype(BF16)
        start += size


def frame_sums(blocks, order, split, place, code_table, spread, slot_at, sessions, steps):
    books, shard, channels = code_table.shape
    sources = list(range(len(blocks)))
    rows = blocks[0].shape[0]
    total = rows * len(order)
    vmem = pl.BlockSpec(memory_space=pltpu.VMEM)
    return pl.pallas_call(
        functools.partial(frames_kernel, slot_at, shard, sessions, steps, sources, order),
        out_shape=[jax.ShapeDtypeStruct((total // split, channels), BF16)] * split,
        in_specs=[pl.BlockSpec(memory_space=pltpu.SMEM)] + [vmem] * (len(sources) + 2),
        out_specs=[vmem] * split,
        scratch_shapes=[pltpu.VMEM((total, books * shard), BF16)],
        compiler_params=pltpu.CompilerParams(
            vmem_limit_bytes=VMEM_LIMIT + 12 * total * rows * len(sources)
        ),
        cost_estimate=pl.CostEstimate(
            flops=2 * total * books * shard * channels,
            bytes_accessed=2 * books * shard * channels,
            transcendentals=0,
        ),
        name="frame_sums",
    )(place, *[blocks[k] for k in sources], spread, code_table.reshape(books * shard, channels))


def finish_kernel(left, right, whole, width, *refs):
    state_ref, taps_ref, bias_ref, up_ref, mixed_ref, wave_ref, new_ref = refs[-7:]
    past, sessions, _ = state_ref.shape
    steps = mixed_ref.shape[1]
    rows = steps * sessions
    taps = taps_ref.shape[0]
    frames = summed(refs, right, rows, slice(None))
    for index, row in whole:
        frames = frames + refs[index][row : row + rows, width:].astype(F32)
    history = [state_ref[i].astype(F32) for i in range(past)]
    history += [frames[t * sessions : (t + 1) * sessions] for t in range(steps)]
    decoded = []
    for t in range(steps):
        filtered = bias_ref[...] + taps_ref[0:1, :] * history[past + t]
        for j in range(1, taps):
            filtered = filtered + taps_ref[j : j + 1, :] * history[past + t - j]
        decoded.append(jax.nn.gelu(filtered).astype(BF16))
    samples = jnp.dot(jnp.concatenate(decoded), up_ref[...], preferred_element_type=F32)
    total = summed(refs, left, rows, slice(None))
    for index, row in whole:
        total = total + refs[index][row : row + rows, 0:width].astype(F32)
    for t in range(steps):
        at = slice(t * sessions, (t + 1) * sessions)
        wave_ref[:, t, :] = samples[at].astype(BF16)
        mixed_ref[:, t, :] = total[at].astype(BF16)
    for i in range(past):
        new_ref[i] = history[i + steps].astype(BF16)


def finish(left, right, arrived, width, conv_state, conv_taps, conv_bias, upsample, steps):
    sessions, past, channels = conv_state.shape
    arrays, numbered = tidy([[(left, right, [(v, 0) for v in arrived])]])
    mixed, wave, state = pl.pallas_call(
        functools.partial(finish_kernel, *numbered[0][0], width),
        out_shape=(
            jax.ShapeDtypeStruct((sessions, steps, width), BF16),
            jax.ShapeDtypeStruct((sessions, steps, upsample.shape[1]), BF16),
            jax.ShapeDtypeStruct((past, sessions, channels), BF16),
        ),
        compiler_params=pltpu.CompilerParams(vmem_limit_bytes=VMEM_LIMIT),
        cost_estimate=pl.CostEstimate(flops=0, bytes_accessed=1 << 21, transcendentals=0),
        name="finish",
    )(
        *arrays,
        jnp.transpose(conv_state, (1, 0, 2)),
        conv_taps,
        conv_bias.reshape(1, channels),
        upsample,
    )
    return mixed, wave, jnp.transpose(state, (1, 0, 2))


def per_device(
    hidden_rows,
    expert_ids,
    route_weights,
    w_gate,
    w_up,
    w_down,
    codes,
    owner_slot,
    code_table,
    conv_state,
    conv_taps,
    conv_bias,
    upsample,
):
    count = lax.axis_size("expert")
    sessions, steps, width = hidden_rows.shape
    rows = sessions * steps
    books = codes.shape[2]
    expert_count = count * w_gate.shape[0]
    place = lax.axis_index("expert").astype(jnp.int32)[None]
    columns = (2 * expert_count, 2 * expert_count + 2 * books)

    own = pack(
        place,
        hidden_rows,
        expert_ids,
        route_weights,
        codes,
        owner_slot,
        columns,
        lax.axis_size("wave"),
    )
    half = count // 2
    weights = (w_gate, w_up, w_down.reshape(-1, width))
    sibling = [swap_wave(v) for v in after(weights, own)]
    meta_width = own.shape[1] - width
    *loaded, spread = load(
        own, weights, meta_width, columns[0], books, code_table.shape[1]
    )
    held = [loaded]

    blocks = {0: own}
    behind = ahead = own
    for step in range(1, half + 1):
        got = {step: shift(ahead, -1)}
        if step < half:
            got[count - step] = shift(behind, 1)
        first = held[0] if step == 1 else sibling[step - 2 : step - 1]
        got = {k: after((v,), first)[0] for k, v in got.items()}
        ahead, behind = got[step], got.get(count - step)
        blocks.update(got)

    held.append(sibling)
    near = [0, 1, count - 1, half]
    far = [
        [step, half + step - 1, count - step, half - step + 1] for step in range(2, count // 4 + 1)
    ]
    pairs, turn = [], place
    for group in far[::-1]:
        pairs.insert(0, experts([blocks[k] for k in group], 2, turn, held))
        (turn,) = after((place,), pairs[0])
    arrived = carry(pairs)

    def frames(order, split, turn):
        return frame_sums(
            blocks, order, split, turn, code_table, spread, columns[1], sessions, steps
        )

    far_frames = frames([k for group in far for k in group], 2 * len(far), turn)
    frames_arrived = carry(list(zip(far_frames[::2], far_frames[1::2])))
    (turn,) = after((place,), far_frames)
    (near_rows,) = experts([blocks[k] for k in near], 1, turn, held)
    (turn,) = after((place,), near_rows)
    (near_frames,) = frames(near, 1, turn)
    left = towards(near_rows, arrived, rows)
    right = towards(near_frames, frames_arrived, rows)
    one, minus, across = join(list(zip(left, right)), rows, width, code_table.shape[2])
    last = [shift(one, 1), shift(across, half), shift(minus, -1)]
    return finish(
        [(near_rows, 0)],
        [(near_frames, 0)],
        last,
        width,
        conv_state,
        conv_taps,
        conv_bias,
        upsample,
        steps,
    )


def solution(mesh):
    rows = P(("groups", "expert", "wave"), None, None)
    placed = (
        rows,
        rows,
        rows,
        P("expert", None, "wave"),
        P("expert", None, "wave"),
        P("expert", "wave", None),
        rows,
        P(("groups", "expert", "wave")),
        P(None, "expert", None),
        rows,
        P(),
        P(),
        P(),
    )
    return jax.shard_map(
        per_device,
        mesh=mesh,
        in_specs=placed,
        out_specs=(rows, rows, rows),
        check_vma=False,
    )
```

```python
import functools

import jax
import jax.numpy as jnp
from jax import lax
from jax.experimental import pallas as pl
from jax.experimental.pallas import tpu as pltpu
from jax.sharding import PartitionSpec as P

F32 = jnp.float32
BF16 = jnp.bfloat16
VMEM_LIMIT = 8 * 1024 * 1024


def ring_order(count):
    return list(range(0, count, 2)) + list(range(1, count, 2))[::-1]


def shift(value, distance):
    count = lax.axis_size("expert")
    ring = ring_order(count)
    pairs = [(ring[i], ring[(i + distance) % count]) for i in range(count)]
    return lax.ppermute(value, "expert", pairs)


def swap_wave(value):
    return lax.ppermute(value, "wave", [(0, 1), (1, 0)])


def tidy(plan):
    arrays, numbers = [], {}

    def number(source):
        array, row = source
        if id(array) not in numbers:
            numbers[id(array)] = len(arrays)
            arrays.append(array)
        return numbers[id(array)], row

    return arrays, [[[[number(v) for v in part] for part in block] for block in out] for out in plan]


def summed(refs, sources, rows, columns):
    total = None
    for index, row in sources:
        value = refs[index][row : row + rows, columns].astype(F32)
        total = value if total is None else total + value
    return total


def join_kernel(plan, rows, width, *refs):
    for out_ref, ((left, right),) in zip(refs[-len(plan) :], plan):
        out_ref[:, 0:width] = summed(refs, left, rows, slice(None)).astype(BF16)
        out_ref[:, width:] = summed(refs, right, rows, slice(None)).astype(BF16)


def join(plan, rows, width, channels):
    arrays, numbered = tidy([[pair] for pair in plan])
    return pl.pallas_call(
        functools.partial(join_kernel, numbered, rows, width),
        out_shape=[jax.ShapeDtypeStruct((rows, width + channels), BF16)] * len(plan),
        compiler_params=pltpu.CompilerParams(vmem_limit_bytes=VMEM_LIMIT),
        cost_estimate=pl.CostEstimate(flops=0, bytes_accessed=1 << 20, transcendentals=0),
        name="join",
    )(*arrays)


def carry(pairs):
    ahead = back = None
    for forward, backward in pairs[::-1]:
        if ahead is not None:
            forward = (forward.astype(F32) + ahead.astype(F32)).astype(BF16)
            backward = (backward.astype(F32) + back.astype(F32)).astype(BF16)
        ahead, back = shift(forward, 1), shift(backward, -1)
    return ahead, back


def towards(near, arrived, rows):
    ahead, back = arrived
    return (
        [(near, rows), (ahead, 0)],
        [(near, 2 * rows), (back, 0)],
        [(near, 3 * rows), (ahead, rows), (back, rows)],
    )


def after(values, *earlier):
    return lax.optimization_barrier((tuple(values), earlier))[0]


def spot(rows, columns, offset):
    down = lax.broadcasted_iota(jnp.int32, (rows, columns), 0)
    across = lax.broadcasted_iota(jnp.int32, (rows, columns), 1)
    return jnp.where(across == down + offset, 1.0, 0.0).astype(BF16)


def digits(value):
    return [(value % 256).astype(F32).astype(BF16), (value // 256).astype(F32).astype(BF16)]


def pack_kernel(columns, n_wave, _, *refs):
    sources, out_ref, held = refs[:5], refs[5], refs[6:11]
    sems = refs[11]
    copies = [
        pltpu.make_async_copy(source, ref, sems.at[i])
        for i, (source, ref) in enumerate(zip(sources, held))
    ]
    hidden_ref, ids_ref, weights_ref, codes_ref, owner_ref = held
    for copy in copies:
        copy.start()
    for copy in copies[1:]:
        copy.wait()
    sessions, steps, width = hidden_ref.shape
    expert_count = columns[0] // 2
    books = codes_ref.shape[2]
    meta_width = out_ref.shape[1] - width
    owner = owner_ref[...]
    slots = (owner // sessions // n_wave) * sessions + owner % sessions
    down = lax.broadcasted_iota(jnp.int32, (sessions, sessions), 0)
    across = lax.broadcasted_iota(jnp.int32, (sessions, sessions), 1)
    slot = jnp.sum(jnp.where(down == across, slots, 0).astype(F32), axis=1, keepdims=True)
    slot = slot.astype(jnp.int32)
    lane = lax.broadcasted_iota(jnp.int32, (sessions, meta_width), 1)
    named = lax.broadcasted_iota(jnp.int32, (expert_count, sessions), 0)
    for t in range(steps):
        at = slice(t * sessions, (t + 1) * sessions)
        weight = jnp.zeros((expert_count, sessions), F32)
        for k in range(ids_ref.shape[1]):
            weight += jnp.where(named == ids_ref[t, k : k + 1, :], weights_ref[t, k : k + 1, :], 0.0)
        high = weight.astype(BF16)
        low = (weight - high.astype(F32)).astype(BF16)
        meta = jnp.zeros((sessions, meta_width), F32)
        for piece, offset in ((high, 0), (low, expert_count)):
            meta += lax.dot_general(
                piece,
                spot(expert_count, meta_width, offset),
                (((0,), (0,)), ((), ())),
                preferred_element_type=F32,
            )
        for i, piece in enumerate(digits(codes_ref[:, t, :])):
            move = spot(books, meta_width, columns[0] + i * books)
            meta += jnp.dot(piece, move, preferred_element_type=F32)
        for i, piece in enumerate(digits(slot * steps + t)):
            meta += jnp.where(lane == columns[1] + i, piece.astype(F32), 0.0)
        out_ref[at, width:] = meta.astype(BF16)
    copies[0].wait()
    for t in range(steps):
        out_ref[t * sessions : (t + 1) * sessions, 0:width] = hidden_ref[:, t, :]


def pack(place, hidden_rows, expert_ids, route_weights, codes, owner_slot, columns, n_wave):
    sessions, steps, width = hidden_rows.shape
    meta_width = -(-(columns[1] + 2) // 128) * 128
    args = (
        hidden_rows,
        jnp.transpose(expert_ids, (1, 2, 0)),
        jnp.transpose(route_weights, (1, 2, 0)),
        codes,
        owner_slot[None],
    )
    return pl.pallas_call(
        functools.partial(pack_kernel, columns, n_wave),
        out_shape=jax.ShapeDtypeStruct((steps * sessions, width + meta_width), BF16),
        in_specs=[pl.BlockSpec(memory_space=pltpu.SMEM)]
        + [pl.BlockSpec(memory_space=pltpu.HBM)] * len(args),
        out_specs=pl.BlockSpec(memory_space=pltpu.VMEM),
        scratch_shapes=[pltpu.VMEM(arg.shape, arg.dtype) for arg in args]
        + [pltpu.SemaphoreType.DMA((len(args),))],
        compiler_params=pltpu.CompilerParams(vmem_limit_bytes=VMEM_LIMIT),
        name="pack",
    )(place, *[pltpu.with_memory_space_constraint(arg, pltpu.HBM) for arg in args])


def load_kernel(code_at, books, shard, *refs):
    count = (len(refs) - 3) // 2
    sources, held, spread_ref, sems = refs[1 : count + 1], refs[count + 1 : -2], refs[-2], refs[-1]
    copies = [
        pltpu.make_async_copy(source, ref, sems.at[i])
        for i, (source, ref) in enumerate(zip(sources, held))
    ]
    for copy in copies:
        copy.start()
    column = lax.broadcasted_iota(jnp.int32, spread_ref.shape, 0) - code_at
    book = lax.broadcasted_iota(jnp.int32, spread_ref.shape, 1) // shard
    spread = jnp.where(column == book, 1.0, jnp.where(column == book + books, 256.0, 0.0))
    spread_ref[...] = spread.astype(BF16)
    for copy in copies:
        copy.wait()


def load(earlier, arrays, meta_width, code_at, books, shard):
    hbm = pl.BlockSpec(memory_space=pltpu.HBM)
    return pl.pallas_call(
        functools.partial(load_kernel, code_at, books, shard),
        out_shape=[pltpu.VMEM(v.shape, v.dtype) for v in arrays]
        + [pltpu.VMEM((meta_width, books * shard), BF16)],
        in_specs=[pl.BlockSpec(memory_space=pl.ANY)] + [hbm] * len(arrays),
        out_specs=[pl.BlockSpec(memory_space=pltpu.VMEM)] * (len(arrays) + 1),
        scratch_shapes=[pltpu.SemaphoreType.DMA((len(arrays),))],
        compiler_params=pltpu.CompilerParams(vmem_limit_bytes=VMEM_LIMIT),
        cost_estimate=pl.CostEstimate(
            flops=0, bytes_accessed=sum(2 * v.size for v in arrays), transcendentals=0
        ),
        name="load",
    )(earlier, *[pltpu.with_memory_space_constraint(v, pltpu.HBM) for v in arrays])


def experts_kernel(width, expert_count, block_count, out_count, place_ref, *refs):
    blocks = refs[:block_count]
    parts = [refs[i : i + 3] for i in range(block_count, len(refs) - 2 - out_count, 3)]
    outs, (rows_ref, act_ref) = refs[-2 - out_count : -2], refs[-2:]
    rows = blocks[0].shape[0]
    for i, block in enumerate(blocks):
        rows_ref[i * rows : (i + 1) * rows, :] = block[:, 0:width]
    meta = jnp.concatenate([block[:, width:].astype(F32) for block in blocks], axis=0)
    lane = lax.broadcasted_iota(jnp.int32, meta.shape, 1)
    total = None
    for gate_ref, up_ref, down_ref in parts:
        local, _, units = gate_ref.shape
        for j in range(local):
            mine = place_ref[0] * local + j
            hit = (lane == mine) | (lane == expert_count + mine)
            weight = jnp.sum(jnp.where(hit, meta, 0.0), axis=1, keepdims=True)
            both = jnp.concatenate([gate_ref[j], up_ref[j]], axis=1)
            both = jnp.dot(rows_ref[...], both, preferred_element_type=F32)
            gate, up = both[:, 0:units], both[:, units:]
            value = gate * jax.nn.sigmoid(gate) * up
            act_ref[:, j * units : (j + 1) * units] = (value * weight).astype(BF16)
        result = jnp.dot(act_ref[...], down_ref[...], preferred_element_type=F32)
        total = result if total is None else total + result
    start = 0
    for out_ref in outs:
        size = out_ref.shape[0]
        out_ref[...] = total[start : start + size].astype(BF16)
        start += size


def experts(blocks, split, place, held):
    local, width, units = held[0][0].shape
    rows = blocks[0].shape[0]
    total = rows * len(blocks)
    vmem = pl.BlockSpec(memory_space=pltpu.VMEM)
    weights = [v for part in held for v in part]
    return pl.pallas_call(
        functools.partial(
            experts_kernel, width, lax.axis_size("expert") * local, len(blocks), split
        ),
        out_shape=[jax.ShapeDtypeStruct((total // split, width), BF16)] * split,
        in_specs=[pl.BlockSpec(memory_space=pltpu.SMEM)] + [vmem] * (len(blocks) + len(weights)),
        out_specs=[vmem] * split,
        scratch_shapes=[
            pltpu.VMEM((total, width), BF16),
            pltpu.VMEM((total, local * units), BF16),
        ],
        compiler_params=pltpu.CompilerParams(vmem_limit_bytes=VMEM_LIMIT),
        cost_estimate=pl.CostEstimate(
            flops=6 * total * width * units * local * len(held),
            bytes_accessed=2 * sum(v.size for v in weights),
            transcendentals=total * units * local * len(held),
        ),
        name="experts",
    )(place, *blocks, *weights)


def frames_kernel(slot_at, shard, sessions, steps, sources, order, place_ref, *refs):
    count = len(sources)
    metas, (spread_ref, table_ref, *outs, hot_ref) = refs[:count], refs[count:]
    rows = metas[0].shape[0]
    meta = jnp.concatenate([m[...] for m in metas], axis=0)
    column = lax.broadcasted_iota(jnp.int32, (8, meta.shape[1]), 1)
    digit = lax.broadcasted_iota(jnp.int32, (8, meta.shape[1]), 0)
    picks = jnp.where((column == slot_at + digit) & (digit < 2), 1.0, 0.0).astype(BF16)
    slots = lax.dot_general(picks, meta, (((1,), (1,)), ((), ())), preferred_element_type=F32)
    source = (slots[0:1] + 256.0 * slots[1:2]).astype(jnp.int32)
    row = lax.broadcasted_iota(jnp.int32, (rows * len(order), 1), 0)
    inside = row % rows
    target = (inside % sessions) * steps + inside // sessions
    place = place_ref[0]
    turn = jnp.where(place % 2 == 0, place // 2, count - 1 - place // 2)
    for i, k in enumerate(order):
        at = (turn + k) % count
        device = jnp.where(at < count // 2, 2 * at, 2 * (count - 1 - at) + 1)
        target = target + jnp.where(row // rows == i, device * rows, 0)
    chooser = jnp.where(target == source, 1.0, 0.0).astype(BF16)
    ordered = jnp.dot(chooser, meta, preferred_element_type=F32).astype(BF16)
    codes = jnp.dot(ordered, spread_ref[...], preferred_element_type=F32)
    entry = lax.broadcasted_iota(jnp.int32, (1, hot_ref.shape[1]), 1) % shard + place * shard
    hot_ref[...] = jnp.where(codes == entry.astype(F32), 1.0, 0.0).astype(BF16)
    result = jnp.dot(hot_ref[...], table_ref[...], preferred_element_type=F32)
    start = 0
    for out_ref in outs:
        size = out_ref.shape[0]
        out_ref[...] = result[start : start + size].astype(BF16)
        start += size


def frame_sums(blocks, order, split, place, code_table, spread, slot_at, sessions, steps):
    books, shard, channels = code_table.shape
    meta_width = spread.shape[0]
    sources = list(range(len(blocks)))
    rows, width = blocks[0].shape
    total = rows * len(order)
    block = pl.BlockSpec((rows, meta_width), lambda i: (0, width // meta_width - 1))
    vmem = pl.BlockSpec(memory_space=pltpu.VMEM)
    return pl.pallas_call(
        functools.partial(frames_kernel, slot_at, shard, sessions, steps, sources, order),
        grid=(1,),
        out_shape=[jax.ShapeDtypeStruct((total // split, channels), BF16)] * split,
        in_specs=[pl.BlockSpec(memory_space=pltpu.SMEM)] + [block] * len(sources) + [vmem] * 2,
        out_specs=[vmem] * split,
        scratch_shapes=[pltpu.VMEM((total, books * shard), BF16)],
        compiler_params=pltpu.CompilerParams(
            vmem_limit_bytes=VMEM_LIMIT + 12 * total * rows * len(sources)
        ),
        cost_estimate=pl.CostEstimate(
            flops=2 * total * books * shard * channels,
            bytes_accessed=2 * books * shard * channels,
            transcendentals=0,
        ),
        name="frame_sums",
    )(place, *[blocks[k] for k in sources], spread, code_table.reshape(books * shard, channels))


def near_kernel(for_experts, for_frames, near, width, place_ref, *refs):
    count = len(for_frames[-2])
    sources, weights = refs[:count], refs[count:-7]
    spread_ref, table_ref, rows_out, frames_out, rows_ref, act_ref, hot_ref = refs[-7:]
    blocks = [sources[k] for k in near]
    metas = [m.at[:, width : m.shape[1]] for m in sources]
    experts_kernel(*for_experts, place_ref, *blocks, *weights, rows_out, rows_ref, act_ref)
    frames_kernel(*for_frames, place_ref, *metas, spread_ref, table_ref, frames_out, hot_ref)


def near_sums(blocks, near, place, held, code_table, spread, slot_at, sessions, steps):
    local, width, units = held[0][0].shape
    books, shard, channels = code_table.shape
    rows = blocks[0].shape[0]
    total = rows * len(near)
    vmem = pl.BlockSpec(memory_space=pltpu.VMEM)
    weights = [v for part in held for v in part]
    sources = [blocks[k] for k in range(len(blocks))]
    for_experts = (width, lax.axis_size("expert") * local, len(near), 1)
    for_frames = (slot_at, shard, sessions, steps, list(range(len(sources))), near)
    return pl.pallas_call(
        functools.partial(near_kernel, for_experts, for_frames, near, width),
        out_shape=[jax.ShapeDtypeStruct((total, size), BF16) for size in (width, channels)],
        in_specs=[pl.BlockSpec(memory_space=pltpu.SMEM)]
        + [vmem] * (len(sources) + len(weights) + 2),
        out_specs=[vmem] * 2,
        scratch_shapes=[
            pltpu.VMEM((total, width), BF16),
            pltpu.VMEM((total, local * units), BF16),
            pltpu.VMEM((total, books * shard), BF16),
        ],
        compiler_params=pltpu.CompilerParams(
            vmem_limit_bytes=2 * VMEM_LIMIT + 12 * total * rows * len(sources)
        ),
        cost_estimate=pl.CostEstimate(
            flops=6 * total * width * units * local * len(held),
            bytes_accessed=2 * sum(v.size for v in weights),
            transcendentals=total * units * local * len(held),
        ),
        name="near_sums",
    )(place, *sources, *weights, spread, code_table.reshape(books * shard, channels))


def finish_kernel(left, right, whole, width, *refs):
    state_ref, taps_ref, bias_ref, up_ref, mixed_ref, wave_ref, new_ref = refs[-7:]
    past, sessions, _ = state_ref.shape
    steps = mixed_ref.shape[1]
    rows = steps * sessions
    taps = taps_ref.shape[0]
    frames = summed(refs, right, rows, slice(None))
    for index, row in whole:
        frames = frames + refs[index][row : row + rows, width:].astype(F32)
    history = [state_ref[i].astype(F32) for i in range(past)]
    history += [frames[t * sessions : (t + 1) * sessions] for t in range(steps)]
    decoded = []
    for t in range(steps):
        filtered = bias_ref[...] + taps_ref[0:1, :] * history[past + t]
        for j in range(1, taps):
            filtered = filtered + taps_ref[j : j + 1, :] * history[past + t - j]
        decoded.append(jax.nn.gelu(filtered).astype(BF16))
    samples = jnp.dot(jnp.concatenate(decoded), up_ref[...], preferred_element_type=F32)
    total = summed(refs, left, rows, slice(None))
    for index, row in whole:
        total = total + refs[index][row : row + rows, 0:width].astype(F32)
    for t in range(steps):
        at = slice(t * sessions, (t + 1) * sessions)
        wave_ref[:, t, :] = samples[at].astype(BF16)
        mixed_ref[:, t, :] = total[at].astype(BF16)
    for i in range(past):
        new_ref[i] = history[i + steps].astype(BF16)


def finish(left, right, arrived, width, conv_state, conv_taps, conv_bias, upsample, steps):
    sessions, past, channels = conv_state.shape
    arrays, numbered = tidy([[(left, right, [(v, 0) for v in arrived])]])
    mixed, wave, state = pl.pallas_call(
        functools.partial(finish_kernel, *numbered[0][0], width),
        out_shape=(
            jax.ShapeDtypeStruct((sessions, steps, width), BF16),
            jax.ShapeDtypeStruct((sessions, steps, upsample.shape[1]), BF16),
            jax.ShapeDtypeStruct((past, sessions, channels), BF16),
        ),
        compiler_params=pltpu.CompilerParams(vmem_limit_bytes=VMEM_LIMIT),
        cost_estimate=pl.CostEstimate(flops=0, bytes_accessed=1 << 21, transcendentals=0),
        name="finish",
    )(
        *arrays,
        jnp.transpose(conv_state, (1, 0, 2)),
        conv_taps,
        conv_bias.reshape(1, channels),
        upsample,
    )
    return mixed, wave, jnp.transpose(state, (1, 0, 2))


def per_device(
    hidden_rows,
    expert_ids,
    route_weights,
    w_gate,
    w_up,
    w_down,
    codes,
    owner_slot,
    code_table,
    conv_state,
    conv_taps,
    conv_bias,
    upsample,
):
    count = lax.axis_size("expert")
    sessions, steps, width = hidden_rows.shape
    rows = sessions * steps
    books = codes.shape[2]
    expert_count = count * w_gate.shape[0]
    place = lax.axis_index("expert").astype(jnp.int32)[None]
    columns = (2 * expert_count, 2 * expert_count + 2 * books)

    own = pack(
        place,
        hidden_rows,
        expert_ids,
        route_weights,
        codes,
        owner_slot,
        columns,
        lax.axis_size("wave"),
    )
    half = count // 2
    weights = (w_gate, w_up, w_down.reshape(-1, width))
    sibling = [swap_wave(v) for v in after(weights, own)]
    meta_width = own.shape[1] - width
    *loaded, spread = load(
        own, weights, meta_width, columns[0], books, code_table.shape[1]
    )
    held = [loaded]

    blocks = {0: own}
    behind = ahead = own
    for step in range(1, half + 1):
        got = {step: shift(ahead, -1)}
        if step < half:
            got[count - step] = shift(behind, 1)
        first = held[0] if step == 1 else sibling[step - 2 : step - 1]
        got = {k: after((v,), first)[0] for k, v in got.items()}
        ahead, behind = got[step], got.get(count - step)
        blocks.update(got)

    held.append(sibling)
    near = [0, 1, count - 1, half]
    far = [
        [step, half + step - 1, count - step, half - step + 1] for step in range(2, count // 4 + 1)
    ]
    pairs, turn = [], place
    for group in far[::-1]:
        pairs.insert(0, experts([blocks[k] for k in group], 2, turn, held))
        (turn,) = after((place,), pairs[0])
    arrived = carry(pairs)

    def frames(order, split, turn):
        return frame_sums(
            blocks, order, split, turn, code_table, spread, columns[1], sessions, steps
        )

    far_frames = frames([k for group in far for k in group], 2 * len(far), turn)
    frames_arrived = carry(list(zip(far_frames[::2], far_frames[1::2])))
    (turn,) = after((place,), far_frames)
    near_rows, near_frames = near_sums(
        blocks, near, turn, held, code_table, spread, columns[1], sessions, steps
    )
    left = towards(near_rows, arrived, rows)
    right = towards(near_frames, frames_arrived, rows)
    one, minus, across = join(list(zip(left, right)), rows, width, code_table.shape[2])
    last = [shift(one, 1), shift(across, half), shift(minus, -1)]
    return finish(
        [(near_rows, 0)],
        [(near_frames, 0)],
        last,
        width,
        conv_state,
        conv_taps,
        conv_bias,
        upsample,
        steps,
    )


def solution(mesh):
    rows = P(("groups", "expert", "wave"), None, None)
    placed = (
        rows,
        rows,
        rows,
        P("expert", None, "wave"),
        P("expert", None, "wave"),
        P("expert", "wave", None),
        rows,
        P(("groups", "expert", "wave")),
        P(None, "expert", None),
        rows,
        P(),
        P(),
        P(),
    )
    return jax.shard_map(
        per_device,
        mesh=mesh,
        in_specs=placed,
        out_specs=(rows, rows, rows),
        check_vma=False,
    )
```

```python
import functools

import jax
import jax.numpy as jnp
from jax import lax
from jax.experimental import pallas as pl
from jax.experimental.pallas import tpu as pltpu
from jax.sharding import PartitionSpec as P

F32 = jnp.float32
BF16 = jnp.bfloat16
VMEM_LIMIT = 8 * 1024 * 1024


def ring_order(count):
    return list(range(0, count, 2)) + list(range(1, count, 2))[::-1]


def shift(value, distance):
    count = lax.axis_size("expert")
    ring = ring_order(count)
    pairs = [(ring[i], ring[(i + distance) % count]) for i in range(count)]
    return lax.ppermute(value, "expert", pairs)


def swap_wave(value):
    return lax.ppermute(value, "wave", [(0, 1), (1, 0)])


def tidy(plan):
    arrays, numbers = [], {}

    def number(source):
        array, row = source
        if id(array) not in numbers:
            numbers[id(array)] = len(arrays)
            arrays.append(array)
        return numbers[id(array)], row

    return arrays, [[[[number(v) for v in part] for part in block] for block in out] for out in plan]


def summed(refs, sources, rows, columns):
    total = None
    for index, row in sources:
        value = refs[index][row : row + rows, columns].astype(F32)
        total = value if total is None else total + value
    return total


def join_kernel(plan, rows, width, *refs):
    for out_ref, ((left, right),) in zip(refs[-len(plan) :], plan):
        out_ref[:, 0:width] = summed(refs, left, rows, slice(None)).astype(BF16)
        out_ref[:, width:] = summed(refs, right, rows, slice(None)).astype(BF16)


def join(plan, rows, width, channels):
    arrays, numbered = tidy([[pair] for pair in plan])
    return pl.pallas_call(
        functools.partial(join_kernel, numbered, rows, width),
        out_shape=[jax.ShapeDtypeStruct((rows, width + channels), BF16)] * len(plan),
        compiler_params=pltpu.CompilerParams(vmem_limit_bytes=VMEM_LIMIT),
        cost_estimate=pl.CostEstimate(flops=0, bytes_accessed=1 << 20, transcendentals=0),
        name="join",
    )(*arrays)


def carry(pairs):
    ahead = back = None
    for forward, backward in pairs[::-1]:
        if ahead is not None:
            forward = (forward.astype(F32) + ahead.astype(F32)).astype(BF16)
            backward = (backward.astype(F32) + back.astype(F32)).astype(BF16)
        ahead, back = shift(forward, 1), shift(backward, -1)
    return ahead, back


def towards(near, arrived, rows):
    ahead, back = arrived
    return (
        [(near, rows), (ahead, 0)],
        [(near, 2 * rows), (back, 0)],
        [(near, 3 * rows), (ahead, rows), (back, rows)],
    )


def after(values, *earlier):
    return lax.optimization_barrier((tuple(values), earlier))[0]


def spot(rows, columns, offset):
    down = lax.broadcasted_iota(jnp.int32, (rows, columns), 0)
    across = lax.broadcasted_iota(jnp.int32, (rows, columns), 1)
    return jnp.where(across == down + offset, 1.0, 0.0).astype(BF16)


def digits(value):
    return [(value % 256).astype(F32).astype(BF16), (value // 256).astype(F32).astype(BF16)]


def pack_kernel(columns, n_wave, _, *refs):
    sources, out_ref, held = refs[:5], refs[5], refs[6:11]
    sems = refs[11]
    copies = [
        pltpu.make_async_copy(source, ref, sems.at[i])
        for i, (source, ref) in enumerate(zip(sources, held))
    ]
    hidden_ref, ids_ref, weights_ref, codes_ref, owner_ref = held
    for copy in copies:
        copy.start()
    for copy in copies[1:]:
        copy.wait()
    sessions, steps, width = hidden_ref.shape
    expert_count = columns[0] // 2
    books = codes_ref.shape[2]
    meta_width = out_ref.shape[1] - width
    owner = owner_ref[...]
    slots = (owner // sessions // n_wave) * sessions + owner % sessions
    down = lax.broadcasted_iota(jnp.int32, (sessions, sessions), 0)
    across = lax.broadcasted_iota(jnp.int32, (sessions, sessions), 1)
    slot = jnp.sum(jnp.where(down == across, slots, 0).astype(F32), axis=1, keepdims=True)
    slot = slot.astype(jnp.int32)
    lane = lax.broadcasted_iota(jnp.int32, (sessions, meta_width), 1)
    named = lax.broadcasted_iota(jnp.int32, (expert_count, sessions), 0)
    for t in range(steps):
        at = slice(t * sessions, (t + 1) * sessions)
        weight = jnp.zeros((expert_count, sessions), F32)
        for k in range(ids_ref.shape[1]):
            weight += jnp.where(named == ids_ref[t, k : k + 1, :], weights_ref[t, k : k + 1, :], 0.0)
        high = weight.astype(BF16)
        low = (weight - high.astype(F32)).astype(BF16)
        meta = jnp.zeros((sessions, meta_width), F32)
        for piece, offset in ((high, 0), (low, expert_count)):
            meta += lax.dot_general(
                piece,
                spot(expert_count, meta_width, offset),
                (((0,), (0,)), ((), ())),
                preferred_element_type=F32,
            )
        for i, piece in enumerate(digits(codes_ref[:, t, :])):
            move = spot(books, meta_width, columns[0] + i * books)
            meta += jnp.dot(piece, move, preferred_element_type=F32)
        for i, piece in enumerate(digits(slot * steps + t)):
            meta += jnp.where(lane == columns[1] + i, piece.astype(F32), 0.0)
        out_ref[at, width:] = meta.astype(BF16)
    copies[0].wait()
    for t in range(steps):
        out_ref[t * sessions : (t + 1) * sessions, 0:width] = hidden_ref[:, t, :]


def pack(place, hidden_rows, expert_ids, route_weights, codes, owner_slot, columns, n_wave):
    sessions, steps, width = hidden_rows.shape
    meta_width = -(-(columns[1] + 2) // 128) * 128
    args = (
        hidden_rows,
        jnp.transpose(expert_ids, (1, 2, 0)),
        jnp.transpose(route_weights, (1, 2, 0)),
        codes,
        owner_slot[None],
    )
    return pl.pallas_call(
        functools.partial(pack_kernel, columns, n_wave),
        out_shape=jax.ShapeDtypeStruct((steps * sessions, width + meta_width), BF16),
        in_specs=[pl.BlockSpec(memory_space=pltpu.SMEM)]
        + [pl.BlockSpec(memory_space=pltpu.HBM)] * len(args),
        out_specs=pl.BlockSpec(memory_space=pltpu.VMEM),
        scratch_shapes=[pltpu.VMEM(arg.shape, arg.dtype) for arg in args]
        + [pltpu.SemaphoreType.DMA((len(args),))],
        compiler_params=pltpu.CompilerParams(vmem_limit_bytes=VMEM_LIMIT),
        name="pack",
    )(place, *[pltpu.with_memory_space_constraint(arg, pltpu.HBM) for arg in args])


def load_kernel(code_at, books, shard, *refs):
    count = (len(refs) - 3) // 2
    sources, held, spread_ref, sems = refs[1 : count + 1], refs[count + 1 : -2], refs[-2], refs[-1]
    copies = [
        pltpu.make_async_copy(source, ref, sems.at[i])
        for i, (source, ref) in enumerate(zip(sources, held))
    ]
    for copy in copies:
        copy.start()
    column = lax.broadcasted_iota(jnp.int32, spread_ref.shape, 0) - code_at
    book = lax.broadcasted_iota(jnp.int32, spread_ref.shape, 1) // shard
    spread = jnp.where(column == book, 1.0, jnp.where(column == book + books, 256.0, 0.0))
    spread_ref[...] = spread.astype(BF16)
    for copy in copies:
        copy.wait()


def load(earlier, arrays, meta_width, code_at, books, shard):
    hbm = pl.BlockSpec(memory_space=pltpu.HBM)
    return pl.pallas_call(
        functools.partial(load_kernel, code_at, books, shard),
        out_shape=[pltpu.VMEM(v.shape, v.dtype) for v in arrays]
        + [pltpu.VMEM((meta_width, books * shard), BF16)],
        in_specs=[pl.BlockSpec(memory_space=pl.ANY)] + [hbm] * len(arrays),
        out_specs=[pl.BlockSpec(memory_space=pltpu.VMEM)] * (len(arrays) + 1),
        scratch_shapes=[pltpu.SemaphoreType.DMA((len(arrays),))],
        compiler_params=pltpu.CompilerParams(vmem_limit_bytes=VMEM_LIMIT),
        cost_estimate=pl.CostEstimate(
            flops=0, bytes_accessed=sum(2 * v.size for v in arrays), transcendentals=0
        ),
        name="load",
    )(earlier, *[pltpu.with_memory_space_constraint(v, pltpu.HBM) for v in arrays])


def experts_kernel(width, expert_count, block_count, out_count, place_ref, *refs):
    blocks = refs[:block_count]
    parts = [refs[i : i + 3] for i in range(block_count, len(refs) - 2 - out_count, 3)]
    outs, (rows_ref, act_ref) = refs[-2 - out_count : -2], refs[-2:]
    rows = blocks[0].shape[0]
    for i, block in enumerate(blocks):
        rows_ref[i * rows : (i + 1) * rows, :] = block[:, 0:width]
    meta = jnp.concatenate([block[:, width:].astype(F32) for block in blocks], axis=0)
    lane = lax.broadcasted_iota(jnp.int32, meta.shape, 1)
    total = None
    for gate_ref, up_ref, down_ref in parts:
        local, _, units = gate_ref.shape
        for j in range(local):
            mine = place_ref[0] * local + j
            hit = (lane == mine) | (lane == expert_count + mine)
            weight = jnp.sum(jnp.where(hit, meta, 0.0), axis=1, keepdims=True)
            both = jnp.concatenate([gate_ref[j], up_ref[j]], axis=1)
            both = jnp.dot(rows_ref[...], both, preferred_element_type=F32)
            gate, up = both[:, 0:units], both[:, units:]
            value = gate * jax.nn.sigmoid(gate) * up
            act_ref[:, j * units : (j + 1) * units] = (value * weight).astype(BF16)
        result = jnp.dot(act_ref[...], down_ref[...], preferred_element_type=F32)
        total = result if total is None else total + result
    start = 0
    for out_ref in outs:
        size = out_ref.shape[0]
        out_ref[...] = total[start : start + size].astype(BF16)
        start += size


def experts(blocks, split, place, held):
    local, width, units = held[0][0].shape
    rows = blocks[0].shape[0]
    total = rows * len(blocks)
    vmem = pl.BlockSpec(memory_space=pltpu.VMEM)
    weights = [v for part in held for v in part]
    return pl.pallas_call(
        functools.partial(
            experts_kernel, width, lax.axis_size("expert") * local, len(blocks), split
        ),
        out_shape=[jax.ShapeDtypeStruct((total // split, width), BF16)] * split,
        in_specs=[pl.BlockSpec(memory_space=pltpu.SMEM)] + [vmem] * (len(blocks) + len(weights)),
        out_specs=[vmem] * split,
        scratch_shapes=[
            pltpu.VMEM((total, width), BF16),
            pltpu.VMEM((total, local * units), BF16),
        ],
        compiler_params=pltpu.CompilerParams(vmem_limit_bytes=VMEM_LIMIT),
        cost_estimate=pl.CostEstimate(
            flops=6 * total * width * units * local * len(held),
            bytes_accessed=2 * sum(v.size for v in weights),
            transcendentals=total * units * local * len(held),
        ),
        name="experts",
    )(place, *blocks, *weights)


def frames_kernel(slot_at, shard, sessions, steps, sources, order, place_ref, *refs):
    count = len(sources)
    metas, (spread_ref, table_ref, *outs, hot_ref) = refs[:count], refs[count:]
    rows = metas[0].shape[0]
    last = metas[0].shape[1] - spread_ref.shape[0]
    meta = jnp.concatenate([m[:, last:] for m in metas], axis=0)
    column = lax.broadcasted_iota(jnp.int32, (8, meta.shape[1]), 1)
    digit = lax.broadcasted_iota(jnp.int32, (8, meta.shape[1]), 0)
    picks = jnp.where((column == slot_at + digit) & (digit < 2), 1.0, 0.0).astype(BF16)
    slots = lax.dot_general(picks, meta, (((1,), (1,)), ((), ())), preferred_element_type=F32)
    source = (slots[0:1] + 256.0 * slots[1:2]).astype(jnp.int32)
    row = lax.broadcasted_iota(jnp.int32, (rows * len(order), 1), 0)
    inside = row % rows
    target = (inside % sessions) * steps + inside // sessions
    place = place_ref[0]
    turn = jnp.where(place % 2 == 0, place // 2, count - 1 - place // 2)
    for i, k in enumerate(order):
        at = (turn + k) % count
        device = jnp.where(at < count // 2, 2 * at, 2 * (count - 1 - at) + 1)
        target = target + jnp.where(row // rows == i, device * rows, 0)
    chooser = jnp.where(target == source, 1.0, 0.0).astype(BF16)
    ordered = jnp.dot(chooser, meta, preferred_element_type=F32).astype(BF16)
    codes = jnp.dot(ordered, spread_ref[...], preferred_element_type=F32)
    entry = lax.broadcasted_iota(jnp.int32, (1, hot_ref.shape[1]), 1) % shard + place * shard
    hot_ref[...] = jnp.where(codes == entry.astype(F32), 1.0, 0.0).astype(BF16)
    result = jnp.dot(hot_ref[...], table_ref[...], preferred_element_type=F32)
    start = 0
    for out_ref in outs:
        size = out_ref.shape[0]
        out_ref[...] = result[start : start + size].astype(BF16)
        start += size


def frame_sums(blocks, order, split, place, code_table, spread, slot_at, sessions, steps):
    books, shard, channels = code_table.shape
    sources = list(range(len(blocks)))
    rows = blocks[0].shape[0]
    total = rows * len(order)
    vmem = pl.BlockSpec(memory_space=pltpu.VMEM)
    return pl.pallas_call(
        functools.partial(frames_kernel, slot_at, shard, sessions, steps, sources, order),
        out_shape=[jax.ShapeDtypeStruct((total // split, channels), BF16)] * split,
        in_specs=[pl.BlockSpec(memory_space=pltpu.SMEM)] + [vmem] * (len(sources) + 2),
        out_specs=[vmem] * split,
        scratch_shapes=[pltpu.VMEM((total, books * shard), BF16)],
        compiler_params=pltpu.CompilerParams(
            vmem_limit_bytes=VMEM_LIMIT + 12 * total * rows * len(sources)
        ),
        cost_estimate=pl.CostEstimate(
            flops=2 * total * books * shard * channels,
            bytes_accessed=2 * books * shard * channels,
            transcendentals=0,
        ),
        name="frame_sums",
    )(place, *[blocks[k] for k in sources], spread, code_table.reshape(books * shard, channels))


def near_kernel(for_experts, for_frames, near, place_ref, *refs):
    count = len(for_frames[-2])
    sources, weights = refs[:count], refs[count:-7]
    spread_ref, table_ref, rows_out, frames_out, rows_ref, act_ref, hot_ref = refs[-7:]
    blocks = [sources[k] for k in near]
    experts_kernel(*for_experts, place_ref, *blocks, *weights, rows_out, rows_ref, act_ref)
    frames_kernel(*for_frames, place_ref, *sources, spread_ref, table_ref, frames_out, hot_ref)


def near_sums(blocks, near, place, held, code_table, spread, slot_at, sessions, steps):
    local, width, units = held[0][0].shape
    books, shard, channels = code_table.shape
    rows = blocks[0].shape[0]
    total = rows * len(near)
    vmem = pl.BlockSpec(memory_space=pltpu.VMEM)
    weights = [v for part in held for v in part]
    sources = [blocks[k] for k in range(len(blocks))]
    for_experts = (width, lax.axis_size("expert") * local, len(near), 1)
    for_frames = (slot_at, shard, sessions, steps, list(range(len(sources))), near)
    return pl.pallas_call(
        functools.partial(near_kernel, for_experts, for_frames, near),
        out_shape=[jax.ShapeDtypeStruct((total, size), BF16) for size in (width, channels)],
        in_specs=[pl.BlockSpec(memory_space=pltpu.SMEM)]
        + [vmem] * (len(sources) + len(weights) + 2),
        out_specs=[vmem] * 2,
        scratch_shapes=[
            pltpu.VMEM((total, width), BF16),
            pltpu.VMEM((total, local * units), BF16),
            pltpu.VMEM((total, books * shard), BF16),
        ],
        compiler_params=pltpu.CompilerParams(
            vmem_limit_bytes=2 * VMEM_LIMIT + 12 * total * rows * len(sources)
        ),
        cost_estimate=pl.CostEstimate(
            flops=6 * total * width * units * local * len(held),
            bytes_accessed=2 * sum(v.size for v in weights),
            transcendentals=total * units * local * len(held),
        ),
        name="near_sums",
    )(place, *sources, *weights, spread, code_table.reshape(books * shard, channels))


def finish_kernel(left, right, whole, width, *refs):
    state_ref, taps_ref, bias_ref, up_ref, mixed_ref, wave_ref, new_ref = refs[-7:]
    past, sessions, _ = state_ref.shape
    steps = mixed_ref.shape[1]
    rows = steps * sessions
    taps = taps_ref.shape[0]
    frames = summed(refs, right, rows, slice(None))
    for index, row in whole:
        frames = frames + refs[index][row : row + rows, width:].astype(F32)
    history = [state_ref[i].astype(F32) for i in range(past)]
    history += [frames[t * sessions : (t + 1) * sessions] for t in range(steps)]
    decoded = []
    for t in range(steps):
        filtered = bias_ref[...] + taps_ref[0:1, :] * history[past + t]
        for j in range(1, taps):
            filtered = filtered + taps_ref[j : j + 1, :] * history[past + t - j]
        decoded.append(jax.nn.gelu(filtered).astype(BF16))
    samples = jnp.dot(jnp.concatenate(decoded), up_ref[...], preferred_element_type=F32)
    total = summed(refs, left, rows, slice(None))
    for index, row in whole:
        total = total + refs[index][row : row + rows, 0:width].astype(F32)
    for t in range(steps):
        at = slice(t * sessions, (t + 1) * sessions)
        wave_ref[:, t, :] = samples[at].astype(BF16)
        mixed_ref[:, t, :] = total[at].astype(BF16)
    for i in range(past):
        new_ref[i] = history[i + steps].astype(BF16)


def finish(left, right, arrived, width, conv_state, conv_taps, conv_bias, upsample, steps):
    sessions, past, channels = conv_state.shape
    arrays, numbered = tidy([[(left, right, [(v, 0) for v in arrived])]])
    mixed, wave, state = pl.pallas_call(
        functools.partial(finish_kernel, *numbered[0][0], width),
        out_shape=(
            jax.ShapeDtypeStruct((sessions, steps, width), BF16),
            jax.ShapeDtypeStruct((sessions, steps, upsample.shape[1]), BF16),
            jax.ShapeDtypeStruct((past, sessions, channels), BF16),
        ),
        compiler_params=pltpu.CompilerParams(vmem_limit_bytes=VMEM_LIMIT),
        cost_estimate=pl.CostEstimate(flops=0, bytes_accessed=1 << 21, transcendentals=0),
        name="finish",
    )(
        *arrays,
        jnp.transpose(conv_state, (1, 0, 2)),
        conv_taps,
        conv_bias.reshape(1, channels),
        upsample,
    )
    return mixed, wave, jnp.transpose(state, (1, 0, 2))


def per_device(
    hidden_rows,
    expert_ids,
    route_weights,
    w_gate,
    w_up,
    w_down,
    codes,
    owner_slot,
    code_table,
    conv_state,
    conv_taps,
    conv_bias,
    upsample,
):
    count = lax.axis_size("expert")
    sessions, steps, width = hidden_rows.shape
    rows = sessions * steps
    books = codes.shape[2]
    expert_count = count * w_gate.shape[0]
    place = lax.axis_index("expert").astype(jnp.int32)[None]
    columns = (2 * expert_count, 2 * expert_count + 2 * books)

    own = pack(
        place,
        hidden_rows,
        expert_ids,
        route_weights,
        codes,
        owner_slot,
        columns,
        lax.axis_size("wave"),
    )
    half = count // 2
    weights = (w_gate, w_up, w_down.reshape(-1, width))
    sibling = [swap_wave(v) for v in after(weights, own)]
    meta_width = own.shape[1] - width
    *loaded, spread = load(
        own, weights, meta_width, columns[0], books, code_table.shape[1]
    )
    held = [loaded]

    blocks = {0: own}
    behind = ahead = own
    for step in range(1, half + 1):
        got = {step: shift(ahead, -1)}
        if step < half:
            got[count - step] = shift(behind, 1)
        first = held[0] if step == 1 else sibling[step - 2 : step - 1]
        got = {k: after((v,), first)[0] for k, v in got.items()}
        ahead, behind = got[step], got.get(count - step)
        blocks.update(got)

    held.append(sibling)
    near = [0, 1, count - 1, half]
    far = [
        [step, half + step - 1, count - step, half - step + 1] for step in range(2, count // 4 + 1)
    ]
    pairs, turn = [], place
    for group in far[::-1]:
        pairs.insert(0, experts([blocks[k] for k in group], 2, turn, held))
        (turn,) = after((place,), pairs[0])
    arrived = carry(pairs)

    def frames(order, split, turn):
        return frame_sums(
            blocks, order, split, turn, code_table, spread, columns[1], sessions, steps
        )

    far_frames = frames([k for group in far for k in group], 2 * len(far), turn)
    frames_arrived = carry(list(zip(far_frames[::2], far_frames[1::2])))
    (turn,) = after((place,), far_frames)
    near_rows, near_frames = near_sums(
        blocks, near, turn, held, code_table, spread, columns[1], sessions, steps
    )
    left = towards(near_rows, arrived, rows)
    right = towards(near_frames, frames_arrived, rows)
    one, minus, across = join(list(zip(left, right)), rows, width, code_table.shape[2])
    last = [shift(one, 1), shift(across, half), shift(minus, -1)]
    return finish(
        [(near_rows, 0)],
        [(near_frames, 0)],
        last,
        width,
        conv_state,
        conv_taps,
        conv_bias,
        upsample,
        steps,
    )


def solution(mesh):
    rows = P(("groups", "expert", "wave"), None, None)
    placed = (
        rows,
        rows,
        rows,
        P("expert", None, "wave"),
        P("expert", None, "wave"),
        P("expert", "wave", None),
        rows,
        P(("groups", "expert", "wave")),
        P(None, "expert", None),
        rows,
        P(),
        P(),
        P(),
    )
    return jax.shard_map(
        per_device,
        mesh=mesh,
        in_specs=placed,
        out_specs=(rows, rows, rows),
        check_vma=False,
    )
```
